32 devices in a mesh: dp: 16 (over z, y, x), tensor: 2 (over core).
Axes of the slice: x: 2, y: 2, z: 4, core: 2. Of those that a mesh axis runs over, the one named last changes fastest.
Arguments:
- tokens: bfloat16 [8192, 2048], P('dp'), may hold values from -24 to 24
- segments: int32 [16, 512], P('dp'), may hold values from 0 to 3, never falling along the last dimension, each value on 1 to 320 neighbouring positions
- cotangent: float32 [8192, 2048], P('dp'), may hold values from -6 to 6
- attn_gain: float32 [2048], replicated, may hold values from 0.5 to 1.5
- ffn_gain: float32 [2048], replicated, may hold values from 0.5 to 1.5
- query_gain: float32 [64], replicated, may hold values from 0.5 to 1.5
- key_gain: float32 [64], replicated, may hold values from 0.5 to 1.5
- w_query: bfloat16 [2048, 2048], P('dp', 'tensor'), may hold values from -0.125 to 0.125
- key_weight: bfloat16 [2048, 512], P('dp', 'tensor'), may hold values from -0.125 to 0.125
- value_weight: bfloat16 [2048, 512], P('dp', 'tensor'), may hold values from -0.125 to 0.125
- w_out: bfloat16 [2048, 2048], P('dp', 'tensor'), may hold values from -0.375 to 0.375
- w_gate: bfloat16 [2048, 8192], P('dp', 'tensor'), may hold values from -0.125 to 0.125
- w_up: bfloat16 [2048, 8192], P('dp', 'tensor'), may hold values from -0.125 to 0.125
- w_down: bfloat16 [2048, 8192], P('dp', 'tensor'), may hold values from -0.0625 to 0.0625
Outputs:
- mixed: float32 [8192, 2048], P('dp')
- input_grad: float32 [8192, 2048], P('dp')
- attn_gain_grad: float32 [2048], replicated
- ffn_gain_grad: float32 [2048], replicated
- query_gain_grad: float32 [64], replicated
- key_gain_grad: float32 [64], replicated
- w_query_grad: float32 [2048, 2048], P('dp', 'tensor')
- w_key_grad: float32 [2048, 512], P('dp', 'tensor')
- w_value_grad: float32 [2048, 512], P('dp', 'tensor')
- w_out_grad: float32 [2048, 2048], P('dp', 'tensor')
- w_gate_grad: float32 [2048, 8192], P('dp', 'tensor')
- w_up_grad: float32 [2048, 8192], P('dp', 'tensor')
- w_down_grad: float32 [2048, 8192], P('dp', 'tensor')
The draws below stay inside these ranges and needn't reach their ends.
Inputs may be any that keep to these rules, and one draw needn't show every extreme that they name: `segments`: within each sequence the numbers never fall; each document holds 1 to 320 tokens and one holds exactly 320.
All inputs are finite; a program needn't handle non-finite values.
Results may differ from the reference program's by a relative error of at most 0.014.
Values may be sent and summed in bfloat16 or wider, within the bound.
No kernel may reach another device: no remote copies, remote signals or barrier semaphores. Data moves between devices by JAX's collectives and lax.ppermute only.
A program may use at most 320 MiB of HBM per device.

```python
import math
import jax
import jax.numpy as jnp
import numpy as np
from jax import lax

MODEL_WIDTH = 2048
QUERY_HEADS = 32
KEY_VALUE_HEADS = 8
HEAD_SIZE = 64
FF = 8192
TOK_DEV = 512
DOCS = 4
SEG_MOST = 320
SEQS = 16
TOKENS = 8192


def draw_tokens(key, part):
    key = jax.random.fold_in(key, 11)
    key_base, key_column, key_row = jax.random.split(key, 3)
    column_scale = jnp.exp(jax.random.uniform(key_column, (1, MODEL_WIDTH), jnp.float32, jnp.log(0.3), jnp.log(3.0)))
    row_scale = jnp.exp(jax.random.uniform(key_row, (TOKENS, 1), jnp.float32, jnp.log(0.5), jnp.log(2.0)))
    values = jax.random.normal(key_base, (TOKENS, MODEL_WIDTH), jnp.float32) * column_scale * row_scale
    return jnp.clip(values, -24.0, 24.0).astype(jnp.bfloat16)


def with_spikes(result, rng, source, target, shards_of, factor):
    def block_of(position):
        return (jnp.arange(result.shape[position]) // (result.shape[position] // shards_of)).reshape((-1,) + (1,) * (result.ndim - 1 - position))

    one_side = jax.random.permutation(rng, shards_of)[block_of(target)]
    second = (block_of(target) + shards_of // 2) % shards_of
    return jnp.where((block_of(source) == one_side) | (block_of(source) == second), factor * result, result)


def levels(key, shape, pieces, smallest, high):
    def one(axis_at, blocks):
        draws = jax.random.uniform(jax.random.fold_in(jax.random.fold_in(key, 6), axis_at), (blocks,), jnp.float32, smallest / len(pieces), high / len(pieces))
        return jnp.repeat(jnp.exp(draws), shape[axis_at] // blocks).reshape((-1,) + (1,) * (len(shape) - axis_at - 1))

    level = one(*pieces[0])
    for cut in pieces[1:]:
        level = level * one(*cut)
    return level


def profile(amount, total, most, skew):
    loads = [(1 << 20) // math.isqrt(standing ** skew) + 1 for standing in range(2, amount + 1)]
    rest, given = total - most - (amount - 1), [1] * (amount - 1)
    while rest > 0:
        free = [i for i in range(amount - 1) if given[i] < most]
        pool, budget = sum([loads[i] for i in free]), rest
        for i in free:
            more = min(most - given[i], max(1, budget * loads[i] // pool), rest)
            given[i] = given[i] + more
            rest = rest - more
    return np.array([most] + given)


def ragged(own_key, amount, total, limit, lean):
    if amount == 2:
        one = jax.random.randint(own_key, (), max(1, total - limit), min(limit, total - 1) + 1)
        return jnp.stack([one, total - one])
    sizes = jnp.asarray(profile(amount, total, limit, lean), jnp.int32)
    couples = (amount - 1) // 2
    giver, taker = sizes[1:1 + 2 * couples:2], sizes[2:2 + 2 * couples:2]
    margin = jnp.minimum(giver - 1, limit - taker)
    passed = jax.random.randint(jax.random.fold_in(own_key, 1), (couples,), 0, 1 << 20) % (margin + 1)
    sizes = sizes.at[1:1 + 2 * couples:2].set(giver - passed).at[2:2 + 2 * couples:2].set(taker + passed)
    return sizes[jax.random.permutation(jax.random.fold_in(own_key, 2), amount)]


def centred(stream_key, shape, spread, bound, pieces=(), kind=jnp.bfloat16):
    level = levels(stream_key, shape, pieces, -0.22, 0.18) if pieces else 1.0
    array = jax.random.normal(stream_key, shape, jnp.float32) * spread * level
    return jnp.minimum(jnp.maximum(array, -bound), bound).astype(kind)


def gaussian_with(key, shape, scale, reach, cuts, heavy, kind=jnp.bfloat16):
    values = scale * jax.random.normal(key, shape, jnp.float32)
    if cuts:
        values = values * levels(key, shape, cuts, -0.22, 0.18)
    return jnp.clip(with_spikes(values, jax.random.fold_in(key, 3), *heavy), -reach, reach).astype(kind)


def setup_inputs(seed: int = 0) -> dict:
    splits = jax.random.split(jax.random.key(seed), 15)
    tokens = draw_tokens(jax.random.fold_in(splits[14], 71), 0)
    segments = jax.vmap(lambda own: jnp.searchsorted(jnp.cumsum(ragged(own, DOCS, TOK_DEV, SEG_MOST, 1)), jnp.arange(TOK_DEV), side="right"))(jax.random.split(splits[1], SEQS)).reshape((SEQS, TOK_DEV)).astype(jnp.int32)
    cotangent = gaussian_with(splits[2], (TOKENS, MODEL_WIDTH), 1.0, 6.0, ((0, 16),), (0, 1, 16, 2.0), jnp.float32)
    attn_gain = jnp.clip(1.0 + 0.1 * jax.random.normal(splits[3], (MODEL_WIDTH,), jnp.float32), 0.5, 1.5)
    ffn_gain = jnp.clip(1.0 + 0.1 * jax.random.normal(splits[4], (MODEL_WIDTH,), jnp.float32), 0.5, 1.5)
    query_gain = jnp.clip(1.0 + 0.1 * jax.random.normal(splits[5], (HEAD_SIZE,), jnp.float32), 0.5, 1.5)
    key_gain = jnp.clip(1.0 + 0.1 * jax.random.normal(splits[6], (HEAD_SIZE,), jnp.float32), 0.5, 1.5)
    w_query = centred(splits[7], (MODEL_WIDTH, QUERY_HEADS * HEAD_SIZE), MODEL_WIDTH ** -0.5, 0.125, ((0, 16), (1, 2)))
    key_weight = centred(splits[8], (MODEL_WIDTH, KEY_VALUE_HEADS * HEAD_SIZE), MODEL_WIDTH ** -0.5, 0.125, ((0, 16), (1, 2)))
    value_weight = centred(splits[9], (MODEL_WIDTH, KEY_VALUE_HEADS * HEAD_SIZE), MODEL_WIDTH ** -0.5, 0.125, ((0, 16), (1, 2)))
    w_out = centred(splits[10], (MODEL_WIDTH, QUERY_HEADS * HEAD_SIZE), (QUERY_HEADS * HEAD_SIZE // 8) ** -0.5, 0.375, ((0, 16), (1, 2)))
    w_gate = centred(splits[11], (MODEL_WIDTH, FF), MODEL_WIDTH ** -0.5, 0.125, ((0, 16), (1, 2)))
    w_up = centred(splits[12], (MODEL_WIDTH, FF), MODEL_WIDTH ** -0.5, 0.125, ((0, 16), (1, 2)))
    w_down = centred(splits[13], (MODEL_WIDTH, FF), FF ** -0.5, 0.0625, ((0, 16), (1, 2)))
    return dict(tokens=tokens, segments=segments, cotangent=cotangent, attn_gain=attn_gain, ffn_gain=ffn_gain, query_gain=query_gain, key_gain=key_gain, w_query=w_query, key_weight=key_weight, value_weight=value_weight, w_out=w_out, w_gate=w_gate, w_up=w_up, w_down=w_down)


eps = 1e-05
rope_base = 1000000.0

@jax.custom_vjp
def lowered_input(v):
    return lax.optimization_barrier(v.astype(jnp.bfloat16)).astype(jnp.float32)

@jax.custom_vjp
def lowered_backward(v):
    return v

def low_keep(v):
    return (lowered_input(v), None)

def low_pass(kept, grad):
    return (grad,)

def back_keep(v):
    return (v, None)

def back_low(kept, grad):
    return (lowered_input(grad),)
lowered_input.defvjp(low_keep, low_pass)
lowered_backward.defvjp(back_keep, back_low)

def matrix_product_exact(left, right):
    return jnp.dot(left, right, precision=lax.Precision.HIGHEST, preferred_element_type=jnp.float32)

def rms_scale(values, gain):
    return values * lax.rsqrt(lax.optimization_barrier(jnp.mean(values * values, axis=-1, keepdims=True)) + eps) * gain

def positions_of(segment_row):
    row_index = jnp.arange(segment_row.shape[0], dtype=jnp.int32)
    earlier = jnp.concatenate([segment_row[:1] - 1, segment_row[:-1]])
    starts = jnp.where(segment_row != earlier, row_index, jnp.zeros_like(row_index))
    return row_index - lax.cummax(starts, axis=0)

def angles(positions, width):
    frequency = rope_base ** (-jnp.arange(0, width, 2, dtype=jnp.float32) / width)
    phases = positions.astype(jnp.float32)[:, None] * frequency[None, :]
    phases = jnp.concatenate([phases, phases], axis=-1)
    return (jnp.cos(phases)[:, None, :], jnp.sin(phases)[:, None, :])

def rotate(values, cosine_table, sine_table):
    half_width = values.shape[-1] // 2
    turned = jnp.concatenate([-values[..., half_width:], values[..., :half_width]], axis=-1)
    return values * cosine_table + turned * sine_table

def block_forward(weights_all, source, segment_row):
    attn_gain, ffn_gain, query_gain, key_gain, w_query, key_weight, value_weight, w_out, w_gate, w_up, w_down = weights_all
    token_length = source.shape[0]
    query_group_count = QUERY_HEADS // KEY_VALUE_HEADS
    cosine_table, sine_table = angles(positions_of(segment_row), HEAD_SIZE)
    normalized_input = lowered_input(rms_scale(source, attn_gain))
    query_raw = lowered_backward(matrix_product_exact(normalized_input, w_query)).reshape(token_length, QUERY_HEADS, HEAD_SIZE)
    key_unrotated = lowered_backward(matrix_product_exact(normalized_input, key_weight)).reshape(token_length, KEY_VALUE_HEADS, HEAD_SIZE)
    value_rows = lowered_input(lowered_backward(matrix_product_exact(normalized_input, value_weight))).reshape(token_length, KEY_VALUE_HEADS, HEAD_SIZE)
    query_rows = lowered_input(rotate(rms_scale(query_raw, query_gain), cosine_table, sine_table))
    key = lowered_input(rotate(rms_scale(key_unrotated, key_gain), cosine_table, sine_table))
    query_rows = query_rows.reshape(token_length, KEY_VALUE_HEADS, query_group_count, HEAD_SIZE)
    attention_logits = lowered_backward(0.125 * jnp.einsum('hcfw,kcw->cfhk', query_rows, key, precision=lax.Precision.HIGHEST))
    row_index = jnp.arange(token_length, dtype=jnp.int32)
    allowed = (segment_row[:, None] == segment_row[None, :]) & (row_index[:, None] >= row_index[None, :])
    attention_logits = jnp.where(allowed, attention_logits, -1000000000.0)
    attention_probabilities = lowered_input(jax.nn.softmax(attention_logits, axis=-1))
    head_outputs = lowered_input(lowered_backward(jnp.einsum('ljxe,elv->xljv', attention_probabilities, value_rows, precision=lax.Precision.HIGHEST)))
    head_outputs = head_outputs.reshape(token_length, QUERY_HEADS * HEAD_SIZE)
    attended = lowered_backward(matrix_product_exact(head_outputs, w_out.T))
    state = source + attended
    normed2 = lowered_input(rms_scale(state, ffn_gain))
    gate_proj = lowered_backward(matrix_product_exact(normed2, w_gate))
    up_proj = lowered_backward(matrix_product_exact(normed2, w_up))
    inner = lowered_input(jax.nn.silu(gate_proj) * up_proj)
    branch = lowered_backward(matrix_product_exact(inner, w_down.T))
    return state + branch

def reference(tokens, segments, cotangent, attn_gain, ffn_gain, query_gain, key_gain, w_query, key_weight, value_weight, w_out, w_gate, w_up, w_down):
    weights_all = tuple((item.astype(jnp.float32) for item in (attn_gain, ffn_gain, query_gain, key_gain, w_query, key_weight, value_weight, w_out, w_gate, w_up, w_down)))
    sources = tokens.astype(jnp.float32).reshape(SEQS, TOK_DEV, MODEL_WIDTH)
    cot_rows = cotangent.astype(jnp.float32).reshape(SEQS, TOK_DEV, MODEL_WIDTH)

    def per_sequence(totals, inputs_row):
        source_row, segment_row, cot_row = inputs_row
        output_row, pullback = jax.vjp(lambda weights_in, source_in: block_forward(weights_in, source_in, segment_row), weights_all, source_row)
        weight_grads, source_grad = pullback(cot_row)
        totals = jax.tree.map(lambda left, right: left + right, totals, weight_grads)
        return (totals, (output_row, source_grad))
    zero_grads = jax.tree.map(jnp.zeros_like, weights_all)
    totals, (outputs, source_grads) = lax.scan(per_sequence, zero_grads, (sources, segments, cot_rows))
    return (outputs.reshape(TOKENS, MODEL_WIDTH), source_grads.reshape(TOKENS, MODEL_WIDTH), totals[0], totals[1], totals[2], totals[3], totals[4], totals[5], totals[6], totals[7], totals[8], totals[9], totals[10])
```

```python
import jax
import jax.numpy as jnp
from jax import lax
from jax.sharding import PartitionSpec as P

eps = 1e-05
rope_base = 1000000.0
group = 4
sub_count = 2


def norm_rows(values, gain):
    scale = lax.rsqrt(jnp.mean(values * values, axis=-1, keepdims=True) + eps)
    return (values * scale * gain, scale)


def norm_back(values, scale, gain, incoming):
    weighted = incoming * gain
    return scale * weighted - values * (scale * scale * scale) * jnp.mean(
        weighted * values, axis=-1, keepdims=True
    )


def positions_of(segment_row):
    row_index = jnp.arange(segment_row.shape[0], dtype=jnp.int32)
    earlier = jnp.concatenate([segment_row[:1] - 1, segment_row[:-1]])
    starts = jnp.where(segment_row != earlier, row_index, jnp.zeros_like(row_index))
    return row_index - lax.cummax(starts, axis=0)


def angles(positions, width):
    frequency = rope_base ** (-jnp.arange(0, width, 2, dtype=jnp.float32) / width)
    phases = positions.astype(jnp.float32)[..., None] * frequency
    phases = jnp.concatenate([phases, phases], axis=-1)
    return (jnp.cos(phases)[..., None, :], jnp.sin(phases)[..., None, :])


def head_prepare(raw_heads, gain, cosine_table, sine_table):
    scaled = (
        raw_heads * lax.rsqrt(jnp.mean(raw_heads * raw_heads, axis=-1, keepdims=True) + eps) * gain
    )
    half_width = scaled.shape[-1] // 2
    turned = jnp.concatenate([-scaled[..., half_width:], scaled[..., :half_width]], axis=-1)
    return scaled * cosine_table + turned * sine_table


def rows_product(left, right):
    return lax.dot_general(
        left, right, (((0,), (0,)), ((), ())), preferred_element_type=jnp.float32
    )


def cols_product(left, right):
    return lax.dot_general(
        left, right, (((1,), (1,)), ((), ())), preferred_element_type=jnp.float32
    )


def swap_cores(values):
    return lax.ppermute(values, "tensor", [(0, 1), (1, 0)])


class Lines:
    def __init__(self, dp):
        self.dp = dp
        self.length = dp // group
        index = lax.axis_index("dp")
        self.place = index % group
        self.spot = index // group

    def flip(self, values, relation):
        return lax.ppermute(values, "dp", [(i, i ^ relation) for i in range(self.dp)])

    def hop(self, values, first, last, step):
        pairs = [
            (spot * group + place, (spot + step) * group + place)
            for spot in range(first, last + 1)
            for place in range(group)
        ]
        return lax.ppermute(values, "dp", pairs)

    def turn(self, values, step):
        pairs = [
            (spot * group + place, ((spot + step) % self.length) * group + place)
            for spot in range(self.length)
            for place in range(group)
        ]
        return lax.ppermute(values, "dp", pairs)

    def by_place(self, related):
        odd = self.place % 2 == 1
        high = self.place // 2 == 1
        own, one, two, three = related
        pairs = (
            (jnp.where(odd, one, own), jnp.where(odd, own, one)),
            (jnp.where(odd, three, two), jnp.where(odd, two, three)),
        )
        return [
            jnp.where(high, pairs[1][0], pairs[0][0]),
            jnp.where(high, pairs[1][1], pairs[0][1]),
            jnp.where(high, pairs[0][0], pairs[1][0]),
            jnp.where(high, pairs[0][1], pairs[1][1]),
        ]

    def share_columns(self, piece_of):
        pieces = [piece_of(self.place ^ relation) for relation in range(group)]
        related = [pieces[0]] + [self.flip(pieces[r], r) for r in range(1, group)]
        return jnp.concatenate(self.by_place(related), axis=0)

    def gather_line(self, block):
        length = self.length
        if length != 4:
            return [block] + [self.turn(block, -k) for k in range(1, length)]
        ups, downs = [block], [block]
        for k in range(1, length):
            ups.append(self.hop(ups[-1], k - 1, length - 2, 1))
            downs.append(self.hop(downs[-1], 1, length - k, -1))
        return [block] + [
            jnp.where(self.spot + k < length, downs[k], ups[length - k])
            for k in range(1, length)
        ]

    def scatter_line(self, blocks):
        length = self.length
        total = blocks[0].astype(jnp.float32)
        if length != 4:
            for k in range(1, length):
                total = total + self.turn(blocks[k], k).astype(jnp.float32)
            return total
        up = down = None
        for s in range(1, length):
            send_up, send_down = blocks[length - s], blocks[s]
            if up is not None:
                send_up = (send_up.astype(jnp.float32) + up.astype(jnp.float32)).astype(jnp.bfloat16)
                send_down = (send_down.astype(jnp.float32) + down.astype(jnp.float32)).astype(
                    jnp.bfloat16
                )
            up = self.hop(send_up, 0, min(s - 1, length - 2), 1)
            down = self.hop(send_down, max(length - s, 1), length - 1, -1)
        return total + up.astype(jnp.float32) + down.astype(jnp.float32)

    def share_rows(self, total):
        rows = total.shape[0] // group
        parts = total.astype(jnp.bfloat16)
        related = [lax.dynamic_slice_in_dim(total, self.place * rows, rows)]
        for r in range(1, group):
            piece = lax.dynamic_slice_in_dim(parts, (self.place ^ r) * rows, rows)
            related.append(self.flip(piece, r).astype(jnp.float32))
        return self.by_place(related)

    def gather_tokens(self, mine):
        kept = [mine] + [self.flip(mine, r) for r in range(1, group)]
        return jnp.stack([jnp.stack([one, swap_cores(one)]) for one in kept])

    def scatter_tokens(self, part):
        total = None
        for r in range(1, group):
            both = part[r, 0].astype(jnp.float32) + swap_cores(part[r, 1]).astype(jnp.float32)
            term = self.flip(both.astype(jnp.bfloat16), r).astype(jnp.float32)
            total = term if total is None else total + term
        return total + part[0, 0].astype(jnp.float32) + swap_cores(part[0, 1]).astype(jnp.float32)


def sum_all(values, dp):
    bit = 1
    while bit < dp:
        values = values + lax.ppermute(values, "dp", [(i, i ^ bit) for i in range(dp)])
        bit *= 2
    return values + swap_cores(values)


def local(
    dp,
    tokens,
    segments,
    cotangent,
    attn_gain,
    ffn_gain,
    query_gain,
    key_gain,
    w_query,
    key_weight,
    value_weight,
    w_out,
    w_gate,
    w_up,
    w_down,
):
    lines = Lines(dp)
    core = lax.axis_index("tensor")
    length, width = tokens.shape
    half = length // 2
    head_dim = query_gain.shape[0]
    rows = w_query.shape[0]
    block_rows = rows * group
    query_width = w_query.shape[1] // group
    key_width = key_weight.shape[1] // group
    query_heads = query_width // head_dim
    value_heads = key_width // head_dim
    query_group_count = query_heads // value_heads
    ff = w_gate.shape[1] // group
    ff_sub = ff // sub_count
    all_tokens = group * length

    def around(values):
        return jnp.roll(values, -lines.spot * block_rows, axis=-1)

    def back_around(values):
        return jnp.roll(values, lines.spot * block_rows, axis=-1)

    def halves(values, axis=0):
        return jnp.roll(values, -core * half, axis=axis)

    attn_gain_r, ffn_gain_r = around(attn_gain), around(ffn_gain)

    def columns(weight, start, size):
        return lax.dynamic_slice_in_dim(weight, start, size, axis=1)

    qkv_block = lines.share_columns(
        lambda j: jnp.concatenate(
            [
                columns(w_query, j * query_width, query_width),
                columns(key_weight, j * key_width, key_width),
                columns(value_weight, j * key_width, key_width),
            ],
            axis=1,
        )
    )
    out_block = lines.share_columns(lambda j: columns(w_out, j * query_width, query_width))
    qkv_w = jnp.concatenate(lines.gather_line(qkv_block), axis=0)
    out_w = jnp.concatenate(lines.gather_line(out_block), axis=0)
    gate_up_w, down_w = [], []
    for s in range(sub_count):
        ffn_block = lines.share_columns(
            lambda j: jnp.concatenate(
                [
                    columns(weight, s * group * ff_sub + j * ff_sub, ff_sub)
                    for weight in (w_gate, w_up, w_down)
                ],
                axis=1,
            )
        )
        got = lines.gather_line(ffn_block)
        gate_up_w.append(jnp.concatenate([b[:, : 2 * ff_sub] for b in got], axis=0))
        down_w.append(jnp.concatenate([b[:, 2 * ff_sub :] for b in got], axis=0))

    seg_all = jnp.stack([segments[0]] + [lines.flip(segments, r)[0] for r in range(1, group)])
    positions = halves(jax.vmap(positions_of)(seg_all), axis=1)
    seg_all = halves(seg_all, axis=1)
    row_index = halves(jnp.arange(length, dtype=jnp.int32))
    allowed = (seg_all[:, :, None] == seg_all[:, None, :]) & (
        row_index[:, None] >= row_index[None, :]
    )
    cosine_table, sine_table = angles(positions, head_dim)

    source = around(lax.dynamic_slice_in_dim(tokens, core * half, half)).astype(jnp.float32)
    normed_f, scale_first = norm_rows(source, attn_gain_r)
    normed = lines.gather_tokens(normed_f.astype(jnp.bfloat16)).reshape(all_tokens, width)
    cot_half = around(lax.dynamic_slice_in_dim(cotangent, core * half, half))
    out_b = lines.gather_tokens(cot_half.astype(jnp.bfloat16)).reshape(all_tokens, width)

    qkv = jnp.dot(normed, qkv_w, preferred_element_type=jnp.float32)
    query_raw = qkv[:, :query_width].reshape(group, length, query_heads, head_dim)
    key_raw = qkv[:, query_width : query_width + key_width].reshape(
        group, length, value_heads, head_dim
    )
    value = (
        qkv[:, query_width + key_width :]
        .astype(jnp.bfloat16)
        .reshape(group, length, value_heads, head_dim)
    )
    query_turned, query_pull = jax.vjp(
        lambda raw_in, gain_in: head_prepare(raw_in, gain_in, cosine_table, sine_table),
        query_raw,
        query_gain,
    )
    key_turned, key_pull = jax.vjp(
        lambda raw_in, gain_in: head_prepare(raw_in, gain_in, cosine_table, sine_table),
        key_raw,
        key_gain,
    )
    query = query_turned.astype(jnp.bfloat16).reshape(
        group, length, value_heads, query_group_count, head_dim
    )
    key = key_turned.astype(jnp.bfloat16)
    scores = 0.125 * jnp.einsum("shcfw,skcw->scfhk", query, key, preferred_element_type=jnp.float32)
    scores = jnp.where(allowed[:, None, None], scores, -1000000000.0)
    probs_f = jax.nn.softmax(scores, axis=-1)
    probs = probs_f.astype(jnp.bfloat16)
    heads_out = jnp.einsum("scfhk,skcw->shcfw", probs, value, preferred_element_type=jnp.float32)
    heads_out = heads_out.astype(jnp.bfloat16).reshape(all_tokens, query_width)
    attended_part = cols_product(heads_out, out_w).astype(jnp.bfloat16)
    attended = lines.scatter_tokens(attended_part.reshape(group, 2, half, width))

    state = source + attended
    normed2_f, scale_second = norm_rows(state, ffn_gain_r)
    normed2 = lines.gather_tokens(normed2_f.astype(jnp.bfloat16)).reshape(all_tokens, width)
    branch_part = normed2_part = None
    ffn_grads = []
    for s in range(sub_count):
        gate_up = jnp.dot(normed2, gate_up_w[s], preferred_element_type=jnp.float32)
        gate, up = gate_up[:, :ff_sub], gate_up[:, ff_sub:]
        sigmoid_gate = jax.nn.sigmoid(gate)
        silu_gate = gate * sigmoid_gate
        inner = (silu_gate * up).astype(jnp.bfloat16)
        inner_grad = jnp.dot(out_b, down_w[s], preferred_element_type=jnp.float32)
        gate_grad = (inner_grad * up * sigmoid_gate * (1.0 + gate * (1.0 - sigmoid_gate))).astype(
            jnp.bfloat16
        )
        up_grad = (inner_grad * silu_gate).astype(jnp.bfloat16)
        both_grad = jnp.concatenate([gate_grad, up_grad], axis=1)
        gate_up_g = rows_product(normed2, both_grad).astype(jnp.bfloat16)
        down_g = rows_product(out_b, inner).astype(jnp.bfloat16)
        blocks = [
            jnp.concatenate(
                [
                    gate_up_g[k * block_rows : (k + 1) * block_rows],
                    down_g[k * block_rows : (k + 1) * block_rows],
                ],
                axis=1,
            )
            for k in range(lines.length)
        ]
        ffn_grads.append(lines.share_rows(lines.scatter_line(blocks)))
        more = cols_product(both_grad, gate_up_w[s])
        normed2_part = more if normed2_part is None else normed2_part + more
        more = cols_product(inner, down_w[s])
        branch_part = more if branch_part is None else branch_part + more
    normed2_grad = lines.scatter_tokens(
        normed2_part.astype(jnp.bfloat16).reshape(group, 2, half, width)
    )
    ffn_gain_part = jnp.sum(normed2_grad * state * scale_second, axis=0)
    state_grad = cot_half + norm_back(state, scale_second, ffn_gain_r, normed2_grad)

    attended_b = lines.gather_tokens(state_grad.astype(jnp.bfloat16)).reshape(all_tokens, width)
    heads_grad = jnp.dot(attended_b, out_w, preferred_element_type=jnp.float32).astype(jnp.bfloat16)
    heads_grad = heads_grad.reshape(group, length, value_heads, query_group_count, head_dim)

    def attention_grads(product):
        return lines.share_rows(
            lines.scatter_line(
                [product[k * block_rows : (k + 1) * block_rows] for k in range(lines.length)]
            )
        )

    out_grads = attention_grads(rows_product(attended_b, heads_out).astype(jnp.bfloat16))
    probs_grad = jnp.einsum(
        "shcfw,skcw->scfhk", heads_grad, value, preferred_element_type=jnp.float32
    )
    value_grad = jnp.einsum("scfhk,shcfw->skcw", probs, heads_grad, preferred_element_type=jnp.float32)
    value_grad = value_grad.astype(jnp.bfloat16).reshape(all_tokens, key_width)
    score_grad = probs_f * (probs_grad - jnp.sum(probs_f * probs_grad, axis=-1, keepdims=True))
    score_grad = score_grad.astype(jnp.bfloat16)
    query_grad = 0.125 * jnp.einsum(
        "scfhk,skcw->shcfw", score_grad, key, preferred_element_type=jnp.float32
    )
    key_grad = 0.125 * jnp.einsum(
        "scfhk,shcfw->skcw", score_grad, query, preferred_element_type=jnp.float32
    )
    query_raw_grad, query_gain_part = query_pull(
        query_grad.reshape(group, length, query_heads, head_dim)
    )
    key_raw_grad, key_gain_part = key_pull(key_grad)
    qkv_grad = jnp.concatenate(
        [
            query_raw_grad.astype(jnp.bfloat16).reshape(all_tokens, query_width),
            key_raw_grad.astype(jnp.bfloat16).reshape(all_tokens, key_width),
            value_grad,
        ],
        axis=1,
    )
    qkv_grads = attention_grads(rows_product(normed, qkv_grad).astype(jnp.bfloat16))
    normed_part = cols_product(qkv_grad, qkv_w).astype(jnp.bfloat16)
    normed_grad = lines.scatter_tokens(normed_part.reshape(group, 2, half, width))
    attn_gain_part = jnp.sum(normed_grad * source * scale_first, axis=0)
    input_grad = state_grad + norm_back(source, scale_first, attn_gain_r, normed_grad)
    mixed = state + lines.scatter_tokens(
        branch_part.astype(jnp.bfloat16).reshape(group, 2, half, width)
    )

    def whole_rows(mine):
        mine = back_around(mine)
        return jnp.roll(jnp.concatenate([mine, swap_cores(mine)], axis=0), core * half, axis=0)

    gains = sum_all(
        jnp.concatenate(
            [
                back_around(attn_gain_part),
                back_around(ffn_gain_part),
                query_gain_part,
                key_gain_part,
            ]
        ),
        dp,
    )

    def columns_of(blocks, start, stop):
        return jnp.concatenate([b[:, start:stop] for b in blocks], axis=1)

    def ffn_columns(which):
        return jnp.concatenate(
            [columns_of(blocks, which * ff_sub, (which + 1) * ff_sub) for blocks in ffn_grads],
            axis=1,
        )

    return (
        whole_rows(mixed),
        whole_rows(input_grad),
        gains[:width],
        gains[width : 2 * width],
        gains[2 * width : 2 * width + head_dim],
        gains[2 * width + head_dim :],
        columns_of(qkv_grads, 0, query_width),
        columns_of(qkv_grads, query_width, query_width + key_width),
        columns_of(qkv_grads, query_width + key_width, query_width + 2 * key_width),
        columns_of(out_grads, 0, query_width),
        ffn_columns(0),
        ffn_columns(1),
        ffn_columns(2),
    )


def solution(mesh):
    dp = mesh.shape["dp"]
    weight = P("dp", "tensor")
    rows = P("dp", None)
    return jax.shard_map(
        lambda *arrays: local(dp, *arrays),
        mesh=mesh,
        in_specs=(rows, rows, rows, P(), P(), P(), P()) + (weight,) * 7,
        out_specs=(rows, rows, P(), P(), P(), P()) + (weight,) * 7,
        check_vma=False,
    )
```

```python
import functools

import jax
import jax.numpy as jnp
from jax import lax
from jax.experimental import pallas as pl
from jax.experimental.pallas import tpu as pltpu
from jax.sharding import PartitionSpec as P

eps = 1e-05
rope_base = 1000000.0
group = 4
sub_count = 2
vmem_limit = 52 * 1024 * 1024


def norm_rows(values, gain):
    scale = lax.rsqrt(jnp.mean(values * values, axis=-1, keepdims=True) + eps)
    return (values * scale * gain, scale)


def norm_back(values, scale, gain, incoming):
    weighted = incoming * gain
    return scale * weighted - values * (scale * scale * scale) * jnp.mean(
        weighted * values, axis=-1, keepdims=True
    )


def positions_of(segment_row):
    row_index = jnp.arange(segment_row.shape[0], dtype=jnp.int32)
    earlier = jnp.concatenate([segment_row[:1] - 1, segment_row[:-1]])
    starts = jnp.where(segment_row != earlier, row_index, jnp.zeros_like(row_index))
    return row_index - lax.cummax(starts, axis=0)


def angles(positions, width, lanes):
    frequency = rope_base ** (-jnp.arange(0, width, 2, dtype=jnp.float32) / width)
    frequency = jnp.tile(frequency, 2 * lanes // width)
    phases = positions.astype(jnp.float32)[..., None] * frequency
    return (jnp.cos(phases), jnp.sin(phases))


def dot_nn(left, right):
    return jnp.dot(left, right, preferred_element_type=jnp.float32)


def dot_nt(left, right):
    return lax.dot_general(
        left, right, (((1,), (1,)), ((), ())), preferred_element_type=jnp.float32
    )


def dot_tn(left, right):
    return lax.dot_general(
        left, right, (((0,), (0,)), ((), ())), preferred_element_type=jnp.float32
    )


def exact_dot(left, right):
    return jnp.dot(
        left, right, preferred_element_type=jnp.float32, precision=lax.Precision.HIGHEST
    )


def kernel_call(body, grid, in_specs, out_specs, out_shape, flops, moved):
    return pl.pallas_call(
        body,
        grid=grid,
        in_specs=in_specs,
        out_specs=out_specs,
        out_shape=out_shape,
        compiler_params=pltpu.CompilerParams(vmem_limit_bytes=vmem_limit),
        cost_estimate=pl.CostEstimate(flops=flops, bytes_accessed=moved, transcendentals=0),
    )


def whole(array):
    rank = len(array.shape)
    return pl.BlockSpec(array.shape, lambda *_: (0,) * rank)


def shape_of(shape, kind):
    return jax.ShapeDtypeStruct(shape, kind)


def turn_heads(values, head_dim):
    lanes = values.shape[-1]
    middle = head_dim // 2
    lane = lax.broadcasted_iota(jnp.int32, values.shape, 1) % head_dim
    ahead = pltpu.roll(values, lanes - middle, 1)
    behind = pltpu.roll(values, middle, 1)
    return jnp.where(lane < middle, -ahead, behind)


def index_pair(rows, columns):
    return (
        lax.broadcasted_iota(jnp.int32, (rows, columns), 0),
        lax.broadcasted_iota(jnp.int32, (rows, columns), 1),
    )


def spread(values, offset, columns, head_dim):
    row, column = index_pair(values.shape[1], columns)
    return exact_dot(values, (row - offset == column % head_dim).astype(jnp.float32))


def fold(values, head_dim):
    row, column = index_pair(values.shape[1], values.shape[1])
    return exact_dot(values, (row % head_dim == column % head_dim).astype(jnp.float32))


def head_mean(values, head_dim):
    row, column = index_pair(values.shape[1], values.shape[1])
    same = (row // head_dim == column // head_dim).astype(jnp.float32)
    return exact_dot(values, same) * (1.0 / head_dim)


def prepare_heads(raw, gain, cosine, sine, head_dim):
    scale = lax.rsqrt(head_mean(raw * raw, head_dim) + eps)
    scaled = raw * scale * gain
    return scaled * cosine + turn_heads(scaled, head_dim) * sine, scale


def prepare_back(raw, scale, gain, cosine, sine, incoming, head_dim):
    turned = incoming * cosine - turn_heads(incoming * sine, head_dim)
    weighted = turned * gain
    grad = scale * weighted - raw * (scale * scale * scale) * head_mean(weighted * raw, head_dim)
    return grad, jnp.sum(turned * raw * scale, axis=0, keepdims=True)


def head_inputs(raw, gains, cosine, sine, head_dim, width):
    query, query_scale = prepare_heads(raw[:, :width], gains[0:1], cosine, sine, head_dim)
    rest = raw[:, width:]
    key_raw = spread(rest, 0, width, head_dim)
    key, key_scale = prepare_heads(key_raw, gains[1:2], cosine, sine, head_dim)
    value = spread(rest, head_dim, width, head_dim).astype(jnp.bfloat16)
    return (
        query.astype(jnp.bfloat16),
        query_scale,
        key_raw,
        key.astype(jnp.bfloat16),
        key_scale,
        value,
    )


def only_head(values, head, head_dim):
    lane = lax.broadcasted_iota(jnp.int32, values.shape, 1)
    return jnp.where(lane // head_dim == head, values, jnp.zeros_like(values))


def softmax_of(query_h, key, allowed):
    scores = 0.125 * dot_nt(query_h, key)
    scores = jnp.where(allowed, scores, -1000000000.0)
    exps = jnp.exp(scores - jnp.max(scores, axis=-1, keepdims=True))
    return exps * (1.0 / jnp.sum(exps, axis=-1, keepdims=True))


def block_product(kept, other, blocks, start, stop):
    rows = blocks[0].shape[0]
    total = None
    for k, block in enumerate(blocks):
        left = jnp.concatenate(
            [kept[:, k * rows : (k + 1) * rows], other[:, k * rows : (k + 1) * rows]], axis=0
        )
        more = dot_nn(left, block[:, start:stop])
        total = more if total is None else total + more
    return total


def allowed_of(start_ref, index_column, index_row):
    key_index = index_row[...]
    return (key_index <= index_column[...]) & (key_index >= start_ref[0])


def attention_forward(count, head_dim, width, *refs):
    kept, other, cosine_ref, sine_ref, start_ref, index_column, index_row, gains = refs[:8]
    blocks = refs[8 : 8 + count]
    raw_ref, heads_ref, part_kept, part_other = refs[8 + count :]
    half = kept.shape[0]
    attn_width = raw_ref.shape[-1]
    raw = block_product(kept, other, blocks, 0, attn_width)
    raw_ref[0, 0] = raw[:half]
    raw_ref[1, 0] = raw[half:]
    repeat = width // cosine_ref.shape[-1]
    cosine = jnp.concatenate([cosine_ref[0]] * repeat, axis=1)
    sine = jnp.concatenate([sine_ref[0]] * repeat, axis=1)
    query, _, _, key, _, value = head_inputs(raw, gains[...], cosine, sine, head_dim, width)
    allowed = allowed_of(start_ref, index_column, index_row)
    heads = jnp.zeros((2 * half, width), jnp.float32)
    for head in range(width // head_dim):
        probs = softmax_of(only_head(query, head, head_dim), key, allowed).astype(jnp.bfloat16)
        heads = heads + only_head(dot_nn(probs, value), head, head_dim)
    heads = heads.astype(jnp.bfloat16)
    heads_ref[0, 0] = heads[:half]
    heads_ref[1, 0] = heads[half:]
    rows = blocks[0].shape[0]
    for k, block in enumerate(blocks):
        out = dot_nt(heads, block[:, attn_width : attn_width + width]).astype(jnp.bfloat16)
        part_kept[:, k * rows : (k + 1) * rows] = out[:half]
        part_other[:, k * rows : (k + 1) * rows] = out[half:]


def attention_backward(count, head_dim, width, *refs):
    kept, other, raw_ref, cosine_ref, sine_ref, start_ref, index_column, index_row, gains = refs[:9]
    blocks = refs[9 : 9 + count]
    grad_ref, gain_ref = refs[9 + count :]
    half = kept.shape[0]
    attn_width = raw_ref.shape[-1]
    heads_grad = block_product(kept, other, blocks, attn_width, attn_width + width)
    heads_grad = heads_grad.astype(jnp.bfloat16)
    raw = jnp.concatenate([raw_ref[0, 0], raw_ref[1, 0]], axis=0)
    repeat = width // cosine_ref.shape[-1]
    cosine = jnp.concatenate([cosine_ref[0]] * repeat, axis=1)
    sine = jnp.concatenate([sine_ref[0]] * repeat, axis=1)
    query, query_scale, key_raw, key, key_scale, value = head_inputs(
        raw, gains[...], cosine, sine, head_dim, width
    )
    allowed = allowed_of(start_ref, index_column, index_row)
    zero = jnp.zeros((2 * half, width), jnp.float32)
    query_grad, key_grad, value_grad = zero, zero, zero
    for head in range(width // head_dim):
        query_h = only_head(query, head, head_dim)
        grad_h = only_head(heads_grad, head, head_dim)
        probs_f = softmax_of(query_h, key, allowed)
        value_grad = value_grad + dot_tn(probs_f.astype(jnp.bfloat16), grad_h)
        probs_grad = dot_nt(grad_h, value)
        inner = jnp.sum(probs_f * probs_grad, axis=-1, keepdims=True)
        score_grad = (probs_f * (probs_grad - inner)).astype(jnp.bfloat16)
        query_grad = query_grad + only_head(dot_nn(score_grad, key), head, head_dim)
        key_grad = key_grad + dot_tn(score_grad, query_h)
    query_grad, query_gain_part = prepare_back(
        raw[:, :width], query_scale, gains[0:1], cosine, sine, 0.125 * query_grad, head_dim
    )
    key_grad, key_gain_part = prepare_back(
        key_raw, key_scale, gains[1:2], cosine, sine, 0.125 * fold(key_grad, head_dim), head_dim
    )
    value_grad = fold(value_grad, head_dim)
    rest = attn_width - width
    lane = lax.broadcasted_iota(jnp.int32, (2 * half, rest), 1)
    rest_grad = jnp.where(lane < head_dim, key_grad[:, :rest], value_grad[:, :rest])
    query_grad = query_grad.astype(jnp.bfloat16)
    rest_grad = rest_grad.astype(jnp.bfloat16)
    for side in range(2):
        rows = slice(side * half, (side + 1) * half)
        grad_ref[side, 0, :, :width] = query_grad[rows]
        grad_ref[side, 0, :, width:] = rest_grad[rows]
    parts = jnp.concatenate([query_gain_part, key_gain_part], axis=0)

    @pl.when(pl.program_id(0) == 0)
    def _():
        gain_ref[...] = parts

    @pl.when(pl.program_id(0) != 0)
    def _():
        gain_ref[...] = gain_ref[...] + parts


def run_attention(forward, pair, blocks, tables, gains, head_dim, width, attn_width, raw=None):
    half = pair[0].shape[0] // group
    model = pair[0].shape[1]
    cosine, sine, starts, index = tables
    rows = pl.BlockSpec((half, model), lambda s: (s, 0))
    halves = lambda n: pl.BlockSpec((2, 1, half, n), lambda s: (0, s, 0, 0))
    per_sequence = lambda a: pl.BlockSpec((1,) + a.shape[1:], lambda s: (s, 0, 0))
    column, row = index[:, None], index[None, :]
    common = [cosine, sine, starts, column, row, gains]
    common_specs = [per_sequence(cosine), per_sequence(sine), per_sequence(starts)]
    common_specs += [whole(column), whole(row), whole(gains)]
    flops = 2 * 2 * group * half * model * attn_width
    if forward:
        return kernel_call(
            functools.partial(attention_forward, len(blocks), head_dim, width),
            (group,),
            [rows, rows] + common_specs + [whole(b) for b in blocks],
            [halves(attn_width), halves(width), rows, rows],
            [
                shape_of((2, group, half, attn_width), jnp.float32),
                shape_of((2, group, half, width), jnp.bfloat16),
                shape_of((group * half, model), jnp.bfloat16),
                shape_of((group * half, model), jnp.bfloat16),
            ],
            flops,
            16 * group * half * model,
        )(*pair, *common, *blocks)
    return kernel_call(
        functools.partial(attention_backward, len(blocks), head_dim, width),
        (group,),
        [rows, rows, halves(attn_width)] + common_specs + [whole(b) for b in blocks],
        [halves(attn_width), pl.BlockSpec((2, width), lambda s: (0, 0))],
        [
            shape_of((2, group, half, attn_width), jnp.bfloat16),
            shape_of((2, width), jnp.float32),
        ],
        flops,
        16 * group * half * model,
    )(*pair, raw, *common, *blocks)


def ffn_units(count, ff_sub, *refs):
    normed, out = refs[0:2], refs[2:4]
    blocks = refs[4 : 4 + count]
    inner_refs, grad_refs = refs[4 + count : 6 + count], refs[6 + count :]
    tile = normed[0].shape[0]
    gate_up = block_product(normed[0], normed[1], blocks, 0, 2 * ff_sub)
    inner_grad = block_product(out[0], out[1], blocks, 2 * ff_sub, 3 * ff_sub)
    gate, up = gate_up[:, :ff_sub], gate_up[:, ff_sub:]
    sigmoid = 1.0 / (1.0 + jnp.exp(-gate))
    silu = gate * sigmoid
    inner = (silu * up).astype(jnp.bfloat16)
    gate_grad = (inner_grad * up * sigmoid * (1.0 + gate * (1.0 - sigmoid))).astype(jnp.bfloat16)
    up_grad = (inner_grad * silu).astype(jnp.bfloat16)
    for side in range(2):
        rows = slice(side * tile, (side + 1) * tile)
        inner_refs[side][...] = inner[rows]
        grad_refs[side][:, :ff_sub] = gate_grad[rows]
        grad_refs[side][:, ff_sub:] = up_grad[rows]


def run_ffn_units(normed, out, blocks, ff_sub):
    tokens, model = normed[0].shape
    tile = min(256, tokens)
    rows = lambda n: pl.BlockSpec((tile, n), lambda i: (i, 0))
    return kernel_call(
        functools.partial(ffn_units, len(blocks), ff_sub),
        (tokens // tile,),
        [rows(model)] * 4 + [whole(b) for b in blocks],
        [rows(ff_sub)] * 2 + [rows(2 * ff_sub)] * 2,
        [shape_of((tokens, ff_sub), jnp.bfloat16)] * 2
        + [shape_of((tokens, 2 * ff_sub), jnp.bfloat16)] * 2,
        12 * tokens * model * ff_sub,
        8 * tokens * model,
    )(*normed, *out, *blocks)


def weight_gradients(count, per, *refs):
    first, second = refs[0:2], refs[2:4]
    first_grad, second_grad = refs[4:6], refs[6:8]
    outs = refs[8:]
    one = dot_tn(first[0][...], first_grad[0][...]) + dot_tn(first[1][...], first_grad[1][...])
    two = dot_tn(second[0][...], second_grad[0][...]) + dot_tn(second[1][...], second_grad[1][...])
    width = one.shape[1]
    for k in range(count):

        @pl.when(pl.program_id(0) // per == k)
        def _(k=k):
            outs[k][:, :width] = one.astype(jnp.bfloat16)
            outs[k][:, width:] = two.astype(jnp.bfloat16)


def run_weight_gradients(first, first_grad, second, second_grad, count):
    tokens, model = first[0].shape
    block_rows = model // count
    tile = min(256, block_rows)
    per = block_rows // tile
    width = first_grad[0].shape[1] + second_grad[0].shape[1]
    columns = pl.BlockSpec((tokens, tile), lambda i: (0, i))
    out_spec = lambda k: pl.BlockSpec(
        (tile, width), lambda i: (jnp.clip(i - per * k, 0, per - 1), 0)
    )
    return kernel_call(
        functools.partial(weight_gradients, count, per),
        (model // tile,),
        [columns] * 4 + [whole(a) for a in (*first_grad, *second_grad)],
        [out_spec(k) for k in range(count)],
        [shape_of((block_rows, width), jnp.bfloat16)] * count,
        4 * tokens * model * width,
        8 * tokens * model,
    )(*first, *second, *first_grad, *second_grad)


def transposed_product(parts, count, *refs):
    lefts = refs[: 2 * parts]
    blocks = refs[2 * parts : 2 * parts + parts * count]
    outs = refs[2 * parts + parts * count :]
    tile = lefts[0].shape[0]
    rows = blocks[0].shape[0]
    for k in range(count):
        total = None
        for p in range(parts):
            left = jnp.concatenate([lefts[2 * p][...], lefts[2 * p + 1][...]], axis=0)
            more = dot_nt(left, blocks[p * count + k][...])
            total = more if total is None else total + more
        total = total.astype(jnp.bfloat16)
        outs[0][:, k * rows : (k + 1) * rows] = total[:tile]
        outs[1][:, k * rows : (k + 1) * rows] = total[tile:]


def run_transposed_product(pairs, blocks, column, columns):
    count = len(blocks[0])
    tokens = pairs[0][0].shape[0]
    model = count * blocks[0][0].shape[0]
    tile = min(256, tokens)
    rows = lambda n: pl.BlockSpec((tile, n), lambda i: (i, 0))
    lefts = [a for pair in pairs for a in pair]
    flat = [b for one in blocks for b in one]
    return kernel_call(
        functools.partial(transposed_product, len(pairs), count),
        (tokens // tile,),
        [rows(a.shape[1]) for a in lefts]
        + [pl.BlockSpec((b.shape[0], columns), lambda i: (0, column)) for b in flat],
        [rows(model)] * 2,
        [shape_of((tokens, model), jnp.bfloat16)] * 2,
        4 * tokens * model * columns * len(pairs),
        8 * tokens * model,
    )(*lefts, *flat)


def place_halves(place, mine, other, out):
    half = mine.shape[0]
    core = place[0]
    out[pl.ds(core * half, half), :] = mine[...]
    out[pl.ds((1 - core) * half, half), :] = other[...]


def run_place_halves(core, spot, count, mine, other):
    half, model = mine.shape
    block = model // count
    source = pl.BlockSpec((half, block), lambda k, place: (0, k))
    return pl.pallas_call(
        place_halves,
        grid_spec=pltpu.PrefetchScalarGridSpec(
            num_scalar_prefetch=1,
            grid=(count,),
            in_specs=[source, source],
            out_specs=pl.BlockSpec((2 * half, block), lambda k, place: (0, (k + place[1]) % count)),
        ),
        out_shape=shape_of((2 * half, model), jnp.float32),
        compiler_params=pltpu.CompilerParams(vmem_limit_bytes=vmem_limit),
        cost_estimate=pl.CostEstimate(flops=1, bytes_accessed=16 * half * model, transcendentals=0),
    )(jnp.stack([core, spot]).astype(jnp.int32), mine, other)


def swap_cores(values):
    return lax.ppermute(values, "tensor", [(0, 1), (1, 0)])


class Lines:
    def __init__(self, dp):
        self.dp = dp
        self.length = dp // group
        index = lax.axis_index("dp")
        self.place = index % group
        self.spot = index // group

    def flip(self, values, relation):
        return lax.ppermute(values, "dp", [(i, i ^ relation) for i in range(self.dp)])

    def hop(self, values, first, last, step):
        pairs = [
            (spot * group + place, (spot + step) * group + place)
            for spot in range(first, last + 1)
            for place in range(group)
        ]
        return lax.ppermute(values, "dp", pairs)

    def turn(self, values, step):
        pairs = [
            (spot * group + place, ((spot + step) % self.length) * group + place)
            for spot in range(self.length)
            for place in range(group)
        ]
        return lax.ppermute(values, "dp", pairs)

    def by_place(self, related):
        odd = self.place % 2 == 1
        high = self.place // 2 == 1
        own, one, two, three = related
        pairs = (
            (jnp.where(odd, one, own), jnp.where(odd, own, one)),
            (jnp.where(odd, three, two), jnp.where(odd, two, three)),
        )
        return [
            jnp.where(high, pairs[1][0], pairs[0][0]),
            jnp.where(high, pairs[1][1], pairs[0][1]),
            jnp.where(high, pairs[0][0], pairs[1][0]),
            jnp.where(high, pairs[0][1], pairs[1][1]),
        ]

    def pieces(self, piece_of):
        return [piece_of(self.place ^ relation) for relation in range(group)]

    def flip_pieces(self, pieces):
        return [pieces[0]] + [self.flip(pieces[r], r) for r in range(1, group)]

    def row_pieces(self, total):
        rows = total.shape[0] // group
        return [
            lax.dynamic_slice_in_dim(total, (self.place ^ r) * rows, rows) for r in range(group)
        ]

    def gather_near(self, mine):
        return [self.flip(mine, 1), self.flip(mine, 2)]

    def gather_across(self, near):
        middle = near[0].shape[0] // 2
        return [self.flip(near[0][:middle], 2), self.flip(near[1][middle:], 1)]

    def scatter_across(self, across):
        middle = across.shape[0] // 2
        return [self.flip(across[:middle], 1), self.flip(across[middle:], 2)]

    def gather_far(self, mine):
        near = self.gather_near(mine)
        return near, self.gather_across(near)

    def gather_tokens(self, mine):
        return self.both_cores(mine, *self.gather_far(mine))

    def both_cores(self, mine, near, across):
        kept = jnp.concatenate([mine] + near + across)
        return kept, swap_cores(kept)

    def terms(self, kept, other, relation):
        rows = kept.shape[0] // group
        span = slice(relation * rows, (relation + 1) * rows)
        return kept[span].astype(jnp.float32) + other[span].astype(jnp.float32)

    def across_terms(self, kept, other):
        return self.scatter_across(self.terms(kept, other, 3).astype(jnp.bfloat16))

    def near_terms(self, kept, other, got):
        one, two = self.terms(kept, other, 1), self.terms(kept, other, 2)
        middle = one.shape[0] // 2
        one = jnp.concatenate([one[:middle], one[middle:] + got[1].astype(jnp.float32)])
        two = jnp.concatenate([two[:middle] + got[0].astype(jnp.float32), two[middle:]])
        one = self.flip(one.astype(jnp.bfloat16), 1)
        two = self.flip(two.astype(jnp.bfloat16), 2)
        return self.terms(kept, other, 0) + one.astype(jnp.float32) + two.astype(jnp.float32)

    def scatter_tokens(self, kept, other):
        return self.near_terms(kept, other, self.across_terms(kept, other))


class LineGather:
    def __init__(self, lines, block):
        self.lines, self.block, self.got = lines, block, []

    def hop(self):
        lines, step = self.lines, len(self.got) + 1
        if lines.length != 4:
            turns = range(1, lines.length) if step == 1 else ()
            self.got.append([lines.turn(self.block, -k) for k in turns])
            return
        up, down = self.got[-1] if self.got else (self.block, self.block)
        self.got.append(
            [
                lines.hop(up, step - 1, lines.length - 2, 1),
                lines.hop(down, 1, lines.length - step, -1),
            ]
        )

    def blocks(self):
        lines = self.lines
        if lines.length != 4:
            return [self.block] + self.got[0]
        return [self.block] + [
            jnp.where(
                lines.spot + k < lines.length,
                self.got[k - 1][1],
                self.got[lines.length - k - 1][0],
            )
            for k in range(1, lines.length)
        ]


class LineScatter:
    def __init__(self, lines, blocks):
        self.lines, self.blocks, self.got = lines, blocks, []

    def hop(self):
        lines, step = self.lines, len(self.got) + 1
        if lines.length != 4:
            turns = range(1, lines.length) if step == 1 else ()
            self.got.append([lines.turn(self.blocks[k], k) for k in turns])
            return
        up, down = self.blocks[lines.length - step], self.blocks[step]
        if self.got:
            up, down = add(up, self.got[-1][0]), add(down, self.got[-1][1])
        self.got.append(
            [
                lines.hop(up, 0, min(step - 1, lines.length - 2), 1),
                lines.hop(down, max(lines.length - step, 1), lines.length - 1, -1),
            ]
        )

    def total(self):
        last = self.got[-1] if self.lines.length == 4 else self.got[0]
        result = self.blocks[0].astype(jnp.float32)
        for one in last:
            result = result + one.astype(jnp.float32)
        return result.astype(jnp.bfloat16)


def add(left, right):
    return (left.astype(jnp.float32) + right.astype(jnp.float32)).astype(jnp.bfloat16)


def tie(*values):
    return lax.optimization_barrier(values)


def sum_all(values, dp):
    bit = 1
    while bit < dp:
        values = values + lax.ppermute(values, "dp", [(i, i ^ bit) for i in range(dp)])
        bit *= 2
    return values + swap_cores(values)


def local(
    dp,
    tokens,
    segments,
    cotangent,
    attn_gain,
    ffn_gain,
    query_gain,
    key_gain,
    w_query,
    key_weight,
    value_weight,
    w_out,
    w_gate,
    w_up,
    w_down,
):
    lines = Lines(dp)
    core = lax.axis_index("tensor")
    length, width = tokens.shape
    half = length // 2
    head_dim = query_gain.shape[0]
    rows = w_query.shape[0]
    block_rows = rows * group
    query_width = w_query.shape[1] // group
    key_width = key_weight.shape[1] // group
    attn_width = query_width + 2 * key_width
    ff_sub = w_gate.shape[1] // group // sub_count

    def around(values):
        return jnp.roll(values, -lines.spot * block_rows, axis=-1)

    def back_around(values):
        return jnp.roll(values, lines.spot * block_rows, axis=-1)

    def halves(values, axis=0):
        return jnp.roll(values, -core * half, axis=axis)

    attn_gain_r, ffn_gain_r = around(attn_gain), around(ffn_gain)

    def columns(weight, start, size):
        return lax.dynamic_slice_in_dim(weight, start, size, axis=1)

    attn_pieces = lines.pieces(
        lambda j: jnp.concatenate(
            [
                columns(w_query, j * query_width, query_width),
                columns(key_weight, j * key_width, key_width),
                columns(value_weight, j * key_width, key_width),
                columns(w_out, j * query_width, query_width),
            ],
            axis=1,
        )
    )
    attn_shared = lines.flip_pieces(attn_pieces)
    source = around(lax.dynamic_slice_in_dim(tokens, core * half, half)).astype(jnp.float32)
    normed_f, scale_first = norm_rows(source, attn_gain_r)
    normed_mine = normed_f.astype(jnp.bfloat16)

    seg_all = jnp.stack([segments[0]] + [lines.flip(segments, r)[0] for r in range(1, group)])
    positions = halves(jax.vmap(positions_of)(seg_all), axis=1)
    index = halves(jnp.arange(length, dtype=jnp.int32))
    cosine, sine = angles(positions, head_dim, 2 * head_dim)
    tables = (cosine, sine, (index[None] - positions)[..., None], index)
    gains_two = jnp.stack(
        [
            jnp.tile(query_gain, query_width // head_dim),
            jnp.tile(key_gain, query_width // head_dim),
        ]
    )

    def ffn_piece(s):
        return lines.pieces(
            lambda j: jnp.concatenate(
                [
                    columns(weight, s * group * ff_sub + j * ff_sub, ff_sub)
                    for weight in (w_gate, w_up, w_down)
                ],
                axis=1,
            )
        )

    pieces_0, pieces_1 = ffn_piece(0), ffn_piece(1)
    cot_half = around(lax.dynamic_slice_in_dim(cotangent, core * half, half))
    out_mine = cot_half.astype(jnp.bfloat16)
    attn_shared, normed_mine, pieces_0, out_mine = tie(attn_shared, normed_mine, pieces_0, out_mine)

    attn_line = LineGather(lines, jnp.concatenate(lines.by_place(attn_shared), axis=0))
    attn_line.hop()
    near = lines.gather_near(normed_mine)
    near, attn_line.got[0], pieces_0 = tie(near, attn_line.got[0], pieces_0)
    attn_line.hop()
    across = lines.gather_across(near)
    across, attn_line.got[1], pieces_0, tables = tie(across, attn_line.got[1], pieces_0, tables)
    attn_line.hop()
    normed = lines.both_cores(normed_mine, near, across)
    shared_0 = lines.flip_pieces(pieces_0)
    normed, attn_line.got[2], shared_0, pieces_1, out_mine = tie(
        normed, attn_line.got[2], shared_0, pieces_1, out_mine
    )
    attn_w = attn_line.blocks()

    line_0 = LineGather(lines, jnp.concatenate(lines.by_place(shared_0), axis=0))
    line_0.hop()
    out_near, out_across = lines.gather_far(out_mine)
    qkv_raw, heads_out, attended_kept, attended_other = run_attention(
        True, normed, attn_w, tables, gains_two, head_dim, query_width, attn_width
    )
    attended_other, line_0.got[0], out_near, out_across, pieces_1 = tie(
        attended_other, line_0.got[0], out_near, out_across, pieces_1
    )

    line_0.hop()
    shared_1 = lines.flip_pieces(pieces_1)
    attended_other = swap_cores(attended_other)
    attended_other, shared_1 = tie(attended_other, shared_1)
    out_b = lines.both_cores(out_mine, out_near, out_across)
    attended = lines.scatter_tokens(attended_kept, attended_other)
    attended, line_0.got[1], out_b, shared_1 = tie(attended, line_0.got[1], out_b, shared_1)

    line_0.hop()
    line_1 = LineGather(lines, jnp.concatenate(lines.by_place(shared_1), axis=0))
    state = source + attended
    normed2_f, scale_second = norm_rows(state, ffn_gain_r)
    near, across = lines.gather_far(normed2_f.astype(jnp.bfloat16))
    near, across, line_0.got[2], line_1.block = tie(near, across, line_0.got[2], line_1.block)

    line_1.hop()
    normed2 = lines.both_cores(normed2_f.astype(jnp.bfloat16), near, across)
    ffn_w = [line_0.blocks()]
    units_0 = run_ffn_units(normed2, out_b, ffn_w[0], ff_sub)
    units_0, line_1.got[0] = tie(units_0, line_1.got[0])
    line_1.hop()
    ffn_g = run_weight_gradients(normed2, units_0[2:], out_b, units_0[:2], lines.length)
    ffn_g, line_1.got[1], units_0 = tie(ffn_g, line_1.got[1], units_0)
    line_1.hop()
    sum_0 = LineScatter(lines, ffn_g)
    line_1.got[2], sum_0.blocks = tie(line_1.got[2], sum_0.blocks)
    ffn_w.append(line_1.blocks())

    sum_0.hop()
    units_1 = run_ffn_units(normed2, out_b, ffn_w[1], ff_sub)
    kept, other = run_transposed_product([units_0[2:], units_1[2:]], ffn_w, 0, 2 * ff_sub)
    kept, other, sum_0.got[0], units_1 = tie(kept, other, sum_0.got[0], units_1)

    sum_0.hop()
    other = swap_cores(other)
    got = lines.across_terms(kept, other)
    got, units_1 = tie(got, units_1)
    sum_1 = LineScatter(
        lines, run_weight_gradients(normed2, units_1[2:], out_b, units_1[:2], lines.length)
    )
    normed2_grad = lines.near_terms(kept, other, got)
    normed2_grad, sum_0.got[1], sum_1.blocks, units_0, units_1 = tie(
        normed2_grad, sum_0.got[1], sum_1.blocks, units_0, units_1
    )

    sum_0.hop()
    ffn_gain_part = jnp.sum(normed2_grad * state * scale_second, axis=0)
    state_grad = cot_half + norm_back(state, scale_second, ffn_gain_r, normed2_grad)
    grad_mine = state_grad.astype(jnp.bfloat16)
    near = lines.gather_near(grad_mine)
    branch_kept, branch_other = run_transposed_product(
        [units_0[:2], units_1[:2]], ffn_w, 2, ff_sub
    )
    near, branch_kept, branch_other = tie(near, branch_kept, branch_other)
    across = lines.gather_across(near)
    across, sum_0.got[2], branch_kept, branch_other = tie(
        across, sum_0.got[2], branch_kept, branch_other
    )

    sum_1.hop()
    attended_b = lines.both_cores(grad_mine, near, across)

    def owners_rows(total):
        return lines.flip_pieces(lines.row_pieces(total))

    branch = lines.scatter_tokens(branch_kept, swap_cores(branch_other))
    ffn_grads = [owners_rows(sum_0.total())]
    qkv_grad, gain_parts = run_attention(
        False, attended_b, attn_w, tables, gains_two, head_dim, query_width, attn_width, qkv_raw
    )
    qkv_grad, ffn_grads[0], branch, sum_1.got[0] = tie(
        qkv_grad, ffn_grads[0], branch, sum_1.got[0]
    )

    sum_1.hop()
    qkv_grad = tuple(qkv_grad.reshape(2, group * half, attn_width))
    heads_out = tuple(heads_out.reshape(2, group * half, query_width))
    kept, other = run_transposed_product([qkv_grad], [attn_w], 0, attn_width)
    other = swap_cores(other)
    got = lines.across_terms(kept, other)
    attn_sum = LineScatter(
        lines, run_weight_gradients(normed, qkv_grad, attended_b, heads_out, lines.length)
    )
    got, sum_1.got[1], attn_sum.blocks = tie(got, sum_1.got[1], attn_sum.blocks)
    attn_sum.hop()
    sum_1.hop()
    normed_grad = lines.near_terms(kept, other, got)
    normed_grad, attn_sum.got[0], sum_1.got[2] = tie(normed_grad, attn_sum.got[0], sum_1.got[2])
    attn_sum.hop()
    attn_sum.hop()
    ffn_grads.append(owners_rows(sum_1.total()))
    attn_grads = owners_rows(attn_sum.total())
    mixed = state + branch
    attn_gain_part = jnp.sum(normed_grad * source * scale_first, axis=0)
    input_grad = state_grad + norm_back(source, scale_first, attn_gain_r, normed_grad)

    def whole_rows(mine):
        return run_place_halves(core, lines.spot, lines.length, mine, swap_cores(mine))

    gains = sum_all(
        jnp.concatenate(
            [
                back_around(attn_gain_part),
                back_around(ffn_gain_part),
                jnp.sum(gain_parts[0].reshape(-1, head_dim), axis=0),
                gain_parts[1][:head_dim],
            ]
        ),
        dp,
    )

    def columns_of(related, start, stop):
        blocks = lines.by_place([b[:, start:stop] for b in related])
        return jnp.concatenate(blocks, axis=1).astype(jnp.float32)

    def ffn_columns(which):
        return jnp.concatenate(
            [columns_of(blocks, which * ff_sub, (which + 1) * ff_sub) for blocks in ffn_grads],
            axis=1,
        )

    return (
        whole_rows(mixed),
        whole_rows(input_grad),
        gains[:width],
        gains[width : 2 * width],
        gains[2 * width : 2 * width + head_dim],
        gains[2 * width + head_dim :],
        columns_of(attn_grads, 0, query_width),
        columns_of(attn_grads, query_width, query_width + key_width),
        columns_of(attn_grads, query_width + key_width, attn_width),
        columns_of(attn_grads, attn_width, attn_width + query_width),
        ffn_columns(0),
        ffn_columns(1),
        ffn_columns(2),
    )


def solution(mesh):
    dp = mesh.shape["dp"]
    weight = P("dp", "tensor")
    rows = P("dp", None)
    return jax.shard_map(
        lambda *arrays: local(dp, *arrays),
        mesh=mesh,
        in_specs=(rows, rows, rows, P(), P(), P(), P()) + (weight,) * 7,
        out_specs=(rows, rows, P(), P(), P(), P()) + (weight,) * 7,
        check_vma=False,
    )
```

```python
import functools

import jax
import jax.numpy as jnp
from jax import lax
from jax.experimental import pallas as pl
from jax.experimental.pallas import tpu as pltpu
from jax.sharding import PartitionSpec as P

eps = 1e-05
rope_base = 1000000.0
group = 4
sub_count = 2
vmem_limit = 52 * 1024 * 1024


def norm_rows(values, gain):
    scale = lax.rsqrt(jnp.mean(values * values, axis=-1, keepdims=True) + eps)
    return (values * scale * gain, scale)


def norm_back(values, scale, gain, incoming):
    weighted = incoming * gain
    return scale * weighted - values * (scale * scale * scale) * jnp.mean(
        weighted * values, axis=-1, keepdims=True
    )


def positions_of(segment_row):
    row_index = jnp.arange(segment_row.shape[0], dtype=jnp.int32)
    earlier = jnp.concatenate([segment_row[:1] - 1, segment_row[:-1]])
    starts = jnp.where(segment_row != earlier, row_index, jnp.zeros_like(row_index))
    return row_index - lax.cummax(starts, axis=0)


def angles(positions, width, lanes):
    frequency = rope_base ** (-jnp.arange(0, width, 2, dtype=jnp.float32) / width)
    frequency = jnp.tile(frequency, 2 * lanes // width)
    phases = positions.astype(jnp.float32)[..., None] * frequency
    return (jnp.cos(phases), jnp.sin(phases))


def dot_nn(left, right):
    return jnp.dot(left, right, preferred_element_type=jnp.float32)


def dot_nt(left, right):
    return lax.dot_general(
        left, right, (((1,), (1,)), ((), ())), preferred_element_type=jnp.float32
    )


def dot_tn(left, right):
    return lax.dot_general(
        left, right, (((0,), (0,)), ((), ())), preferred_element_type=jnp.float32
    )


def pick_dot(left, right):
    high = left.astype(jnp.bfloat16)
    low = (left - high.astype(jnp.float32)).astype(jnp.bfloat16)
    return dot_nn(high, right) + dot_nn(low, right)


def kernel_call(body, grid, in_specs, out_specs, out_shape, flops, moved):
    return pl.pallas_call(
        body,
        grid=grid,
        in_specs=in_specs,
        out_specs=out_specs,
        out_shape=out_shape,
        compiler_params=pltpu.CompilerParams(vmem_limit_bytes=vmem_limit),
        cost_estimate=pl.CostEstimate(flops=flops, bytes_accessed=moved, transcendentals=0),
    )


def whole(array):
    rank = len(array.shape)
    return pl.BlockSpec(array.shape, lambda *_: (0,) * rank)


def shape_of(shape, kind):
    return jax.ShapeDtypeStruct(shape, kind)


def turn_heads(values, head_dim):
    lanes = values.shape[-1]
    middle = head_dim // 2
    lane = lax.broadcasted_iota(jnp.int32, values.shape, 1) % head_dim
    ahead = pltpu.roll(values, lanes - middle, 1)
    behind = pltpu.roll(values, middle, 1)
    return jnp.where(lane < middle, -ahead, behind)


def index_pair(rows, columns):
    return (
        lax.broadcasted_iota(jnp.int32, (rows, columns), 0),
        lax.broadcasted_iota(jnp.int32, (rows, columns), 1),
    )


def ones_where(condition):
    return condition.astype(jnp.float32).astype(jnp.bfloat16)


def spread_of(rows, offset, columns, head_dim):
    row, column = index_pair(rows, columns)
    return ones_where(row - offset == column % head_dim)


def fold(values, head_dim):
    row, column = index_pair(values.shape[1], values.shape[1])
    return pick_dot(values, ones_where(row % head_dim == column % head_dim))


def head_mean(values, head_dim):
    row, column = index_pair(values.shape[1], values.shape[1])
    return pick_dot(values, ones_where(row // head_dim == column // head_dim)) * (1.0 / head_dim)


def prepare_heads(raw, gain, cosine, sine, head_dim):
    scale = lax.rsqrt(head_mean(raw * raw, head_dim) + eps)
    scaled = raw * scale * gain
    return scaled * cosine + turn_heads(scaled, head_dim) * sine, scale


def prepare_back(raw, scale, gain, cosine, sine, incoming, head_dim):
    turned = incoming * cosine - turn_heads(incoming * sine, head_dim)
    weighted = turned * gain
    grad = scale * weighted - raw * (scale * scale * scale) * head_mean(weighted * raw, head_dim)
    return grad, jnp.sum(turned * raw * scale, axis=0, keepdims=True)


def head_inputs(raw, gains, cosine, sine, head_dim, width):
    query, query_scale = prepare_heads(raw[:, :width], gains[0:1], cosine, sine, head_dim)
    rest = raw[:, width:]
    key_raw = pick_dot(rest, spread_of(rest.shape[1], 0, width, head_dim))
    key, key_scale = prepare_heads(key_raw, gains[1:2], cosine, sine, head_dim)
    value = dot_nn(
        rest.astype(jnp.bfloat16), spread_of(rest.shape[1], head_dim, width, head_dim)
    ).astype(jnp.bfloat16)
    return (
        query.astype(jnp.bfloat16) * jnp.bfloat16(0.125),
        query_scale,
        key_raw,
        key.astype(jnp.bfloat16),
        key_scale,
        value,
    )


def only_head(values, head, head_dim):
    lane = lax.broadcasted_iota(jnp.int32, values.shape, 1)
    return jnp.where(lane // head_dim == head, values, jnp.zeros_like(values))


def exps_of(scores, allowed):
    return jnp.exp(jnp.where(allowed, scores, -1000000000.0))


def block_product(kept, other, blocks, start, stop):
    rows = blocks[0].shape[0]
    total = None
    for k, block in enumerate(blocks):
        left = jnp.concatenate(
            [kept[:, k * rows : (k + 1) * rows], other[:, k * rows : (k + 1) * rows]], axis=0
        )
        more = dot_nn(left, block[:, start:stop])
        total = more if total is None else total + more
    return total


def by_halves(swapped, one, two):
    return jnp.where(swapped, two, one), jnp.where(swapped, one, two)


def head_tables(cosine_ref, sine_ref, width):
    repeat = width // cosine_ref.shape[-1]
    return (
        jnp.concatenate([cosine_ref[0]] * repeat, axis=1),
        jnp.concatenate([sine_ref[0]] * repeat, axis=1),
    )


def attention_forward(count, head_dim, width, *refs):
    kept, other = refs[:2]
    refs = refs[2:]
    swap_ref, cosine_ref, sine_ref, start_ref, index_column, index_row, gains = refs[:7]
    blocks = refs[7 : 7 + count]
    raw_ref, heads_kept, heads_other, part_kept, part_other = refs[7 + count :]
    half = kept.shape[0]
    attn_width = raw_ref.shape[-1]
    raw = block_product(kept, other, blocks, 0, attn_width)
    swapped = swap_ref[...] == 1
    raw = jnp.concatenate(by_halves(swapped, raw[:half], raw[half:]), axis=0)
    raw_ref[0] = raw
    cosine, sine = head_tables(cosine_ref, sine_ref, width)
    query, _, _, key, _, value = head_inputs(raw, gains[...], cosine, sine, head_dim, width)
    allowed = (index_row[...] <= index_column[...]) & (index_row[...] >= start_ref[0])
    one = jnp.zeros((half, width), jnp.float32)
    two = one
    for head in range(width // head_dim):
        query_h = only_head(query, head, head_dim)
        for first in (True, False):
            span, keys = (slice(0, half), half) if first else (slice(half, 2 * half), 2 * half)
            exps = exps_of(dot_nt(query_h[span], key[:keys]), allowed[span, :keys])
            part = dot_nn(exps.astype(jnp.bfloat16), value[:keys])
            part = part * (1.0 / jnp.sum(exps, axis=-1, keepdims=True))
            part = only_head(part, head, head_dim)
            if first:
                one = one + part
            else:
                two = two + part
    heads = by_halves(swapped, one.astype(jnp.bfloat16), two.astype(jnp.bfloat16))
    heads_kept[...] = heads[0]
    heads_other[...] = heads[1]
    heads = jnp.concatenate(heads, axis=0)
    rows = blocks[0].shape[0]
    for k, block in enumerate(blocks):
        out = dot_nt(heads, block[:, attn_width : attn_width + width]).astype(jnp.bfloat16)
        part_kept[:, k * rows : (k + 1) * rows] = out[:half]
        part_other[:, k * rows : (k + 1) * rows] = out[half:]


def attention_backward(count, head_dim, width, *refs):
    kept, other, raw_ref = refs[:3]
    refs = refs[3:]
    swap_ref, cosine_ref, sine_ref, start_ref, index_column, index_row, gains = refs[:7]
    blocks = refs[7 : 7 + count]
    grad_kept, grad_other, gain_ref = refs[7 + count :]
    half = kept.shape[0]
    attn_width = raw_ref.shape[-1]
    grads = block_product(kept, other, blocks, attn_width, attn_width + width)
    grads = grads.astype(jnp.bfloat16)
    swapped = swap_ref[...] == 1
    grads = jnp.concatenate(by_halves(swapped, grads[:half], grads[half:]), axis=0)
    raw = raw_ref[0]
    cosine, sine = head_tables(cosine_ref, sine_ref, width)
    query, query_scale, key_raw, key, key_scale, value = head_inputs(
        raw, gains[...], cosine, sine, head_dim, width
    )
    allowed = (index_column[...] <= index_row[...]) & (index_column[...] >= start_ref[0])
    zero = jnp.zeros((half, width), jnp.float32)
    query_grads, key_grads, value_grads = [zero, zero], [zero, zero], [zero, zero]
    for head in range(width // head_dim):
        query_h = only_head(query, head, head_dim)
        grad_h = only_head(grads, head, head_dim)
        for part in range(2):
            span, keys = slice(part * half, (part + 1) * half), (part + 1) * half
            exps = exps_of(dot_nt(key[:keys], query_h[span]), allowed[:keys, span])
            probs_f = exps * (1.0 / jnp.sum(exps, axis=0, keepdims=True))
            weighted = probs_f * dot_nt(value[:keys], grad_h[span])
            score_grad = weighted - probs_f * jnp.sum(weighted, axis=0, keepdims=True)
            score_grad = score_grad.astype(jnp.bfloat16)
            query_grads[part] += only_head(dot_tn(score_grad, key[:keys]), head, head_dim)
            value_part = dot_nn(probs_f.astype(jnp.bfloat16), grad_h[span])
            key_part = dot_nn(score_grad, query_h[span])
            for block in range(part + 1):
                rows = slice(block * half, (block + 1) * half)
                value_grads[block] += value_part[rows]
                key_grads[block] += key_part[rows]
    query_grad = 0.125 * jnp.concatenate(query_grads, axis=0)
    key_grad = fold(jnp.concatenate(key_grads, axis=0), head_dim)
    value_grad = fold(jnp.concatenate(value_grads, axis=0), head_dim)
    query_grad, query_gain_part = prepare_back(
        raw[:, :width], query_scale, gains[0:1], cosine, sine, query_grad, head_dim
    )
    key_grad, key_gain_part = prepare_back(
        key_raw, key_scale, gains[1:2], cosine, sine, key_grad, head_dim
    )
    rest = attn_width - width
    lane = lax.broadcasted_iota(jnp.int32, (2 * half, rest), 1)
    rest_grad = jnp.where(lane < head_dim, key_grad[:, :rest], value_grad[:, :rest])
    query_grad = query_grad.astype(jnp.bfloat16)
    rest_grad = rest_grad.astype(jnp.bfloat16)
    query_sides = by_halves(swapped, query_grad[:half], query_grad[half:])
    rest_sides = by_halves(swapped, rest_grad[:half], rest_grad[half:])
    for side, out in enumerate((grad_kept, grad_other)):
        out[:, :width] = query_sides[side]
        out[:, width:] = rest_sides[side]
    parts = jnp.concatenate([query_gain_part, key_gain_part], axis=0)

    @pl.when(pl.program_id(0) == 0)
    def _():
        gain_ref[...] = parts

    @pl.when(pl.program_id(0) != 0)
    def _():
        gain_ref[...] = gain_ref[...] + parts


def run_attention(forward, pair, blocks, tables, gains, head_dim, width, attn_width, raw=None):
    half = pair[0].shape[0] // group
    model = pair[0].shape[1]
    swapped, cosine, sine, start_columns, start_rows, index = tables
    starts = start_columns if forward else start_rows
    rows = lambda n: pl.BlockSpec((half, n), lambda s: (s, 0))
    per_sequence = lambda shape: pl.BlockSpec((1,) + shape[1:], lambda s: (s, 0, 0))
    column, row = index[:, None], index[None, :]
    common = [swapped, cosine, sine, starts, column, row, gains]
    common_specs = [whole(swapped)] + [per_sequence(a.shape) for a in (cosine, sine, starts)]
    common_specs += [whole(column), whole(row), whole(gains)]
    common += blocks
    common_specs += [whole(b) for b in blocks]
    raw_shape = (group, 2 * half, attn_width)
    flops = 2 * 2 * group * half * model * attn_width * 10
    moved = 16 * group * half * model
    side = lambda n: shape_of((group * half, n), jnp.bfloat16)
    if forward:
        results = kernel_call(
            functools.partial(attention_forward, len(blocks), head_dim, width),
            (group,),
            [rows(model)] * 2 + common_specs,
            [per_sequence(raw_shape), rows(width), rows(width), rows(model), rows(model)],
            [shape_of(raw_shape, jnp.float32), side(width), side(width), side(model), side(model)],
            flops,
            moved,
        )(*pair, *common)
        return results[0], tuple(results[1:3]), results[3], results[4]
    results = kernel_call(
        functools.partial(attention_backward, len(blocks), head_dim, width),
        (group,),
        [rows(model)] * 2 + [per_sequence(raw_shape)] + common_specs,
        [rows(attn_width), rows(attn_width), pl.BlockSpec((2, width), lambda s: (0, 0))],
        [side(attn_width), side(attn_width), shape_of((2, width), jnp.float32)],
        flops,
        moved,
    )(*pair, raw, *common)
    return tuple(results[:2]), results[2]


def ffn_units(count, ff_sub, *refs):
    normed, out = refs[0:2], refs[2:4]
    blocks = refs[4 : 4 + count]
    inner_refs, grad_refs = refs[4 + count : 6 + count], refs[6 + count :]
    tile = normed[0].shape[0]
    gate_up = block_product(normed[0], normed[1], blocks, 0, 2 * ff_sub)
    inner_grad = block_product(out[0], out[1], blocks, 2 * ff_sub, 3 * ff_sub)
    gate, up = gate_up[:, :ff_sub], gate_up[:, ff_sub:]
    sigmoid = 1.0 / (1.0 + jnp.exp(-gate))
    silu = gate * sigmoid
    inner = (silu * up).astype(jnp.bfloat16)
    gate_grad = (inner_grad * up * sigmoid * (1.0 + gate * (1.0 - sigmoid))).astype(jnp.bfloat16)
    up_grad = (inner_grad * silu).astype(jnp.bfloat16)
    for side in range(2):
        rows = slice(side * tile, (side + 1) * tile)
        inner_refs[side][...] = inner[rows]
        grad_refs[side][:, :ff_sub] = gate_grad[rows]
        grad_refs[side][:, ff_sub:] = up_grad[rows]


def run_ffn_units(normed, out, blocks, ff_sub):
    tokens, model = normed[0].shape
    tile = min(256, tokens)
    rows = lambda n: pl.BlockSpec((tile, n), lambda i: (i, 0))
    return kernel_call(
        functools.partial(ffn_units, len(blocks), ff_sub),
        (tokens // tile,),
        [rows(model)] * 4 + [whole(b) for b in blocks],
        [rows(ff_sub)] * 2 + [rows(2 * ff_sub)] * 2,
        [shape_of((tokens, ff_sub), jnp.bfloat16)] * 2
        + [shape_of((tokens, 2 * ff_sub), jnp.bfloat16)] * 2,
        12 * tokens * model * ff_sub,
        8 * tokens * model,
    )(*normed, *out, *blocks)


def weight_gradients(count, per, *refs):
    first, second = refs[0:2], refs[2:4]
    first_grad, second_grad = refs[4:6], refs[6:8]
    outs = refs[8:]
    one = dot_tn(first[0][...], first_grad[0][...]) + dot_tn(first[1][...], first_grad[1][...])
    two = dot_tn(second[0][...], second_grad[0][...]) + dot_tn(second[1][...], second_grad[1][...])
    width = one.shape[1]
    for k in range(count):

        @pl.when(pl.program_id(0) // per == k)
        def _(k=k):
            outs[k][:, :width] = one.astype(jnp.bfloat16)
            outs[k][:, width:] = two.astype(jnp.bfloat16)


def run_weight_gradients(first, first_grad, second, second_grad, count):
    tokens, model = first[0].shape
    block_rows = model // count
    tile = min(256, block_rows)
    per = block_rows // tile
    width = first_grad[0].shape[1] + second_grad[0].shape[1]
    columns = pl.BlockSpec((tokens, tile), lambda i: (0, i))
    out_spec = lambda k: pl.BlockSpec(
        (tile, width), lambda i: (jnp.clip(i - per * k, 0, per - 1), 0)
    )
    return kernel_call(
        functools.partial(weight_gradients, count, per),
        (model // tile,),
        [columns] * 4 + [whole(a) for a in (*first_grad, *second_grad)],
        [out_spec(k) for k in range(count)],
        [shape_of((block_rows, width), jnp.bfloat16)] * count,
        4 * tokens * model * width,
        8 * tokens * model,
    )(*first, *second, *first_grad, *second_grad)


def transposed_product(parts, count, gain, *refs):
    lefts = refs[: 2 * parts]
    blocks = refs[2 * parts : 2 * parts + parts * count]
    rest = refs[2 * parts + parts * count :]
    normed, outs = (rest[:2], rest[2:]) if gain else ((), rest)
    tile = lefts[0].shape[0]
    rows = blocks[0].shape[0]
    if gain:

        @pl.when(pl.program_id(0) == 0)
        def _():
            outs[2][...] = jnp.zeros_like(outs[2])

    for k in range(count):
        total = None
        span = slice(k * rows, (k + 1) * rows)
        for p in range(parts):
            left = jnp.concatenate([lefts[2 * p][...], lefts[2 * p + 1][...]], axis=0)
            more = dot_nt(left, blocks[p * count + k][...])
            total = more if total is None else total + more
        if gain:
            here = total[:tile] * normed[0][:, span].astype(jnp.float32)
            here = here + total[tile:] * normed[1][:, span].astype(jnp.float32)
            outs[2][:, span] += jnp.sum(here, axis=0, keepdims=True)
        total = total.astype(jnp.bfloat16)
        outs[0][:, span] = total[:tile]
        outs[1][:, span] = total[tile:]


def run_transposed_product(pairs, blocks, column, columns, normed=()):
    count = len(blocks[0])
    tokens = pairs[0][0].shape[0]
    model = count * blocks[0][0].shape[0]
    tile = min(256, tokens)
    rows = lambda n: pl.BlockSpec((tile, n), lambda i: (i, 0))
    lefts = [a for pair in pairs for a in pair]
    flat = [b for one in blocks for b in one]
    gain = len(normed) > 0
    return kernel_call(
        functools.partial(transposed_product, len(pairs), count, gain),
        (tokens // tile,),
        [rows(a.shape[1]) for a in lefts]
        + [pl.BlockSpec((b.shape[0], columns), lambda i: (0, column)) for b in flat]
        + [rows(model) for _ in normed],
        [rows(model)] * 2 + [pl.BlockSpec((1, model), lambda i: (0, 0))] * gain,
        [shape_of((tokens, model), jnp.bfloat16)] * 2 + [shape_of((1, model), jnp.float32)] * gain,
        1 if gain else 4 * tokens * model * columns * len(pairs),
        1 if gain else 8 * tokens * model,
    )(*lefts, *flat, *normed)


def add_both(*refs):
    for left, right, out in zip(refs[0:2], refs[2:4], refs[4:6]):
        out[...] = (left[...].astype(jnp.float32) + right[...].astype(jnp.float32)).astype(
            jnp.bfloat16
        )


def run_add_both(blocks, got):
    rows, width = blocks[0].shape
    tile = min(128, rows)
    spec = pl.BlockSpec((tile, width), lambda i: (i, 0))
    return kernel_call(
        add_both,
        (rows // tile,),
        [spec] * 4,
        [spec] * 2,
        [shape_of((rows, width), jnp.bfloat16)] * 2,
        1,
        12 * rows * width,
    )(*blocks, *got)


def place_columns(subs, place_ref, *refs):
    ins, outs = refs[: group * subs], refs[group * subs :]
    place = place_ref[0]
    rows = ins[0].shape[0]
    width = ins[0].shape[1] // len(outs)
    for s in range(subs):
        for r, ref in enumerate(ins[group * s : group * (s + 1)]):
            start = ref.shape[0] - rows if r == group - 1 else 0
            column = pl.multiple_of((s * group + (place ^ r)) * width, width)
            for m, out in enumerate(outs):
                piece = ref[start : start + rows, m * width : (m + 1) * width]
                out[:, pl.ds(column, width)] = piece.astype(jnp.float32)


def run_place_columns(place, parts, count):
    rows, width = parts[0][0].shape
    flat = [a for part in parts for a in part]
    full = lambda a: pl.BlockSpec(a.shape, lambda i, place: (0, 0))
    shape = shape_of((rows, width // count * group * len(parts)), jnp.float32)
    return pl.pallas_call(
        functools.partial(place_columns, len(parts)),
        grid_spec=pltpu.PrefetchScalarGridSpec(
            num_scalar_prefetch=1,
            grid=(1,),
            in_specs=[full(a) for a in flat],
            out_specs=[full(shape)] * count,
        ),
        out_shape=[shape] * count,
        compiler_params=pltpu.CompilerParams(vmem_limit_bytes=vmem_limit),
    )(place.reshape(1).astype(jnp.int32), *flat)


def place_halves(place, mine, other, out):
    half = mine.shape[0]
    core = place[0]
    out[pl.ds(core * half, half), :] = mine[...]
    out[pl.ds((1 - core) * half, half), :] = other[...]


def run_place_halves(core, spot, count, mine, other):
    half, model = mine.shape
    block = model // count
    source = pl.BlockSpec((half, block), lambda k, place: (0, k))
    return pl.pallas_call(
        place_halves,
        grid_spec=pltpu.PrefetchScalarGridSpec(
            num_scalar_prefetch=1,
            grid=(count,),
            in_specs=[source, source],
            out_specs=pl.BlockSpec((2 * half, block), lambda k, place: (0, (k + place[1]) % count)),
        ),
        out_shape=shape_of((2 * half, model), jnp.float32),
        compiler_params=pltpu.CompilerParams(vmem_limit_bytes=vmem_limit),
        cost_estimate=pl.CostEstimate(flops=1, bytes_accessed=16 * half * model, transcendentals=0),
    )(jnp.stack([core, spot]).astype(jnp.int32), mine, other)


def swap_cores(values):
    return lax.ppermute(values, "tensor", [(0, 1), (1, 0)])


class Lines:
    def __init__(self, dp):
        self.dp = dp
        self.length = dp // group
        index = lax.axis_index("dp")
        self.place = index % group
        self.spot = index // group

    def flip(self, values, relation):
        return lax.ppermute(values, "dp", [(i, i ^ relation) for i in range(self.dp)])

    def hop(self, values, first, last, step):
        pairs = [
            (spot * group + place, (spot + step) * group + place)
            for spot in range(first, last + 1)
            for place in range(group)
        ]
        return lax.ppermute(values, "dp", pairs)

    def turn(self, values, step):
        pairs = [
            (spot * group + place, ((spot + step) % self.length) * group + place)
            for spot in range(self.length)
            for place in range(group)
        ]
        return lax.ppermute(values, "dp", pairs)

    def by_place(self, related):
        odd = self.place % 2 == 1
        high = self.place // 2 == 1
        own, one, two, three = related
        pairs = (
            (jnp.where(odd, one, own), jnp.where(odd, own, one)),
            (jnp.where(odd, three, two), jnp.where(odd, two, three)),
        )
        return [
            jnp.where(high, pairs[1][0], pairs[0][0]),
            jnp.where(high, pairs[1][1], pairs[0][1]),
            jnp.where(high, pairs[0][0], pairs[1][0]),
            jnp.where(high, pairs[0][1], pairs[1][1]),
        ]

    def pieces(self, piece_of):
        return [piece_of(self.place ^ relation) for relation in range(group)]

    def flip_pieces(self, pieces):
        return [pieces[0]] + [self.flip(pieces[r], r) for r in range(1, group)]

    def flip_first(self, pieces):
        return self.flip(jnp.concatenate([pieces[1], pieces[3]]), 1)

    def flip_second(self, pieces, got):
        return self.flip(jnp.concatenate([pieces[2], got[got.shape[0] // 2 :]]), 2)

    def flipped(self, pieces, first, second):
        rows = pieces[0].shape[0]
        return [pieces[0], first[:rows], second[:rows], second[rows:]]

    def row_pieces(self, total):
        rows = total.shape[0] // group
        return [
            lax.dynamic_slice_in_dim(total, (self.place ^ r) * rows, rows) for r in range(group)
        ]

    def gather_near(self, mine):
        return [self.flip(mine, 1), self.flip(mine, 2)]

    def gather_across(self, near):
        middle = near[0].shape[0] // 2
        return [self.flip(near[0][:middle], 2), self.flip(near[1][middle:], 1)]

    def scatter_across(self, across):
        middle = across.shape[0] // 2
        return [self.flip(across[:middle], 1), self.flip(across[middle:], 2)]

    def gather_far(self, mine):
        near = self.gather_near(mine)
        return near, self.gather_across(near)

    def gather_tokens(self, mine):
        return self.both_cores(mine, *self.gather_far(mine))

    def both_cores(self, mine, near, across):
        kept = jnp.concatenate([mine] + near + across)
        return kept, swap_cores(kept)

    def terms(self, kept, other, relation):
        rows = kept.shape[0] // group
        span = slice(relation * rows, (relation + 1) * rows)
        return kept[span].astype(jnp.float32) + other[span].astype(jnp.float32)

    def across_terms(self, kept, other):
        return self.scatter_across(self.terms(kept, other, 3).astype(jnp.bfloat16))

    def near_sends(self, kept, other, got):
        one, two = self.terms(kept, other, 1), self.terms(kept, other, 2)
        middle = one.shape[0] // 2
        one = jnp.concatenate([one[:middle], one[middle:] + got[1].astype(jnp.float32)])
        two = jnp.concatenate([two[:middle] + got[0].astype(jnp.float32), two[middle:]])
        return [one.astype(jnp.bfloat16), two.astype(jnp.bfloat16)]

    def near_flips(self, kept, other, got):
        one, two = self.near_sends(kept, other, got)
        return [self.flip(one, 1), self.flip(two, 2)]

    def near_sum(self, kept, other, near):
        one, two = near
        return self.terms(kept, other, 0) + one.astype(jnp.float32) + two.astype(jnp.float32)

    def near_terms(self, kept, other, got):
        return self.near_sum(kept, other, self.near_flips(kept, other, got))

    def scatter_tokens(self, kept, other):
        return self.near_terms(kept, other, self.across_terms(kept, other))


class LineGather:
    def __init__(self, lines, block):
        self.lines, self.block, self.got = lines, block, []

    def hop(self):
        lines, step = self.lines, len(self.got) + 1
        if lines.length != 4:
            turns = range(1, lines.length) if step == 1 else ()
            self.got.append([lines.turn(self.block, -k) for k in turns])
            return
        up, down = self.got[-1] if self.got else (self.block, self.block)
        self.got.append(
            [
                lines.hop(up, step - 1, lines.length - 2, 1),
                lines.hop(down, 1, lines.length - step, -1),
            ]
        )

    def blocks(self):
        lines = self.lines
        if lines.length != 4:
            return [self.block] + self.got[0]
        return [self.block] + [
            jnp.where(
                lines.spot + k < lines.length,
                self.got[k - 1][1],
                self.got[lines.length - k - 1][0],
            )
            for k in range(1, lines.length)
        ]


class LineScatter:
    def __init__(self, lines, blocks):
        self.lines, self.blocks, self.got = lines, blocks, []

    def ready(self):
        step = len(self.got) + 1
        if self.lines.length != 4:
            return []
        blocks = [self.blocks[self.lines.length - step], self.blocks[step]]
        return run_add_both(blocks, self.got[-1]) if self.got else blocks

    def hop(self, ready=None):
        lines, step = self.lines, len(self.got) + 1
        if lines.length != 4:
            turns = range(1, lines.length) if step == 1 else ()
            self.got.append([lines.turn(self.blocks[k], k) for k in turns])
            return
        up, down = self.ready() if ready is None else ready
        self.got.append(
            [
                lines.hop(up, 0, min(step - 1, lines.length - 2), 1),
                lines.hop(down, max(lines.length - step, 1), lines.length - 1, -1),
            ]
        )

    def total(self):
        last = self.got[-1] if self.lines.length == 4 else self.got[0]
        result = self.blocks[0].astype(jnp.float32)
        for one in last:
            result = result + one.astype(jnp.float32)
        return result.astype(jnp.bfloat16)


def tie(*values):
    return lax.optimization_barrier(values)


def local(
    dp,
    tokens,
    segments,
    cotangent,
    attn_gain,
    ffn_gain,
    query_gain,
    key_gain,
    w_query,
    key_weight,
    value_weight,
    w_out,
    w_gate,
    w_up,
    w_down,
):
    lines = Lines(dp)
    core = lax.axis_index("tensor")
    length, width = tokens.shape
    half = length // 2
    head_dim = query_gain.shape[0]
    rows = w_query.shape[0]
    block_rows = rows * group
    query_width = w_query.shape[1] // group
    key_width = key_weight.shape[1] // group
    attn_width = query_width + 2 * key_width
    ff_sub = w_gate.shape[1] // group // sub_count

    def around(values):
        return jnp.roll(values, -lines.spot * block_rows, axis=-1)

    def back_around(values):
        return jnp.roll(values, lines.spot * block_rows, axis=-1)

    attn_gain_r, ffn_gain_r = around(attn_gain), around(ffn_gain)

    def columns(weight, start, size):
        return lax.dynamic_slice_in_dim(weight, start, size, axis=1)

    attn_pieces = lines.pieces(
        lambda j: jnp.concatenate(
            [
                columns(w_query, j * query_width, query_width),
                columns(key_weight, j * key_width, key_width),
                columns(value_weight, j * key_width, key_width),
                columns(w_out, j * query_width, query_width),
            ],
            axis=1,
        )
    )
    attn_shared = lines.flip_pieces(attn_pieces)
    source = around(lax.dynamic_slice_in_dim(tokens, core * half, half)).astype(jnp.float32)
    normed_f, scale_first = norm_rows(source, attn_gain_r)
    normed_mine = normed_f.astype(jnp.bfloat16)

    seg_near = jnp.concatenate([segments, lines.flip(segments, 1)])
    seg_second = lines.flip(seg_near, 2)
    attn_shared, normed_mine, seg_near, seg_second = tie(
        attn_shared, normed_mine, seg_near, seg_second
    )

    def ffn_piece(s):
        return lines.pieces(
            lambda j: jnp.concatenate(
                [
                    columns(weight, s * group * ff_sub + j * ff_sub, ff_sub)
                    for weight in (w_gate, w_up, w_down)
                ],
                axis=1,
            )
        )


    seg_all = jnp.concatenate([seg_near, seg_second])
    positions = jax.vmap(positions_of)(seg_all)
    index = jnp.arange(length, dtype=jnp.int32)
    cosine, sine = angles(positions, head_dim, 2 * head_dim)
    swapped = jnp.full((1, 1), core, jnp.int32)
    starts = index[None] - positions
    tables = (swapped, cosine, sine, starts[..., None], starts[:, None, :], index)
    gains_two = jnp.stack(
        [
            jnp.tile(query_gain, query_width // head_dim),
            jnp.tile(key_gain, query_width // head_dim),
        ]
    )

    attn_line = LineGather(lines, jnp.concatenate(lines.by_place(attn_shared), axis=0))
    attn_line.hop()
    near = lines.gather_near(normed_mine)
    mine_other = swap_cores(normed_mine)
    near, attn_line.got[0], tables, mine_other, w_gate, w_up, w_down = tie(
        near, attn_line.got[0], tables, mine_other, w_gate, w_up, w_down
    )
    attn_line.hop()
    across = lines.gather_across(near)
    pieces_0 = ffn_piece(0)
    near_other = swap_cores(near[0])
    near_other, near_two = tie(near_other, near[1])
    near = [near[0], near_two]
    near_other = [near_other, swap_cores(near_two)]
    across, attn_line.got[1], pieces_0, near_other, w_gate, w_up, w_down, cotangent = tie(
        across, attn_line.got[1], pieces_0, near_other, w_gate, w_up, w_down, cotangent
    )
    attn_line.hop()
    pieces_1 = ffn_piece(1)
    cot_half = around(lax.dynamic_slice_in_dim(cotangent, core * half, half))
    out_mine = cot_half.astype(jnp.bfloat16)
    across = jnp.concatenate(across)
    normed = (
        jnp.concatenate([normed_mine] + near + [across]),
        jnp.concatenate([mine_other] + near_other + [swap_cores(across)]),
    )
    shared_0 = lines.flip_pieces(pieces_0)
    normed, attn_line.got[2], shared_0, pieces_1, out_mine = tie(
        normed, attn_line.got[2], shared_0, pieces_1, out_mine
    )
    attn_w = attn_line.blocks()

    line_0 = LineGather(lines, jnp.concatenate(lines.by_place(shared_0), axis=0))
    line_0.hop()
    out_near = lines.gather_near(out_mine)
    qkv_raw, heads_out, attended_kept, attended_other = run_attention(
        True, normed, attn_w, tables, gains_two, head_dim, query_width, attn_width
    )
    attended_other, line_0.got[0], out_near, pieces_1 = tie(
        attended_other, line_0.got[0], out_near, pieces_1
    )

    line_0.hop()
    attended_other = swap_cores(attended_other)
    middle = half // 2
    out_first = lines.flip(out_near[0][:middle], 2)
    attended_other, out_first = tie(attended_other, out_first)
    first_1 = lines.flip_first(pieces_1)
    got = lines.across_terms(attended_kept, attended_other)
    got, first_1, line_0.got[1] = tie(got, first_1, line_0.got[1])
    line_0.hop()
    second_1 = lines.flip_second(pieces_1, first_1)
    attended = lines.near_terms(attended_kept, attended_other, got)
    attended, out_near = tie(attended, out_near)
    out_second = lines.flip(out_near[1][middle:], 1)
    attended, line_0.got[2], out_first, out_second, second_1 = tie(
        attended, line_0.got[2], out_first, out_second, second_1
    )
    shared_1 = lines.flipped(pieces_1, first_1, second_1)
    block_1 = jnp.concatenate(lines.by_place(shared_1), axis=0)

    line_1 = LineGather(lines, block_1)
    out_b = lines.both_cores(out_mine, out_near, [out_first, out_second])
    line_1.hop()
    state = source + attended
    normed2_f, scale_second = norm_rows(state, ffn_gain_r)
    near, across = lines.gather_far(normed2_f.astype(jnp.bfloat16))
    ffn_w = [line_0.blocks()]
    near, across, line_1.got[0], out_b, ffn_w[0] = tie(
        near, across, line_1.got[0], out_b, ffn_w[0]
    )

    line_1.hop()
    normed2 = lines.both_cores(normed2_f.astype(jnp.bfloat16), near, across)
    units_0 = run_ffn_units(normed2, out_b, ffn_w[0], ff_sub)
    units_0, line_1.got[1] = tie(units_0, line_1.got[1])
    line_1.hop()
    ffn_g = run_weight_gradients(normed2, units_0[2:], out_b, units_0[:2], lines.length)
    ffn_g, line_1.got[2], units_0 = tie(ffn_g, line_1.got[2], units_0)
    sum_0 = LineScatter(lines, ffn_g)
    ffn_w.append(line_1.blocks())

    sum_0.hop()
    units_1 = run_ffn_units(normed2, out_b, ffn_w[1], ff_sub)
    kept, other = run_transposed_product([units_0[2:], units_1[2:]], ffn_w, 0, 2 * ff_sub)
    kept, other, sum_0.got[0], units_1 = tie(kept, other, sum_0.got[0], units_1)

    sum_0.hop()
    other = swap_cores(other)
    got = lines.across_terms(kept, other)
    branch_kept, branch_other = run_transposed_product(
        [units_0[:2], units_1[:2]], ffn_w, 2, ff_sub
    )
    branch_other = swap_cores(branch_other)
    got, sum_0.got[1], units_1, branch_kept, branch_other = tie(
        got, sum_0.got[1], units_1, branch_kept, branch_other
    )
    sum_0.hop()
    near = lines.near_flips(kept, other, got)
    sum_1 = LineScatter(
        lines, run_weight_gradients(normed2, units_1[2:], out_b, units_1[:2], lines.length)
    )
    near, branch_kept, branch_other = tie(near, branch_kept, branch_other)
    normed2_grad = lines.near_sum(kept, other, near)
    branch_got = lines.across_terms(branch_kept, branch_other)
    normed2_grad, sum_0.got[2], branch_got, sum_1.blocks = tie(
        normed2_grad, sum_0.got[2], branch_got, sum_1.blocks
    )

    sum_1.hop()
    ffn_gain_part = jnp.sum(normed2_grad * state * scale_second, axis=0)
    state_grad = cot_half + norm_back(state, scale_second, ffn_gain_r, normed2_grad)
    grad_mine = state_grad.astype(jnp.bfloat16)
    near, across = lines.gather_far(grad_mine)
    back_0 = lines.row_pieces(sum_0.total())
    branch_terms = lines.near_sends(branch_kept, branch_other, branch_got)
    near, across, sum_1.got[0], back_0, branch_terms = tie(
        near, across, sum_1.got[0], back_0, branch_terms
    )

    sum_1.hop()
    attended_b = lines.both_cores(grad_mine, near, across)

    branch = [lines.flip(branch_terms[0], 1), lines.flip(branch_terms[1], 2)]
    back_0_first = lines.flip_first(back_0)
    qkv_grad, gain_parts = run_attention(
        False, attended_b, attn_w, tables, gains_two, head_dim, query_width, attn_width, qkv_raw
    )
    kept, other, attn_gain_part = run_transposed_product(
        [qkv_grad], [attn_w], 0, attn_width, normed
    )
    kept, other, qkv_grad, branch, sum_1.got[1], back_0, back_0_first = tie(
        kept, other, qkv_grad, branch, sum_1.got[1], back_0, back_0_first
    )

    sum_1.hop()
    gains = jnp.concatenate(
        [
            back_around(attn_gain_part[0] / attn_gain_r),
            back_around(ffn_gain_part),
            jnp.sum(gain_parts[0].reshape(-1, head_dim), axis=0),
            gain_parts[1][:head_dim],
        ]
    )
    other = swap_cores(other)
    back_0_second = lines.flip_second(back_0, back_0_first)
    got = lines.across_terms(kept, other)
    attn_sum = LineScatter(
        lines, run_weight_gradients(normed, qkv_grad, attended_b, heads_out, lines.length)
    )
    got, sum_1.got[2], attn_sum.blocks, back_0_second, gains = tie(
        got, sum_1.got[2], attn_sum.blocks, back_0_second, gains
    )
    attn_sum.hop()
    back_1 = lines.row_pieces(sum_1.total())
    near = lines.near_flips(kept, other, got)
    attn_sum.hop()
    near, attn_sum.got[1], back_1 = tie(near, attn_sum.got[1], back_1)
    attn_sum.hop()
    back_1 = lines.flip_pieces(back_1)
    attn_sum.got[2], back_1, near, gains = tie(attn_sum.got[2], back_1, near, gains)
    attn_grads = lines.flip_pieces(lines.row_pieces(attn_sum.total()))
    normed_grad = lines.near_sum(kept, other, near)
    input_grad = state_grad + norm_back(source, scale_first, attn_gain_r, normed_grad)
    input_other = swap_cores(input_grad)
    bit = 1
    while bit < dp:
        gains = gains + lines.flip(gains, bit)
        bit *= 2
    gains = gains + swap_cores(gains)
    ffn_grads = run_place_columns(
        lines.place,
        [
            (back_0[0], back_0_first, back_0_second, back_0_second),
            back_1,
        ],
        3,
    )
    mixed = state + lines.near_sum(branch_kept, branch_other, branch)

    def whole_rows(mine, other):
        return run_place_halves(core, lines.spot, lines.length, mine, other)

    def columns_of(related, start, stop):
        blocks = lines.by_place([b[:, start:stop] for b in related])
        return jnp.concatenate(blocks, axis=1).astype(jnp.float32)

    return (
        whole_rows(mixed, swap_cores(mixed)),
        whole_rows(input_grad, input_other),
        gains[:width],
        gains[width : 2 * width],
        gains[2 * width : 2 * width + head_dim],
        gains[2 * width + head_dim :],
        columns_of(attn_grads, 0, query_width),
        columns_of(attn_grads, query_width, query_width + key_width),
        columns_of(attn_grads, query_width + key_width, attn_width),
        columns_of(attn_grads, attn_width, attn_width + query_width),
        *ffn_grads,
    )


def solution(mesh):
    dp = mesh.shape["dp"]
    weight = P("dp", "tensor")
    rows = P("dp", None)
    return jax.shard_map(
        lambda *arrays: local(dp, *arrays),
        mesh=mesh,
        in_specs=(rows, rows, rows, P(), P(), P(), P()) + (weight,) * 7,
        out_specs=(rows, rows, P(), P(), P(), P()) + (weight,) * 7,
        check_vma=False,
    )
```

```python
import functools

import jax
import jax.numpy as jnp
from jax import lax
from jax.experimental import pallas as pl
from jax.experimental.pallas import tpu as pltpu
from jax.sharding import PartitionSpec as P

eps = 1e-05
rope_base = 1000000.0
group = 4
sub_count = 2
vmem_limit = 52 * 1024 * 1024


def norm_rows(values, gain):
    scale = lax.rsqrt(jnp.mean(values * values, axis=-1, keepdims=True) + eps)
    return (values * scale * gain, scale)


def norm_back(values, scale, gain, incoming):
    weighted = incoming * gain
    return scale * weighted - values * (scale * scale * scale) * jnp.mean(
        weighted * values, axis=-1, keepdims=True
    )


def positions_of(segment_row):
    row_index = jnp.arange(segment_row.shape[0], dtype=jnp.int32)
    earlier = jnp.concatenate([segment_row[:1] - 1, segment_row[:-1]])
    starts = jnp.where(segment_row != earlier, row_index, jnp.zeros_like(row_index))
    return row_index - lax.cummax(starts, axis=0)


def angles(positions, width, lanes):
    frequency = rope_base ** (-jnp.arange(0, width, 2, dtype=jnp.float32) / width)
    frequency = jnp.tile(frequency, 2 * lanes // width)
    phases = positions.astype(jnp.float32)[..., None] * frequency
    return (jnp.cos(phases), jnp.sin(phases))


def dot_nn(left, right):
    return jnp.dot(left, right, preferred_element_type=jnp.float32)


def dot_nt(left, right):
    return lax.dot_general(
        left, right, (((1,), (1,)), ((), ())), preferred_element_type=jnp.float32
    )


def dot_tn(left, right):
    return lax.dot_general(
        left, right, (((0,), (0,)), ((), ())), preferred_element_type=jnp.float32
    )


def pick_dot(left, right):
    high = left.astype(jnp.bfloat16)
    low = (left - high.astype(jnp.float32)).astype(jnp.bfloat16)
    return dot_nn(high, right) + dot_nn(low, right)


def kernel_call(body, grid, in_specs, out_specs, out_shape, flops, moved):
    return pl.pallas_call(
        body,
        grid=grid,
        in_specs=in_specs,
        out_specs=out_specs,
        out_shape=out_shape,
        compiler_params=pltpu.CompilerParams(vmem_limit_bytes=vmem_limit),
        cost_estimate=pl.CostEstimate(flops=flops, bytes_accessed=moved, transcendentals=0),
    )


def whole(array):
    rank = len(array.shape)
    return pl.BlockSpec(array.shape, lambda *_: (0,) * rank)


def shape_of(shape, kind):
    return jax.ShapeDtypeStruct(shape, kind)


def turn_heads(values, head_dim):
    lanes = values.shape[-1]
    middle = head_dim // 2
    lane = lax.broadcasted_iota(jnp.int32, values.shape, 1) % head_dim
    ahead = pltpu.roll(values, lanes - middle, 1)
    behind = pltpu.roll(values, middle, 1)
    return jnp.where(lane < middle, -ahead, behind)


def index_pair(rows, columns):
    return (
        lax.broadcasted_iota(jnp.int32, (rows, columns), 0),
        lax.broadcasted_iota(jnp.int32, (rows, columns), 1),
    )


def ones_where(condition):
    return condition.astype(jnp.float32).astype(jnp.bfloat16)


def spread_of(rows, offset, columns, head_dim):
    row, column = index_pair(rows, columns)
    return ones_where(row - offset == column % head_dim)


def fold(values, head_dim):
    row, column = index_pair(values.shape[1], values.shape[1])
    return pick_dot(values, ones_where(row % head_dim == column % head_dim))


def head_mean(values, head_dim):
    row, column = index_pair(values.shape[1], values.shape[1])
    return pick_dot(values, ones_where(row // head_dim == column // head_dim)) * (1.0 / head_dim)


def prepare_heads(raw, gain, cosine, sine, head_dim):
    scale = lax.rsqrt(head_mean(raw * raw, head_dim) + eps)
    scaled = raw * scale * gain
    return scaled * cosine + turn_heads(scaled, head_dim) * sine, scale


def prepare_back(raw, scale, gain, cosine, sine, incoming, head_dim):
    turned = incoming * cosine - turn_heads(incoming * sine, head_dim)
    weighted = turned * gain
    grad = scale * weighted - raw * (scale * scale * scale) * head_mean(weighted * raw, head_dim)
    return grad, jnp.sum(turned * raw * scale, axis=0, keepdims=True)


def head_inputs(raw, gains, cosine, sine, head_dim, width):
    query, query_scale = prepare_heads(raw[:, :width], gains[0:1], cosine, sine, head_dim)
    rest = raw[:, width:]
    key_raw = pick_dot(rest, spread_of(rest.shape[1], 0, width, head_dim))
    key, key_scale = prepare_heads(key_raw, gains[1:2], cosine, sine, head_dim)
    value = dot_nn(
        rest.astype(jnp.bfloat16), spread_of(rest.shape[1], head_dim, width, head_dim)
    ).astype(jnp.bfloat16)
    return (
        query.astype(jnp.bfloat16) * jnp.bfloat16(0.125),
        query_scale,
        key_raw,
        key.astype(jnp.bfloat16),
        key_scale,
        value,
    )


def only_head(values, head, head_dim):
    lane = lax.broadcasted_iota(jnp.int32, values.shape, 1)
    return jnp.where(lane // head_dim == head, values, jnp.zeros_like(values))


def exps_of(scores, allowed):
    return jnp.exp(jnp.where(allowed, scores, -1000000000.0))


def block_product(kept, other, blocks, start, stop):
    rows = blocks[0].shape[0]
    total = None
    for k, block in enumerate(blocks):
        left = jnp.concatenate(
            [kept[:, k * rows : (k + 1) * rows], other[:, k * rows : (k + 1) * rows]], axis=0
        )
        more = dot_nn(left, block[:, start:stop])
        total = more if total is None else total + more
    return total


def by_halves(swapped, one, two):
    return jnp.where(swapped, two, one), jnp.where(swapped, one, two)


def head_tables(cosine_ref, sine_ref, width):
    repeat = width // cosine_ref.shape[-1]
    return (
        jnp.concatenate([cosine_ref[0]] * repeat, axis=1),
        jnp.concatenate([sine_ref[0]] * repeat, axis=1),
    )


def attention_forward(count, head_dim, width, *refs):
    kept, other = refs[:2]
    refs = refs[2:]
    swap_ref, cosine_ref, sine_ref, start_ref, index_column, index_row, gains = refs[:7]
    blocks = refs[7 : 7 + count]
    raw_ref, heads_kept, heads_other, part_kept, part_other = refs[7 + count :]
    half = kept.shape[0]
    attn_width = raw_ref.shape[-1]
    raw = block_product(kept, other, blocks, 0, attn_width)
    swapped = swap_ref[...] == 1
    raw = jnp.concatenate(by_halves(swapped, raw[:half], raw[half:]), axis=0)
    raw_ref[0] = raw
    cosine, sine = head_tables(cosine_ref, sine_ref, width)
    query, _, _, key, _, value = head_inputs(raw, gains[...], cosine, sine, head_dim, width)
    allowed = (index_row[...] <= index_column[...]) & (index_row[...] >= start_ref[0])
    one = jnp.zeros((half, width), jnp.float32)
    two = one
    for head in range(width // head_dim):
        query_h = only_head(query, head, head_dim)
        for first in (True, False):
            span, keys = (slice(0, half), half) if first else (slice(half, 2 * half), 2 * half)
            exps = exps_of(dot_nt(query_h[span], key[:keys]), allowed[span, :keys])
            part = dot_nn(exps.astype(jnp.bfloat16), value[:keys])
            part = part * (1.0 / jnp.sum(exps, axis=-1, keepdims=True))
            part = only_head(part, head, head_dim)
            if first:
                one = one + part
            else:
                two = two + part
    heads = by_halves(swapped, one.astype(jnp.bfloat16), two.astype(jnp.bfloat16))
    heads_kept[...] = heads[0]
    heads_other[...] = heads[1]
    heads = jnp.concatenate(heads, axis=0)
    rows = blocks[0].shape[0]
    for k, block in enumerate(blocks):
        out = dot_nt(heads, block[:, attn_width : attn_width + width]).astype(jnp.bfloat16)
        part_kept[:, k * rows : (k + 1) * rows] = out[:half]
        part_other[:, k * rows : (k + 1) * rows] = out[half:]


def attention_backward(count, head_dim, width, *refs):
    kept, other, raw_ref, normed_kept, normed_other = refs[:5]
    refs = refs[5:]
    swap_ref, cosine_ref, sine_ref, start_ref, index_column, index_row, gains = refs[:7]
    blocks = refs[7 : 7 + count]
    grad_kept, grad_other, gain_ref, part_kept, part_other, scaled_ref = refs[7 + count :]
    half = kept.shape[0]
    attn_width = raw_ref.shape[-1]
    grads = block_product(kept, other, blocks, attn_width, attn_width + width)
    grads = grads.astype(jnp.bfloat16)
    swapped = swap_ref[...] == 1
    grads = jnp.concatenate(by_halves(swapped, grads[:half], grads[half:]), axis=0)
    raw = raw_ref[0]
    cosine, sine = head_tables(cosine_ref, sine_ref, width)
    query, query_scale, key_raw, key, key_scale, value = head_inputs(
        raw, gains[...], cosine, sine, head_dim, width
    )
    allowed = (index_column[...] <= index_row[...]) & (index_column[...] >= start_ref[0])
    zero = jnp.zeros((half, width), jnp.float32)
    query_grads, key_grads, value_grads = [zero, zero], [zero, zero], [zero, zero]
    for head in range(width // head_dim):
        query_h = only_head(query, head, head_dim)
        grad_h = only_head(grads, head, head_dim)
        for part in range(2):
            span, keys = slice(part * half, (part + 1) * half), (part + 1) * half
            exps = exps_of(dot_nt(key[:keys], query_h[span]), allowed[:keys, span])
            probs_f = exps * (1.0 / jnp.sum(exps, axis=0, keepdims=True))
            weighted = probs_f * dot_nt(value[:keys], grad_h[span])
            score_grad = weighted - probs_f * jnp.sum(weighted, axis=0, keepdims=True)
            score_grad = score_grad.astype(jnp.bfloat16)
            query_grads[part] += only_head(dot_tn(score_grad, key[:keys]), head, head_dim)
            value_part = dot_nn(probs_f.astype(jnp.bfloat16), grad_h[span])
            key_part = dot_nn(score_grad, query_h[span])
            for block in range(part + 1):
                rows = slice(block * half, (block + 1) * half)
                value_grads[block] += value_part[rows]
                key_grads[block] += key_part[rows]
    query_grad = 0.125 * jnp.concatenate(query_grads, axis=0)
    key_grad = fold(jnp.concatenate(key_grads, axis=0), head_dim)
    value_grad = fold(jnp.concatenate(value_grads, axis=0), head_dim)
    query_grad, query_gain_part = prepare_back(
        raw[:, :width], query_scale, gains[0:1], cosine, sine, query_grad, head_dim
    )
    key_grad, key_gain_part = prepare_back(
        key_raw, key_scale, gains[1:2], cosine, sine, key_grad, head_dim
    )
    rest = attn_width - width
    lane = lax.broadcasted_iota(jnp.int32, (2 * half, rest), 1)
    rest_grad = jnp.where(lane < head_dim, key_grad[:, :rest], value_grad[:, :rest])
    query_grad = query_grad.astype(jnp.bfloat16)
    rest_grad = rest_grad.astype(jnp.bfloat16)
    query_sides = by_halves(swapped, query_grad[:half], query_grad[half:])
    rest_sides = by_halves(swapped, rest_grad[:half], rest_grad[half:])
    all_sides = []
    for side, out in enumerate((grad_kept, grad_other)):
        both = jnp.concatenate([query_sides[side], rest_sides[side]], axis=1)
        out[...] = both
        all_sides.append(both)
    all_sides = jnp.concatenate(all_sides, axis=0)
    parts = jnp.concatenate([query_gain_part, key_gain_part], axis=0)

    @pl.when(pl.program_id(0) == 0)
    def _():
        scaled_ref[...] = jnp.zeros_like(scaled_ref)

    rows = blocks[0].shape[0]
    for k, block in enumerate(blocks):
        span = slice(k * rows, (k + 1) * rows)
        out = dot_nt(all_sides, block[:, :attn_width])
        scaled = out[:half] * normed_kept[:, span].astype(jnp.float32)
        scaled = scaled + out[half:] * normed_other[:, span].astype(jnp.float32)
        scaled_ref[:, span] += jnp.sum(scaled, axis=0, keepdims=True)
        out = out.astype(jnp.bfloat16)
        part_kept[:, span] = out[:half]
        part_other[:, span] = out[half:]

    @pl.when(pl.program_id(0) == 0)
    def _():
        gain_ref[...] = parts

    @pl.when(pl.program_id(0) != 0)
    def _():
        gain_ref[...] = gain_ref[...] + parts


def run_attention(forward, pair, blocks, tables, gains, head_dim, width, attn_width, raw=None, normed=None):
    half = pair[0].shape[0] // group
    model = pair[0].shape[1]
    swapped, cosine, sine, start_columns, start_rows, index = tables
    starts = start_columns if forward else start_rows
    rows = lambda n: pl.BlockSpec((half, n), lambda s: (s, 0))
    per_sequence = lambda shape: pl.BlockSpec((1,) + shape[1:], lambda s: (s, 0, 0))
    column, row = index[:, None], index[None, :]
    common = [swapped, cosine, sine, starts, column, row, gains]
    common_specs = [whole(swapped)] + [per_sequence(a.shape) for a in (cosine, sine, starts)]
    common_specs += [whole(column), whole(row), whole(gains)]
    common += blocks
    common_specs += [whole(b) for b in blocks]
    raw_shape = (group, 2 * half, attn_width)
    flops = 2 * 2 * group * half * model * attn_width * 10
    moved = 16 * group * half * model
    side = lambda n: shape_of((group * half, n), jnp.bfloat16)
    if forward:
        results = kernel_call(
            functools.partial(attention_forward, len(blocks), head_dim, width),
            (group,),
            [rows(model)] * 2 + common_specs,
            [per_sequence(raw_shape), rows(width), rows(width), rows(model), rows(model)],
            [shape_of(raw_shape, jnp.float32), side(width), side(width), side(model), side(model)],
            flops,
            moved,
        )(*pair, *common)
        return results[0], tuple(results[1:3]), results[3], results[4]
    results = kernel_call(
        functools.partial(attention_backward, len(blocks), head_dim, width),
        (group,),
        [rows(model)] * 2 + [per_sequence(raw_shape)] + [rows(model)] * 2 + common_specs,
        [rows(attn_width), rows(attn_width), pl.BlockSpec((2, width), lambda s: (0, 0))]
        + [rows(model)] * 2
        + [pl.BlockSpec((1, model), lambda s: (0, 0))],
        [side(attn_width), side(attn_width), shape_of((2, width), jnp.float32)]
        + [side(model)] * 2
        + [shape_of((1, model), jnp.float32)],
        flops,
        moved,
    )(*pair, raw, *normed, *common)
    return tuple(results[:2]), *results[2:]


def ffn_units(count, ff_sub, earlier, *refs):
    normed, out = refs[0:2], refs[2:4]
    blocks, refs = refs[4 : 4 + count], refs[4 + count :]
    if earlier:
        before, before_blocks, refs = refs[0:2], refs[2 : 2 + count], refs[2 + count :]
    inner_refs, grad_refs, terms = refs[0:2], refs[2:4], refs[4:6]
    tile = normed[0].shape[0]
    gate_up = block_product(normed[0], normed[1], blocks, 0, 2 * ff_sub)
    inner_grad = block_product(out[0], out[1], blocks, 2 * ff_sub, 3 * ff_sub)
    gate, up = gate_up[:, :ff_sub], gate_up[:, ff_sub:]
    sigmoid = 1.0 / (1.0 + jnp.exp(-gate))
    silu = gate * sigmoid
    inner = (silu * up).astype(jnp.bfloat16)
    gate_grad = (inner_grad * up * sigmoid * (1.0 + gate * (1.0 - sigmoid))).astype(jnp.bfloat16)
    up_grad = (inner_grad * silu).astype(jnp.bfloat16)
    for side in range(2):
        rows = slice(side * tile, (side + 1) * tile)
        inner_refs[side][...] = inner[rows]
        grad_refs[side][:, :ff_sub] = gate_grad[rows]
        grad_refs[side][:, ff_sub:] = up_grad[rows]
    if not earlier:
        return
    here = jnp.concatenate([gate_grad, up_grad], axis=1)
    there = jnp.concatenate([before[0][...], before[1][...]], axis=0)
    rows = blocks[0].shape[0]
    for k in range(count):
        span = slice(k * rows, (k + 1) * rows)
        total = dot_nt(here, blocks[k][:, : 2 * ff_sub]) + dot_nt(there, before_blocks[k][...])
        total = total.astype(jnp.bfloat16)
        terms[0][:, span] = total[:tile]
        terms[1][:, span] = total[tile:]


def run_ffn_units(normed, out, blocks, ff_sub, before=None, before_blocks=()):
    tokens, model = normed[0].shape
    tile = min(256, tokens)
    rows = lambda n: pl.BlockSpec((tile, n), lambda i: (i, 0))
    earlier = before is not None
    shapes = [ff_sub] * 2 + [2 * ff_sub] * 2 + [model] * 2 * earlier
    return kernel_call(
        functools.partial(ffn_units, len(blocks), ff_sub, earlier),
        (tokens // tile,),
        [rows(model)] * 4
        + [whole(b) for b in blocks]
        + [rows(2 * ff_sub)] * 2 * earlier
        + [pl.BlockSpec((b.shape[0], 2 * ff_sub), lambda i: (0, 0)) for b in before_blocks],
        [rows(n) for n in shapes],
        [shape_of((tokens, n), jnp.bfloat16) for n in shapes],
        12 * tokens * model * ff_sub,
        8 * tokens * model,
    )(*normed, *out, *blocks, *(before if earlier else ()), *before_blocks)


def weight_gradients(count, per, *refs):
    first, second = refs[0:2], refs[2:4]
    first_grad, second_grad = refs[4:6], refs[6:8]
    outs = refs[8:]
    one = dot_tn(first[0][...], first_grad[0][...]) + dot_tn(first[1][...], first_grad[1][...])
    two = dot_tn(second[0][...], second_grad[0][...]) + dot_tn(second[1][...], second_grad[1][...])
    width = one.shape[1]
    for k in range(count):

        @pl.when(pl.program_id(0) // per == k)
        def _(k=k):
            outs[k][:, :width] = one.astype(jnp.bfloat16)
            outs[k][:, width:] = two.astype(jnp.bfloat16)


def run_weight_gradients(first, first_grad, second, second_grad, count):
    tokens, model = first[0].shape
    block_rows = model // count
    tile = min(256, block_rows)
    per = block_rows // tile
    width = first_grad[0].shape[1] + second_grad[0].shape[1]
    columns = pl.BlockSpec((tokens, tile), lambda i: (0, i))
    out_spec = lambda k: pl.BlockSpec(
        (tile, width), lambda i: (jnp.clip(i - per * k, 0, per - 1), 0)
    )
    return kernel_call(
        functools.partial(weight_gradients, count, per),
        (model // tile,),
        [columns] * 4 + [whole(a) for a in (*first_grad, *second_grad)],
        [out_spec(k) for k in range(count)],
        [shape_of((block_rows, width), jnp.bfloat16)] * count,
        2 * tokens * model * 256,
        tokens * model,
    )(*first, *second, *first_grad, *second_grad)


def partial_gradients(count, per, *refs):
    left, right, outs = refs[0:2], refs[2:4], refs[-count:]
    product = dot_tn(left[0][...], right[0][...]) + dot_tn(left[1][...], right[1][...])
    product = product.astype(jnp.bfloat16)
    for k in range(count):

        @pl.when(pl.program_id(0) // per == k)
        def _(k=k):
            outs[k][...] = product


def run_partial_gradients(left, right, count, width, column, into=()):
    tokens, model = left[0].shape
    block_rows = model // count
    tile = min(256, block_rows)
    per = block_rows // tile
    columns = pl.BlockSpec((tokens, tile), lambda i: (0, i))
    part = right[0].shape[1]
    out_spec = lambda k: pl.BlockSpec(
        (tile, part), lambda i: (jnp.clip(i - per * k, 0, per - 1), column)
    )
    return pl.pallas_call(
        functools.partial(partial_gradients, count, per),
        grid=(model // tile,),
        in_specs=[columns] * 2
        + [whole(a) for a in right]
        + [pl.BlockSpec(memory_space=pl.ANY)] * len(into),
        out_specs=[out_spec(k) for k in range(count)],
        out_shape=[shape_of((block_rows, width), jnp.bfloat16)] * count,
        input_output_aliases={4 + k: k for k in range(len(into))},
        compiler_params=pltpu.CompilerParams(vmem_limit_bytes=vmem_limit),
        cost_estimate=pl.CostEstimate(
            flops=2 * tokens * model * 128, bytes_accessed=tokens * model // 2, transcendentals=0
        ),
    )(*left, *right, *into)


def transposed_product(parts, count, *refs):
    lefts = refs[: 2 * parts]
    blocks = refs[2 * parts : 2 * parts + parts * count]
    outs = refs[2 * parts + parts * count :]
    tile = lefts[0].shape[0]
    rows = blocks[0].shape[0]
    for k in range(count):
        total = None
        span = slice(k * rows, (k + 1) * rows)
        for p in range(parts):
            left = jnp.concatenate([lefts[2 * p][...], lefts[2 * p + 1][...]], axis=0)
            more = dot_nt(left, blocks[p * count + k][...])
            total = more if total is None else total + more
        total = total.astype(jnp.bfloat16)
        outs[0][:, span] = total[:tile]
        outs[1][:, span] = total[tile:]


def run_transposed_product(pairs, blocks, column, columns):
    count = len(blocks[0])
    tokens = pairs[0][0].shape[0]
    model = count * blocks[0][0].shape[0]
    tile = min(256, tokens)
    rows = lambda n: pl.BlockSpec((tile, n), lambda i: (i, 0))
    lefts = [a for pair in pairs for a in pair]
    flat = [b for one in blocks for b in one]
    return kernel_call(
        functools.partial(transposed_product, len(pairs), count),
        (tokens // tile,),
        [rows(a.shape[1]) for a in lefts]
        + [pl.BlockSpec((b.shape[0], columns), lambda i: (0, column)) for b in flat],
        [rows(model)] * 2,
        [shape_of((tokens, model), jnp.bfloat16)] * 2,
        2 * tokens * model * 256,
        tokens * model,
    )(*lefts, *flat)


def add_both(*refs):
    for left, right, out in zip(refs[0:2], refs[2:4], refs[4:6]):
        out[...] = (left[...].astype(jnp.float32) + right[...].astype(jnp.float32)).astype(
            jnp.bfloat16
        )


def run_add_both(blocks, got):
    rows, width = blocks[0].shape
    tile = min(256, rows)
    spec = pl.BlockSpec((tile, width), lambda i: (i, 0))
    return kernel_call(
        add_both,
        (rows // tile,),
        [spec] * 4,
        [spec] * 2,
        [shape_of((rows, width), jnp.bfloat16)] * 2,
        1,
        12 * rows * width,
    )(*blocks, *got)


def place_columns(subs, place_ref, *refs):
    ins, outs = refs[: group * subs], refs[group * subs :]
    place = place_ref[0]
    rows = ins[0].shape[0]
    width = ins[0].shape[1] // len(outs)
    for s in range(subs):
        for r, ref in enumerate(ins[group * s : group * (s + 1)]):
            start = ref.shape[0] - rows if r == group - 1 else 0
            column = pl.multiple_of((s * group + (place ^ r)) * width, width)
            for m, out in enumerate(outs):
                piece = ref[start : start + rows, m * width : (m + 1) * width]
                out[:, pl.ds(column, width)] = piece.astype(jnp.float32)


def run_place_columns(place, parts, count):
    rows, width = parts[0][0].shape
    flat = [a for part in parts for a in part]
    full = lambda a: pl.BlockSpec(a.shape, lambda i, place: (0, 0))
    shape = shape_of((rows, width // count * group * len(parts)), jnp.float32)
    return pl.pallas_call(
        functools.partial(place_columns, len(parts)),
        grid_spec=pltpu.PrefetchScalarGridSpec(
            num_scalar_prefetch=1,
            grid=(1,),
            in_specs=[full(a) for a in flat],
            out_specs=[full(shape)] * count,
        ),
        out_shape=[shape] * count,
        compiler_params=pltpu.CompilerParams(vmem_limit_bytes=vmem_limit),
    )(place.reshape(1).astype(jnp.int32), *flat)


def place_halves(place, mine, other, out):
    half = mine.shape[0]
    core = place[0]
    out[pl.ds(core * half, half), :] = mine[...]
    out[pl.ds((1 - core) * half, half), :] = other[...]


def run_place_halves(core, spot, count, mine, other):
    half, model = mine.shape
    block = model // count
    source = pl.BlockSpec((half, block), lambda k, place: (0, k))
    return pl.pallas_call(
        place_halves,
        grid_spec=pltpu.PrefetchScalarGridSpec(
            num_scalar_prefetch=1,
            grid=(count,),
            in_specs=[source, source],
            out_specs=pl.BlockSpec((2 * half, block), lambda k, place: (0, (k + place[1]) % count)),
        ),
        out_shape=shape_of((2 * half, model), jnp.float32),
        compiler_params=pltpu.CompilerParams(vmem_limit_bytes=vmem_limit),
        cost_estimate=pl.CostEstimate(flops=1, bytes_accessed=16 * half * model, transcendentals=0),
    )(jnp.stack([core, spot]).astype(jnp.int32), mine, other)


def swap_cores(values):
    return lax.ppermute(values, "tensor", [(0, 1), (1, 0)])


class Lines:
    def __init__(self, dp):
        self.dp = dp
        self.length = dp // group
        index = lax.axis_index("dp")
        self.place = index % group
        self.spot = index // group

    def flip(self, values, relation):
        return lax.ppermute(values, "dp", [(i, i ^ relation) for i in range(self.dp)])

    def hop(self, values, first, last, step):
        pairs = [
            (spot * group + place, (spot + step) * group + place)
            for spot in range(first, last + 1)
            for place in range(group)
        ]
        return lax.ppermute(values, "dp", pairs)

    def turn(self, values, step):
        pairs = [
            (spot * group + place, ((spot + step) % self.length) * group + place)
            for spot in range(self.length)
            for place in range(group)
        ]
        return lax.ppermute(values, "dp", pairs)

    def by_place(self, related):
        odd = self.place % 2 == 1
        high = self.place // 2 == 1
        own, one, two, three = related
        pairs = (
            (jnp.where(odd, one, own), jnp.where(odd, own, one)),
            (jnp.where(odd, three, two), jnp.where(odd, two, three)),
        )
        return [
            jnp.where(high, pairs[1][0], pairs[0][0]),
            jnp.where(high, pairs[1][1], pairs[0][1]),
            jnp.where(high, pairs[0][0], pairs[1][0]),
            jnp.where(high, pairs[0][1], pairs[1][1]),
        ]

    def pieces(self, piece_of):
        return [piece_of(self.place ^ relation) for relation in range(group)]

    def flip_pieces(self, pieces):
        return [pieces[0]] + [self.flip(pieces[r], r) for r in range(1, group)]

    def flip_first(self, pieces):
        return self.flip(jnp.concatenate([pieces[1], pieces[3]]), 1)

    def flip_second(self, pieces, got):
        return self.flip(jnp.concatenate([pieces[2], got[got.shape[0] // 2 :]]), 2)

    def flipped(self, pieces, first, second):
        rows = pieces[0].shape[0]
        return [pieces[0], first[:rows], second[:rows], second[rows:]]

    def row_pieces(self, total):
        rows = total.shape[0] // group
        return [
            lax.dynamic_slice_in_dim(total, (self.place ^ r) * rows, rows) for r in range(group)
        ]

    def gather_near(self, mine):
        return [self.flip(mine, 1), self.flip(mine, 2)]

    def gather_across(self, near):
        middle = near[0].shape[0] // 2
        return [self.flip(near[0][:middle], 2), self.flip(near[1][middle:], 1)]

    def scatter_across(self, across):
        middle = across.shape[0] // 2
        return [self.flip(across[:middle], 1), self.flip(across[middle:], 2)]

    def gather_far(self, mine):
        near = self.gather_near(mine)
        return near, self.gather_across(near)

    def gather_tokens(self, mine):
        return self.both_cores(mine, *self.gather_far(mine))

    def both_cores(self, mine, near, across):
        kept = jnp.concatenate([mine] + near + across)
        return kept, swap_cores(kept)

    def terms(self, kept, other, relation):
        rows = kept.shape[0] // group
        span = slice(relation * rows, (relation + 1) * rows)
        return kept[span].astype(jnp.float32) + other[span].astype(jnp.float32)

    def across_terms(self, kept, other):
        return self.scatter_across(self.terms(kept, other, 3).astype(jnp.bfloat16))

    def near_sends(self, kept, other, got):
        one, two = self.terms(kept, other, 1), self.terms(kept, other, 2)
        middle = one.shape[0] // 2
        one = jnp.concatenate([one[:middle], one[middle:] + got[1].astype(jnp.float32)])
        two = jnp.concatenate([two[:middle] + got[0].astype(jnp.float32), two[middle:]])
        return [one.astype(jnp.bfloat16), two.astype(jnp.bfloat16)]

    def near_flips(self, kept, other, got):
        one, two = self.near_sends(kept, other, got)
        return [self.flip(one, 1), self.flip(two, 2)]

    def near_sum(self, kept, other, near):
        one, two = near
        return self.terms(kept, other, 0) + one.astype(jnp.float32) + two.astype(jnp.float32)

    def near_terms(self, kept, other, got):
        return self.near_sum(kept, other, self.near_flips(kept, other, got))

    def scatter_tokens(self, kept, other):
        return self.near_terms(kept, other, self.across_terms(kept, other))


class LineGather:
    def __init__(self, lines, block):
        self.lines, self.block, self.got = lines, block, []

    def hop(self):
        lines, step = self.lines, len(self.got) + 1
        if lines.length != 4:
            turns = range(1, lines.length) if step == 1 else ()
            self.got.append([lines.turn(self.block, -k) for k in turns])
            return
        up, down = self.got[-1] if self.got else (self.block, self.block)
        self.got.append(
            [
                lines.hop(up, step - 1, lines.length - 2, 1),
                lines.hop(down, 1, lines.length - step, -1),
            ]
        )

    def blocks(self):
        lines = self.lines
        if lines.length != 4:
            return [self.block] + self.got[0]
        return [self.block] + [
            jnp.where(
                lines.spot + k < lines.length,
                self.got[k - 1][1],
                self.got[lines.length - k - 1][0],
            )
            for k in range(1, lines.length)
        ]


class LineScatter:
    def __init__(self, lines, blocks):
        self.lines, self.blocks, self.got = lines, blocks, []

    def ready(self):
        step = len(self.got) + 1
        if self.lines.length != 4:
            return []
        blocks = [self.blocks[self.lines.length - step], self.blocks[step]]
        return run_add_both(blocks, self.got[-1]) if self.got else blocks

    def hop(self, ready=None):
        lines, step = self.lines, len(self.got) + 1
        if lines.length != 4:
            turns = range(1, lines.length) if step == 1 else ()
            self.got.append([lines.turn(self.blocks[k], k) for k in turns])
            return
        up, down = self.ready() if ready is None else ready
        self.got.append(
            [
                lines.hop(up, 0, min(step - 1, lines.length - 2), 1),
                lines.hop(down, max(lines.length - step, 1), lines.length - 1, -1),
            ]
        )

    def total(self):
        last = self.got[-1] if self.lines.length == 4 else self.got[0]
        result = self.blocks[0].astype(jnp.float32)
        for one in last:
            result = result + one.astype(jnp.float32)
        return result.astype(jnp.bfloat16)


def tie(*values):
    return lax.optimization_barrier(values)


def local(
    dp,
    tokens,
    segments,
    cotangent,
    attn_gain,
    ffn_gain,
    query_gain,
    key_gain,
    w_query,
    key_weight,
    value_weight,
    w_out,
    w_gate,
    w_up,
    w_down,
):
    lines = Lines(dp)
    core = lax.axis_index("tensor")
    length, width = tokens.shape
    half = length // 2
    head_dim = query_gain.shape[0]
    rows = w_query.shape[0]
    block_rows = rows * group
    query_width = w_query.shape[1] // group
    key_width = key_weight.shape[1] // group
    attn_width = query_width + 2 * key_width
    ff_sub = w_gate.shape[1] // group // sub_count

    def around(values):
        return jnp.roll(values, -lines.spot * block_rows, axis=-1)

    def back_around(values):
        return jnp.roll(values, lines.spot * block_rows, axis=-1)

    attn_gain_r, ffn_gain_r = around(attn_gain), around(ffn_gain)

    def columns(weight, start, size):
        return lax.dynamic_slice_in_dim(weight, start, size, axis=1)

    attn_pieces = lines.pieces(
        lambda j: jnp.concatenate(
            [
                columns(w_query, j * query_width, query_width),
                columns(key_weight, j * key_width, key_width),
                columns(value_weight, j * key_width, key_width),
                columns(w_out, j * query_width, query_width),
            ],
            axis=1,
        )
    )
    attn_shared = lines.flip_pieces(attn_pieces)
    source = around(lax.dynamic_slice_in_dim(tokens, core * half, half)).astype(jnp.float32)
    normed_f, scale_first = norm_rows(source, attn_gain_r)
    normed_mine = normed_f.astype(jnp.bfloat16)

    seg_near = jnp.concatenate([segments, lines.flip(segments, 1)])
    seg_second = lines.flip(seg_near, 2)
    attn_shared, normed_mine, seg_near, seg_second = tie(
        attn_shared, normed_mine, seg_near, seg_second
    )

    def ffn_piece(s):
        return lines.pieces(
            lambda j: jnp.concatenate(
                [
                    columns(weight, s * group * ff_sub + j * ff_sub, ff_sub)
                    for weight in (w_gate, w_up, w_down)
                ],
                axis=1,
            )
        )


    seg_all = jnp.concatenate([seg_near, seg_second])
    positions = jax.vmap(positions_of)(seg_all)
    index = jnp.arange(length, dtype=jnp.int32)
    cosine, sine = angles(positions, head_dim, 2 * head_dim)
    swapped = jnp.full((1, 1), core, jnp.int32)
    starts = index[None] - positions
    tables = (swapped, cosine, sine, starts[..., None], starts[:, None, :], index)
    gains_two = jnp.stack(
        [
            jnp.tile(query_gain, query_width // head_dim),
            jnp.tile(key_gain, query_width // head_dim),
        ]
    )

    attn_line = LineGather(lines, jnp.concatenate(lines.by_place(attn_shared), axis=0))
    attn_line.hop()
    near = lines.gather_near(normed_mine)
    mine_other = swap_cores(normed_mine)
    near, attn_line.got[0], tables, mine_other, w_gate, w_up, w_down = tie(
        near, attn_line.got[0], tables, mine_other, w_gate, w_up, w_down
    )
    attn_line.hop()
    across = lines.gather_across(near)
    pieces_0 = ffn_piece(0)
    near_other = swap_cores(near[0])
    near_other, near_two = tie(near_other, near[1])
    near = [near[0], near_two]
    near_other = [near_other, swap_cores(near_two)]
    across, attn_line.got[1], pieces_0, near_other, w_gate, w_up, w_down, cotangent = tie(
        across, attn_line.got[1], pieces_0, near_other, w_gate, w_up, w_down, cotangent
    )
    attn_line.hop()
    pieces_1 = ffn_piece(1)
    cot_half = around(lax.dynamic_slice_in_dim(cotangent, core * half, half))
    out_mine = cot_half.astype(jnp.bfloat16)
    across = jnp.concatenate(across)
    normed = (
        jnp.concatenate([normed_mine] + near + [across]),
        jnp.concatenate([mine_other] + near_other + [swap_cores(across)]),
    )
    shared_0 = lines.flip_pieces(pieces_0)
    normed, attn_line.got[2], shared_0, pieces_1, out_mine = tie(
        normed, attn_line.got[2], shared_0, pieces_1, out_mine
    )
    attn_w = attn_line.blocks()

    line_0 = LineGather(lines, jnp.concatenate(lines.by_place(shared_0), axis=0))
    line_0.hop()
    out_near = lines.gather_near(out_mine)
    qkv_raw, heads_out, attended_kept, attended_other = run_attention(
        True, normed, attn_w, tables, gains_two, head_dim, query_width, attn_width
    )
    attended_other, line_0.got[0], out_near, pieces_1 = tie(
        attended_other, line_0.got[0], out_near, pieces_1
    )

    line_0.hop()
    attended_other = swap_cores(attended_other)
    middle = half // 2
    out_first = lines.flip(out_near[0][:middle], 2)
    attended_other, out_first = tie(attended_other, out_first)
    first_1 = lines.flip_first(pieces_1)
    got = lines.across_terms(attended_kept, attended_other)
    got, first_1, line_0.got[1] = tie(got, first_1, line_0.got[1])
    line_0.hop()
    second_1 = lines.flip_second(pieces_1, first_1)
    attended = lines.near_terms(attended_kept, attended_other, got)
    attended, out_near = tie(attended, out_near)
    out_second = lines.flip(out_near[1][middle:], 1)
    attended, line_0.got[2], out_first, out_second, second_1 = tie(
        attended, line_0.got[2], out_first, out_second, second_1
    )
    shared_1 = lines.flipped(pieces_1, first_1, second_1)
    block_1 = jnp.concatenate(lines.by_place(shared_1), axis=0)

    line_1 = LineGather(lines, block_1)
    out_b = lines.both_cores(out_mine, out_near, [out_first, out_second])
    line_1.hop()
    state = source + attended
    normed2_f, scale_second = norm_rows(state, ffn_gain_r)
    near, across = lines.gather_far(normed2_f.astype(jnp.bfloat16))
    ffn_w = [line_0.blocks()]
    near, across, line_1.got[0], out_b, ffn_w[0] = tie(
        near, across, line_1.got[0], out_b, ffn_w[0]
    )

    line_1.hop()
    normed2 = lines.both_cores(normed2_f.astype(jnp.bfloat16), near, across)
    units_0 = run_ffn_units(normed2, out_b, ffn_w[0], ff_sub)
    units_0, line_1.got[1] = tie(units_0, line_1.got[1])
    line_1.hop()
    ffn_g = run_weight_gradients(normed2, units_0[2:], out_b, units_0[:2], lines.length)
    ffn_g, line_1.got[2], units_0 = tie(ffn_g, line_1.got[2], units_0)
    sum_0 = LineScatter(lines, ffn_g)
    ffn_w.append(line_1.blocks())

    sum_0.hop()
    units_1 = run_ffn_units(normed2, out_b, ffn_w[1], ff_sub, units_0[2:], ffn_w[0])
    kept, other = units_1[4:]
    kept, other, sum_0.got[0], units_1 = tie(kept, other, sum_0.got[0], units_1)

    sum_0.hop()
    other = swap_cores(other)
    send = lines.terms(kept, other, 3).astype(jnp.bfloat16)
    send, units_1 = tie(send, units_1)
    got = lines.scatter_across(send)
    branch_kept, branch_other = run_transposed_product(
        [units_0[:2], units_1[:2]], ffn_w, 2, ff_sub
    )
    ffn_g = run_partial_gradients(normed2, units_1[2:4], lines.length, 3 * ff_sub, 0)
    got, sum_0.got[1], ffn_g, branch_kept, branch_other, units_1 = tie(
        got, sum_0.got[1], ffn_g, branch_kept, branch_other, units_1
    )
    sum_0.hop()
    branch_other = swap_cores(branch_other)
    near = lines.near_flips(kept, other, got)
    ffn_g = run_partial_gradients(out_b, units_1[:2], lines.length, 3 * ff_sub, 2, ffn_g)
    near, branch_kept, branch_other, ffn_g = tie(near, branch_kept, branch_other, ffn_g)
    sum_1 = LineScatter(lines, ffn_g)
    normed2_grad = lines.near_sum(kept, other, near)
    branch_got = lines.across_terms(branch_kept, branch_other)
    normed2_grad, sum_0.got[2], branch_got = tie(normed2_grad, sum_0.got[2], branch_got)

    sum_1.hop()
    ffn_gain_part = jnp.sum(normed2_grad * state * scale_second, axis=0)
    state_grad = cot_half + norm_back(state, scale_second, ffn_gain_r, normed2_grad)
    grad_mine = state_grad.astype(jnp.bfloat16)
    near, across = lines.gather_far(grad_mine)
    back_0 = lines.row_pieces(sum_0.total())
    branch_terms = lines.near_sends(branch_kept, branch_other, branch_got)
    ready = sum_1.ready()
    near, across, ready, back_0, branch_terms = tie(near, across, ready, back_0, branch_terms)

    sum_1.hop(ready)
    attended_b = lines.both_cores(grad_mine, near, across)

    branch = [lines.flip(branch_terms[0], 1), lines.flip(branch_terms[1], 2)]
    back_0_first = lines.flip_first(back_0)
    qkv_grad, gain_parts, kept, other, attn_gain_part = run_attention(
        False,
        attended_b,
        attn_w,
        tables,
        gains_two,
        head_dim,
        query_width,
        attn_width,
        qkv_raw,
        normed,
    )
    kept, other, qkv_grad, branch, sum_1.got[1], back_0, back_0_first = tie(
        kept, other, qkv_grad, branch, sum_1.got[1], back_0, back_0_first
    )

    sum_1.hop()
    gains = jnp.concatenate(
        [
            back_around(attn_gain_part[0] / attn_gain_r),
            back_around(ffn_gain_part),
            jnp.sum(gain_parts[0].reshape(-1, head_dim), axis=0),
            gain_parts[1][:head_dim],
        ]
    )
    other = swap_cores(other)
    back_0_second = lines.flip_second(back_0, back_0_first)
    got = lines.across_terms(kept, other)
    attn_sum = LineScatter(
        lines, run_weight_gradients(normed, qkv_grad, attended_b, heads_out, lines.length)
    )
    got, sum_1.got[2], attn_sum.blocks, back_0_second, gains = tie(
        got, sum_1.got[2], attn_sum.blocks, back_0_second, gains
    )
    attn_sum.hop()
    back_1 = lines.row_pieces(sum_1.total())
    near = lines.near_flips(kept, other, got)
    attn_sum.hop()
    gains_got = lines.flip(gains, 1)
    mixed = state + lines.near_sum(branch_kept, branch_other, branch)
    mixed_other = swap_cores(mixed)
    near, attn_sum.got[1], back_1, mixed, mixed_other, gains_got = tie(
        near, attn_sum.got[1], back_1, mixed, mixed_other, gains_got
    )
    attn_sum.hop()
    back_1 = lines.flip_pieces(back_1)
    gains = gains + gains_got
    gains_got = lines.flip(gains, 2)
    mixed = run_place_halves(core, lines.spot, lines.length, mixed, mixed_other)
    attn_sum.got[2], back_1, near, gains, gains_got, mixed = tie(
        attn_sum.got[2], back_1, near, gains, gains_got, mixed
    )
    gains = gains + gains_got
    attn_grads = lines.flip_pieces(lines.row_pieces(attn_sum.total()))
    normed_grad = lines.near_sum(kept, other, near)
    input_grad = state_grad + norm_back(source, scale_first, attn_gain_r, normed_grad)
    input_other = swap_cores(input_grad)
    bit = group
    while bit < dp:
        gains = gains + lines.flip(gains, bit)
        bit *= 2
        if bit == 2 * group:
            gains, attn_grads = tie(gains, attn_grads)
    gains = gains + swap_cores(gains)
    ffn_grads = run_place_columns(
        lines.place,
        [
            (back_0[0], back_0_first, back_0_second, back_0_second),
            back_1,
        ],
        3,
    )

    def columns_of(related, start, stop):
        blocks = lines.by_place([b[:, start:stop] for b in related])
        return jnp.concatenate(blocks, axis=1).astype(jnp.float32)

    return (
        mixed,
        run_place_halves(core, lines.spot, lines.length, input_grad, input_other),
        gains[:width],
        gains[width : 2 * width],
        gains[2 * width : 2 * width + head_dim],
        gains[2 * width + head_dim :],
        columns_of(attn_grads, 0, query_width),
        columns_of(attn_grads, query_width, query_width + key_width),
        columns_of(attn_grads, query_width + key_width, attn_width),
        columns_of(attn_grads, attn_width, attn_width + query_width),
        *ffn_grads,
    )


def solution(mesh):
    dp = mesh.shape["dp"]
    weight = P("dp", "tensor")
    rows = P("dp", None)
    return jax.shard_map(
        lambda *arrays: local(dp, *arrays),
        mesh=mesh,
        in_specs=(rows, rows, rows, P(), P(), P(), P()) + (weight,) * 7,
        out_specs=(rows, rows, P(), P(), P(), P()) + (weight,) * 7,
        check_vma=False,
    )
```

```python
import functools

import jax
import jax.numpy as jnp
from jax import lax
from jax.experimental import pallas as pl
from jax.experimental.pallas import tpu as pltpu
from jax.sharding import PartitionSpec as P

eps = 1e-05
rope_base = 1000000.0
group = 4
sub_count = 2
vmem_limit = 52 * 1024 * 1024


def norm_rows(values, gain):
    scale = lax.rsqrt(jnp.mean(values * values, axis=-1, keepdims=True) + eps)
    return (values * scale * gain, scale)


def norm_back(values, scale, gain, incoming):
    weighted = incoming * gain
    return scale * weighted - values * (scale * scale * scale) * jnp.mean(
        weighted * values, axis=-1, keepdims=True
    )


def positions_of(segment_row):
    row_index = jnp.arange(segment_row.shape[0], dtype=jnp.int32)
    earlier = jnp.concatenate([segment_row[:1] - 1, segment_row[:-1]])
    starts = jnp.where(segment_row != earlier, row_index, jnp.zeros_like(row_index))
    return row_index - lax.cummax(starts, axis=0)


def angles(positions, width, lanes):
    frequency = rope_base ** (-jnp.arange(0, width, 2, dtype=jnp.float32) / width)
    frequency = jnp.tile(frequency, 2 * lanes // width)
    phases = positions.astype(jnp.float32)[..., None] * frequency
    return (jnp.cos(phases), jnp.sin(phases))


def dot_nn(left, right):
    return jnp.dot(left, right, preferred_element_type=jnp.float32)


def dot_nt(left, right):
    return lax.dot_general(
        left, right, (((1,), (1,)), ((), ())), preferred_element_type=jnp.float32
    )


def dot_tn(left, right):
    return lax.dot_general(
        left, right, (((0,), (0,)), ((), ())), preferred_element_type=jnp.float32
    )


def pick_dot(left, right):
    high = left.astype(jnp.bfloat16)
    low = (left - high.astype(jnp.float32)).astype(jnp.bfloat16)
    return dot_nn(high, right) + dot_nn(low, right)


def kernel_call(body, grid, in_specs, out_specs, out_shape, flops, moved):
    return pl.pallas_call(
        body,
        grid=grid,
        in_specs=in_specs,
        out_specs=out_specs,
        out_shape=out_shape,
        compiler_params=pltpu.CompilerParams(vmem_limit_bytes=vmem_limit),
        cost_estimate=pl.CostEstimate(flops=flops, bytes_accessed=moved, transcendentals=0),
    )


def whole(array):
    rank = len(array.shape)
    return pl.BlockSpec(array.shape, lambda *_: (0,) * rank)


def shape_of(shape, kind):
    return jax.ShapeDtypeStruct(shape, kind)


def turn_heads(values, head_dim):
    lanes = values.shape[-1]
    middle = head_dim // 2
    lane = lax.broadcasted_iota(jnp.int32, values.shape, 1) % head_dim
    ahead = pltpu.roll(values, lanes - middle, 1)
    behind = pltpu.roll(values, middle, 1)
    return jnp.where(lane < middle, -ahead, behind)


def index_pair(rows, columns):
    return (
        lax.broadcasted_iota(jnp.int32, (rows, columns), 0),
        lax.broadcasted_iota(jnp.int32, (rows, columns), 1),
    )


def ones_where(condition):
    return condition.astype(jnp.float32).astype(jnp.bfloat16)


def spread_of(rows, offset, columns, head_dim):
    row, column = index_pair(rows, columns)
    return ones_where(row - offset == column % head_dim)


def fold(values, head_dim):
    row, column = index_pair(values.shape[1], values.shape[1])
    return pick_dot(values, ones_where(row % head_dim == column % head_dim))


def head_mean(values, head_dim):
    row, column = index_pair(values.shape[1], values.shape[1])
    return pick_dot(values, ones_where(row // head_dim == column // head_dim)) * (1.0 / head_dim)


def prepare_heads(raw, gain, cosine, sine, head_dim):
    scale = lax.rsqrt(head_mean(raw * raw, head_dim) + eps)
    scaled = raw * scale * gain
    return scaled * cosine + turn_heads(scaled, head_dim) * sine, scale


def prepare_back(raw, scale, gain, cosine, sine, incoming, head_dim):
    turned = incoming * cosine - turn_heads(incoming * sine, head_dim)
    weighted = turned * gain
    grad = scale * weighted - raw * (scale * scale * scale) * head_mean(weighted * raw, head_dim)
    return grad, jnp.sum(turned * raw * scale, axis=0, keepdims=True)


def head_inputs(raw, gains, cosine, sine, head_dim, width):
    query, query_scale = prepare_heads(raw[:, :width], gains[0:1], cosine, sine, head_dim)
    rest = raw[:, width:]
    key_raw = pick_dot(rest, spread_of(rest.shape[1], 0, width, head_dim))
    key, key_scale = prepare_heads(key_raw, gains[1:2], cosine, sine, head_dim)
    value = dot_nn(
        rest.astype(jnp.bfloat16), spread_of(rest.shape[1], head_dim, width, head_dim)
    ).astype(jnp.bfloat16)
    return (
        query.astype(jnp.bfloat16) * jnp.bfloat16(0.125),
        query_scale,
        key_raw,
        key.astype(jnp.bfloat16),
        key_scale,
        value,
    )


def only_head(values, head, head_dim):
    lane = lax.broadcasted_iota(jnp.int32, values.shape, 1)
    return jnp.where(lane // head_dim == head, values, jnp.zeros_like(values))


def exps_of(scores, allowed):
    return jnp.exp(jnp.where(allowed, scores, -1000000000.0))


def block_product(kept, other, blocks, start, stop):
    rows = blocks[0].shape[0]
    total = None
    for k, block in enumerate(blocks):
        left = jnp.concatenate(
            [kept[:, k * rows : (k + 1) * rows], other[:, k * rows : (k + 1) * rows]], axis=0
        )
        more = dot_nn(left, block[:, start:stop])
        total = more if total is None else total + more
    return total


def by_halves(swapped, one, two):
    return jnp.where(swapped, two, one), jnp.where(swapped, one, two)


def head_tables(cosine_ref, sine_ref, width):
    repeat = width // cosine_ref.shape[-1]
    return (
        jnp.concatenate([cosine_ref[0]] * repeat, axis=1),
        jnp.concatenate([sine_ref[0]] * repeat, axis=1),
    )


def attention_forward(count, head_dim, width, *refs):
    kept, other = refs[:2]
    refs = refs[2:]
    swap_ref, cosine_ref, sine_ref, start_ref, index_column, index_row, gains = refs[:7]
    blocks = refs[7 : 7 + count]
    raw_ref, heads_kept, heads_other, part_kept, part_other = refs[7 + count :]
    half = kept.shape[0]
    attn_width = raw_ref.shape[-1]
    raw = block_product(kept, other, blocks, 0, attn_width)
    swapped = swap_ref[...] == 1
    raw = jnp.concatenate(by_halves(swapped, raw[:half], raw[half:]), axis=0)
    raw_ref[0] = raw
    cosine, sine = head_tables(cosine_ref, sine_ref, width)
    query, _, _, key, _, value = head_inputs(raw, gains[...], cosine, sine, head_dim, width)
    allowed = (index_row[...] <= index_column[...]) & (index_row[...] >= start_ref[0])
    one = jnp.zeros((half, width), jnp.float32)
    two = one
    for head in range(width // head_dim):
        query_h = only_head(query, head, head_dim)
        for first in (True, False):
            span, keys = (slice(0, half), half) if first else (slice(half, 2 * half), 2 * half)
            exps = exps_of(dot_nt(query_h[span], key[:keys]), allowed[span, :keys])
            part = dot_nn(exps.astype(jnp.bfloat16), value[:keys])
            part = part * (1.0 / jnp.sum(exps, axis=-1, keepdims=True))
            part = only_head(part, head, head_dim)
            if first:
                one = one + part
            else:
                two = two + part
    heads = by_halves(swapped, one.astype(jnp.bfloat16), two.astype(jnp.bfloat16))
    heads_kept[...] = heads[0]
    heads_other[...] = heads[1]
    heads = jnp.concatenate(heads, axis=0)
    rows = blocks[0].shape[0]
    for k, block in enumerate(blocks):
        out = dot_nt(heads, block[:, attn_width : attn_width + width]).astype(jnp.bfloat16)
        part_kept[:, k * rows : (k + 1) * rows] = out[:half]
        part_other[:, k * rows : (k + 1) * rows] = out[half:]


def attention_backward(count, head_dim, width, *refs):
    kept, other, raw_ref, normed_kept, normed_other = refs[:5]
    refs = refs[5:]
    swap_ref, cosine_ref, sine_ref, start_ref, index_column, index_row, gains = refs[:7]
    blocks = refs[7 : 7 + count]
    grad_kept, grad_other, gain_ref, part_kept, part_other, scaled_ref = refs[7 + count :]
    half = kept.shape[0]
    attn_width = raw_ref.shape[-1]
    grads = block_product(kept, other, blocks, attn_width, attn_width + width)
    grads = grads.astype(jnp.bfloat16)
    swapped = swap_ref[...] == 1
    grads = jnp.concatenate(by_halves(swapped, grads[:half], grads[half:]), axis=0)
    raw = raw_ref[0]
    cosine, sine = head_tables(cosine_ref, sine_ref, width)
    query, query_scale, key_raw, key, key_scale, value = head_inputs(
        raw, gains[...], cosine, sine, head_dim, width
    )
    allowed = (index_column[...] <= index_row[...]) & (index_column[...] >= start_ref[0])
    zero = jnp.zeros((half, width), jnp.float32)
    query_grads, key_grads, value_grads = [zero, zero], [zero, zero], [zero, zero]
    for head in range(width // head_dim):
        query_h = only_head(query, head, head_dim)
        grad_h = only_head(grads, head, head_dim)
        for part in range(2):
            span, keys = slice(part * half, (part + 1) * half), (part + 1) * half
            exps = exps_of(dot_nt(key[:keys], query_h[span]), allowed[:keys, span])
            probs_f = exps * (1.0 / jnp.sum(exps, axis=0, keepdims=True))
            weighted = probs_f * dot_nt(value[:keys], grad_h[span])
            score_grad = weighted - probs_f * jnp.sum(weighted, axis=0, keepdims=True)
            score_grad = score_grad.astype(jnp.bfloat16)
            query_grads[part] += only_head(dot_tn(score_grad, key[:keys]), head, head_dim)
            value_part = dot_nn(probs_f.astype(jnp.bfloat16), grad_h[span])
            key_part = dot_nn(score_grad, query_h[span])
            for block in range(part + 1):
                rows = slice(block * half, (block + 1) * half)
                value_grads[block] += value_part[rows]
                key_grads[block] += key_part[rows]
    query_grad = 0.125 * jnp.concatenate(query_grads, axis=0)
    key_grad = fold(jnp.concatenate(key_grads, axis=0), head_dim)
    value_grad = fold(jnp.concatenate(value_grads, axis=0), head_dim)
    query_grad, query_gain_part = prepare_back(
        raw[:, :width], query_scale, gains[0:1], cosine, sine, query_grad, head_dim
    )
    key_grad, key_gain_part = prepare_back(
        key_raw, key_scale, gains[1:2], cosine, sine, key_grad, head_dim
    )
    rest = attn_width - width
    lane = lax.broadcasted_iota(jnp.int32, (2 * half, rest), 1)
    rest_grad = jnp.where(lane < head_dim, key_grad[:, :rest], value_grad[:, :rest])
    query_grad = query_grad.astype(jnp.bfloat16)
    rest_grad = rest_grad.astype(jnp.bfloat16)
    query_sides = by_halves(swapped, query_grad[:half], query_grad[half:])
    rest_sides = by_halves(swapped, rest_grad[:half], rest_grad[half:])
    all_sides = []
    for side, out in enumerate((grad_kept, grad_other)):
        both = jnp.concatenate([query_sides[side], rest_sides[side]], axis=1)
        out[...] = both
        all_sides.append(both)
    all_sides = jnp.concatenate(all_sides, axis=0)
    parts = jnp.concatenate([query_gain_part, key_gain_part], axis=0)

    @pl.when(pl.program_id(0) == 0)
    def _():
        scaled_ref[...] = jnp.zeros_like(scaled_ref)

    rows = blocks[0].shape[0]
    for k, block in enumerate(blocks):
        span = slice(k * rows, (k + 1) * rows)
        out = dot_nt(all_sides, block[:, :attn_width])
        scaled = out[:half] * normed_kept[:, span].astype(jnp.float32)
        scaled = scaled + out[half:] * normed_other[:, span].astype(jnp.float32)
        scaled_ref[:, span] += jnp.sum(scaled, axis=0, keepdims=True)
        out = out.astype(jnp.bfloat16)
        part_kept[:, span] = out[:half]
        part_other[:, span] = out[half:]

    @pl.when(pl.program_id(0) == 0)
    def _():
        gain_ref[...] = parts

    @pl.when(pl.program_id(0) != 0)
    def _():
        gain_ref[...] = gain_ref[...] + parts


def run_attention(forward, pair, blocks, tables, gains, head_dim, width, attn_width, raw=None, normed=None):
    half = pair[0].shape[0] // group
    model = pair[0].shape[1]
    swapped, cosine, sine, start_columns, start_rows, index = tables
    starts = start_columns if forward else start_rows
    rows = lambda n: pl.BlockSpec((half, n), lambda s: (s, 0))
    per_sequence = lambda shape: pl.BlockSpec((1,) + shape[1:], lambda s: (s, 0, 0))
    column, row = index[:, None], index[None, :]
    common = [swapped, cosine, sine, starts, column, row, gains]
    common_specs = [whole(swapped)] + [per_sequence(a.shape) for a in (cosine, sine, starts)]
    common_specs += [whole(column), whole(row), whole(gains)]
    common += blocks
    common_specs += [whole(b) for b in blocks]
    raw_shape = (group, 2 * half, attn_width)
    flops = 2 * 2 * group * half * model * attn_width * 10
    moved = 16 * group * half * model
    side = lambda n: shape_of((group * half, n), jnp.bfloat16)
    if forward:
        results = kernel_call(
            functools.partial(attention_forward, len(blocks), head_dim, width),
            (group,),
            [rows(model)] * 2 + common_specs,
            [per_sequence(raw_shape), rows(width), rows(width), rows(model), rows(model)],
            [shape_of(raw_shape, jnp.float32), side(width), side(width), side(model), side(model)],
            flops,
            moved,
        )(*pair, *common)
        return results[0], tuple(results[1:3]), results[3], results[4]
    results = kernel_call(
        functools.partial(attention_backward, len(blocks), head_dim, width),
        (group,),
        [rows(model)] * 2 + [per_sequence(raw_shape)] + [rows(model)] * 2 + common_specs,
        [rows(attn_width), rows(attn_width), pl.BlockSpec((2, width), lambda s: (0, 0))]
        + [rows(model)] * 2
        + [pl.BlockSpec((1, model), lambda s: (0, 0))],
        [side(attn_width), side(attn_width), shape_of((2, width), jnp.float32)]
        + [side(model)] * 2
        + [shape_of((1, model), jnp.float32)],
        flops,
        moved,
    )(*pair, raw, *normed, *common)
    return tuple(results[:2]), *results[2:]


def ffn_units(count, ff_sub, earlier, *refs):
    normed, out = refs[0:2], refs[2:4]
    blocks, refs = refs[4 : 4 + count], refs[4 + count :]
    if earlier:
        before, refs = refs[0:2], refs[2:]
    inner_refs, grad_refs, terms = refs[0:2], refs[2:4], refs[4:6]
    tile = normed[0].shape[0]
    gate_up = block_product(normed[0], normed[1], blocks, 0, 2 * ff_sub)
    inner_grad = block_product(out[0], out[1], blocks, 2 * ff_sub, 3 * ff_sub)
    gate, up = gate_up[:, :ff_sub], gate_up[:, ff_sub:]
    sigmoid = 1.0 / (1.0 + jnp.exp(-gate))
    silu = gate * sigmoid
    inner = (silu * up).astype(jnp.bfloat16)
    gate_grad = (inner_grad * up * sigmoid * (1.0 + gate * (1.0 - sigmoid))).astype(jnp.bfloat16)
    up_grad = (inner_grad * silu).astype(jnp.bfloat16)
    for side in range(2):
        rows = slice(side * tile, (side + 1) * tile)
        inner_refs[side][...] = inner[rows]
        grad_refs[side][:, :ff_sub] = gate_grad[rows]
        grad_refs[side][:, ff_sub:] = up_grad[rows]
    if not earlier:
        return
    here = jnp.concatenate([gate_grad, up_grad], axis=1)
    rows = blocks[0].shape[0]
    for k in range(count):
        span = slice(k * rows, (k + 1) * rows)
        total = dot_nt(here, blocks[k][:, : 2 * ff_sub])
        for side in range(2):
            part = total[side * tile : (side + 1) * tile]
            part = part + before[side][:, span].astype(jnp.float32)
            terms[side][:, span] = part.astype(jnp.bfloat16)


def run_ffn_units(normed, out, blocks, ff_sub, before=None):
    tokens, model = normed[0].shape
    tile = min(256, tokens)
    rows = lambda n: pl.BlockSpec((tile, n), lambda i: (i, 0))
    earlier = before is not None
    shapes = [ff_sub] * 2 + [2 * ff_sub] * 2 + [model] * 2 * earlier
    return kernel_call(
        functools.partial(ffn_units, len(blocks), ff_sub, earlier),
        (tokens // tile,),
        [rows(model)] * 4
        + [whole(b) for b in blocks]
        + [rows(model)] * 2 * earlier,
        [rows(n) for n in shapes],
        [shape_of((tokens, n), jnp.bfloat16) for n in shapes],
        12 * tokens * model * ff_sub,
        8 * tokens * model,
    )(*normed, *out, *blocks, *(before if earlier else ()))


def weight_gradients(count, per, *refs):
    first, second = refs[0:2], refs[2:4]
    first_grad, second_grad = refs[4:6], refs[6:8]
    outs = refs[8:]
    one = dot_tn(first[0][...], first_grad[0][...]) + dot_tn(first[1][...], first_grad[1][...])
    two = dot_tn(second[0][...], second_grad[0][...]) + dot_tn(second[1][...], second_grad[1][...])
    width = one.shape[1]
    for k in range(count):

        @pl.when(pl.program_id(0) // per == k)
        def _(k=k):
            outs[k][:, :width] = one.astype(jnp.bfloat16)
            outs[k][:, width:] = two.astype(jnp.bfloat16)


def run_weight_gradients(first, first_grad, second, second_grad, count):
    tokens, model = first[0].shape
    block_rows = model // count
    tile = min(256, block_rows)
    per = block_rows // tile
    width = first_grad[0].shape[1] + second_grad[0].shape[1]
    columns = pl.BlockSpec((tokens, tile), lambda i: (0, i))
    out_spec = lambda k: pl.BlockSpec(
        (tile, width), lambda i: (jnp.clip(i - per * k, 0, per - 1), 0)
    )
    return kernel_call(
        functools.partial(weight_gradients, count, per),
        (model // tile,),
        [columns] * 4 + [whole(a) for a in (*first_grad, *second_grad)],
        [out_spec(k) for k in range(count)],
        [shape_of((block_rows, width), jnp.bfloat16)] * count,
        2 * tokens * model * 256,
        tokens * model,
    )(*first, *second, *first_grad, *second_grad)


def partial_gradients(count, per, *refs):
    left, right, outs = refs[0:2], refs[2:4], refs[-count:]
    product = dot_tn(left[0][...], right[0][...]) + dot_tn(left[1][...], right[1][...])
    product = product.astype(jnp.bfloat16)
    for k in range(count):

        @pl.when(pl.program_id(0) // per == k)
        def _(k=k):
            outs[k][...] = product


def run_partial_gradients(left, right, count, width, column, into=()):
    tokens, model = left[0].shape
    block_rows = model // count
    tile = min(256, block_rows)
    per = block_rows // tile
    columns = pl.BlockSpec((tokens, tile), lambda i: (0, i))
    part = right[0].shape[1]
    out_spec = lambda k: pl.BlockSpec(
        (tile, part), lambda i: (jnp.clip(i - per * k, 0, per - 1), column)
    )
    return pl.pallas_call(
        functools.partial(partial_gradients, count, per),
        grid=(model // tile,),
        in_specs=[columns] * 2
        + [whole(a) for a in right]
        + [pl.BlockSpec(memory_space=pl.ANY)] * len(into),
        out_specs=[out_spec(k) for k in range(count)],
        out_shape=[shape_of((block_rows, width), jnp.bfloat16)] * count,
        input_output_aliases={4 + k: k for k in range(len(into))},
        compiler_params=pltpu.CompilerParams(vmem_limit_bytes=vmem_limit),
        cost_estimate=pl.CostEstimate(
            flops=2 * tokens * model * 128, bytes_accessed=tokens * model // 2, transcendentals=0
        ),
    )(*left, *right, *into)


def transposed_product(parts, count, *refs):
    lefts = refs[: 2 * parts]
    blocks = refs[2 * parts : 2 * parts + parts * count]
    outs = refs[2 * parts + parts * count :]
    tile = lefts[0].shape[0]
    rows = blocks[0].shape[0]
    for k in range(count):
        total = None
        span = slice(k * rows, (k + 1) * rows)
        for p in range(parts):
            left = jnp.concatenate([lefts[2 * p][...], lefts[2 * p + 1][...]], axis=0)
            more = dot_nt(left, blocks[p * count + k][...])
            total = more if total is None else total + more
        total = total.astype(jnp.bfloat16)
        outs[0][:, span] = total[:tile]
        outs[1][:, span] = total[tile:]


def run_transposed_product(pairs, blocks, column, columns):
    count = len(blocks[0])
    tokens = pairs[0][0].shape[0]
    model = count * blocks[0][0].shape[0]
    tile = min(256, tokens)
    rows = lambda n: pl.BlockSpec((tile, n), lambda i: (i, 0))
    lefts = [a for pair in pairs for a in pair]
    flat = [b for one in blocks for b in one]
    return kernel_call(
        functools.partial(transposed_product, len(pairs), count),
        (tokens // tile,),
        [rows(a.shape[1]) for a in lefts]
        + [pl.BlockSpec((b.shape[0], columns), lambda i: (0, column)) for b in flat],
        [rows(model)] * 2,
        [shape_of((tokens, model), jnp.bfloat16)] * 2,
        2 * tokens * model * 256,
        tokens * model,
    )(*lefts, *flat)


def add_three(first, second, third, out):
    total = first[...].astype(jnp.float32) + second[...].astype(jnp.float32)
    out[...] = (total + third[...].astype(jnp.float32)).astype(jnp.bfloat16)


def add_swapped(odd_ref, one, two, first, second, out_first, out_second):
    odd = odd_ref[...] == 1
    for left, right, got, out in ((one, two, first, out_first), (two, one, second, out_second)):
        here = jnp.where(odd, right[...].astype(jnp.float32), left[...].astype(jnp.float32))
        out[...] = (here + got[...].astype(jnp.float32)).astype(jnp.bfloat16)


def run_add(body, arrays, outs, flag=None):
    rows, width = arrays[0].shape
    tile = min(256, rows)
    spec = pl.BlockSpec((tile, width), lambda i: (i, 0))
    flags = [] if flag is None else [flag]
    return kernel_call(
        body,
        (rows // tile,),
        [whole(f) for f in flags] + [spec] * len(arrays),
        [spec] * outs,
        [shape_of((rows, width), jnp.bfloat16)] * outs,
        1,
        12 * rows * width,
    )(*flags, *arrays)


def place_columns(subs, place_ref, *refs):
    ins, outs = refs[: group * subs], refs[group * subs :]
    place = place_ref[0]
    rows = ins[0].shape[0]
    width = ins[0].shape[1] // len(outs)
    for s in range(subs):
        for r, ref in enumerate(ins[group * s : group * (s + 1)]):
            start = ref.shape[0] - rows if r == group - 1 else 0
            column = pl.multiple_of((s * group + (place ^ r)) * width, width)
            for m, out in enumerate(outs):
                piece = ref[start : start + rows, m * width : (m + 1) * width]
                out[:, pl.ds(column, width)] = piece.astype(jnp.float32)


def run_place_columns(place, parts, count):
    rows, width = parts[0][0].shape
    flat = [a for part in parts for a in part]
    full = lambda a: pl.BlockSpec(a.shape, lambda i, place: (0, 0))
    shape = shape_of((rows, width // count * group * len(parts)), jnp.float32)
    return pl.pallas_call(
        functools.partial(place_columns, len(parts)),
        grid_spec=pltpu.PrefetchScalarGridSpec(
            num_scalar_prefetch=1,
            grid=(1,),
            in_specs=[full(a) for a in flat],
            out_specs=[full(shape)] * count,
        ),
        out_shape=[shape] * count,
        compiler_params=pltpu.CompilerParams(vmem_limit_bytes=vmem_limit),
    )(place.reshape(1).astype(jnp.int32), *flat)


def place_halves(place, mine, other, out):
    half = mine.shape[0]
    core = place[0]
    out[pl.ds(core * half, half), :] = mine[...]
    out[pl.ds((1 - core) * half, half), :] = other[...]


def run_place_halves(core, spot, count, mine, other):
    half, model = mine.shape
    block = model // count
    source = pl.BlockSpec((half, block), lambda k, place: (0, k))
    return pl.pallas_call(
        place_halves,
        grid_spec=pltpu.PrefetchScalarGridSpec(
            num_scalar_prefetch=1,
            grid=(count,),
            in_specs=[source, source],
            out_specs=pl.BlockSpec((2 * half, block), lambda k, place: (0, (k + place[1]) % count)),
        ),
        out_shape=shape_of((2 * half, model), jnp.float32),
        compiler_params=pltpu.CompilerParams(vmem_limit_bytes=vmem_limit),
        cost_estimate=pl.CostEstimate(flops=1, bytes_accessed=16 * half * model, transcendentals=0),
    )(jnp.stack([core, spot]).astype(jnp.int32), mine, other)


def swap_cores(values):
    return lax.ppermute(values, "tensor", [(0, 1), (1, 0)])


sides = ((0, 1), (1, 0), (2, 3), (3, 2))
middle = ((1, 2), (2, 1))
outward = ((2, 3), (1, 0))
inward = ((0, 1), (3, 2))


class Lines:
    def __init__(self, dp):
        self.dp = dp
        self.length = dp // group
        index = lax.axis_index("dp")
        self.place = index % group
        self.spot = index // group

    def flip(self, values, relation):
        return lax.ppermute(values, "dp", [(i, i ^ relation) for i in range(self.dp)])

    def ends(self, values, moves):
        pairs = [
            (one * group + place, two * group + place)
            for one, two in moves
            for place in range(group)
        ]
        return lax.ppermute(values, "dp", pairs)

    def turn(self, values, step):
        pairs = [
            (spot * group + place, ((spot + step) % self.length) * group + place)
            for spot in range(self.length)
            for place in range(group)
        ]
        return lax.ppermute(values, "dp", pairs)

    def by_place(self, related):
        odd = self.place % 2 == 1
        high = self.place // 2 == 1
        own, one, two, three = related
        pairs = (
            (jnp.where(odd, one, own), jnp.where(odd, own, one)),
            (jnp.where(odd, three, two), jnp.where(odd, two, three)),
        )
        return [
            jnp.where(high, pairs[1][0], pairs[0][0]),
            jnp.where(high, pairs[1][1], pairs[0][1]),
            jnp.where(high, pairs[0][0], pairs[1][0]),
            jnp.where(high, pairs[0][1], pairs[1][1]),
        ]

    def pieces(self, piece_of):
        return [piece_of(self.place ^ relation) for relation in range(group)]

    def flip_pieces(self, pieces):
        return [pieces[0]] + [self.flip(pieces[r], r) for r in range(1, group)]

    def flip_first(self, pieces):
        return self.flip(jnp.concatenate([pieces[1], pieces[3]]), 1)

    def flip_second(self, pieces, got):
        return self.flip(jnp.concatenate([pieces[2], got[got.shape[0] // 2 :]]), 2)

    def flipped(self, pieces, first, second):
        rows = pieces[0].shape[0]
        return [pieces[0], first[:rows], second[:rows], second[rows:]]

    def row_pieces(self, total):
        rows = total.shape[0] // group
        return [
            lax.dynamic_slice_in_dim(total, (self.place ^ r) * rows, rows) for r in range(group)
        ]

    def gather_near(self, mine):
        return [self.flip(mine, 1), self.flip(mine, 2)]

    def gather_across(self, near):
        middle = near[0].shape[0] // 2
        return [self.flip(near[0][:middle], 2), self.flip(near[1][middle:], 1)]

    def scatter_across(self, across):
        middle = across.shape[0] // 2
        return [self.flip(across[:middle], 1), self.flip(across[middle:], 2)]

    def gather_far(self, mine):
        near = self.gather_near(mine)
        return near, self.gather_across(near)

    def gather_tokens(self, mine):
        return self.both_cores(mine, *self.gather_far(mine))

    def both_cores(self, mine, near, across):
        kept = jnp.concatenate([mine] + near + across)
        return kept, swap_cores(kept)

    def terms(self, kept, other, relation):
        rows = kept.shape[0] // group
        span = slice(relation * rows, (relation + 1) * rows)
        return kept[span].astype(jnp.float32) + other[span].astype(jnp.float32)

    def across_terms(self, kept, other):
        return self.scatter_across(self.terms(kept, other, 3).astype(jnp.bfloat16))

    def near_sends(self, kept, other, got):
        one, two = self.terms(kept, other, 1), self.terms(kept, other, 2)
        middle = one.shape[0] // 2
        one = jnp.concatenate([one[:middle], one[middle:] + got[1].astype(jnp.float32)])
        two = jnp.concatenate([two[:middle] + got[0].astype(jnp.float32), two[middle:]])
        return [one.astype(jnp.bfloat16), two.astype(jnp.bfloat16)]

    def near_flips(self, kept, other, got):
        one, two = self.near_sends(kept, other, got)
        return [self.flip(one, 1), self.flip(two, 2)]

    def near_sum(self, kept, other, near):
        one, two = near
        return self.terms(kept, other, 0) + one.astype(jnp.float32) + two.astype(jnp.float32)

    def near_terms(self, kept, other, got):
        return self.near_sum(kept, other, self.near_flips(kept, other, got))

    def scatter_tokens(self, kept, other):
        return self.near_terms(kept, other, self.across_terms(kept, other))


class LineGather:
    def __init__(self, lines, block):
        self.lines, self.block, self.got = lines, block, []

    def hop(self):
        lines, step = self.lines, len(self.got) + 1
        if lines.length != 4:
            turns = range(1, lines.length) if step == 1 else ()
            self.got.append([lines.turn(self.block, -k) for k in turns])
        elif step == 1:
            self.got.append([lines.ends(self.block, sides), lines.ends(self.block, middle)])
        elif step == 2:
            outer, inner = self.got[0]
            self.got.append([lines.ends(outer, middle), lines.ends(inner, outward)])
        else:
            self.got.append([lines.ends(self.got[1][0], outward)])

    def blocks(self):
        lines = self.lines
        if lines.length != 4:
            return [self.block] + self.got[0]
        (outer, inner), (inner_two, outer_two), (outer_three,) = self.got
        spot = lines.spot
        return [
            self.block,
            jnp.where(spot == 3, outer_three, jnp.where(spot == 1, inner, outer)),
            jnp.where((spot == 1) | (spot == 2), inner_two, outer_two),
            jnp.where(spot == 0, outer_three, jnp.where(spot == 2, inner, outer)),
        ]


class LineScatter:
    def __init__(self, lines, blocks):
        self.lines, self.blocks, self.got = lines, blocks, []

    def ready(self):
        step = len(self.got) + 1
        if self.lines.length != 4:
            return []
        if step == 1:
            return [self.blocks[3], self.blocks[1]]
        if step == 2:
            return run_add(add_three, [self.blocks[2], *self.got[0]], 1)
        odd = (self.lines.spot % 2).astype(jnp.int32).reshape(1, 1)
        return run_add(add_swapped, [self.blocks[1], self.blocks[3], *self.got[1]], 2, odd)

    def hop(self, ready=None):
        lines, step = self.lines, len(self.got) + 1
        if lines.length != 4:
            turns = range(1, lines.length) if step == 1 else ()
            self.got.append([lines.turn(self.blocks[k], k) for k in turns])
            return
        ready = self.ready() if ready is None else ready
        if step == 1:
            self.got.append([lines.ends(ready[0], ((0, 1),)), lines.ends(ready[1], ((3, 2),))])
        elif step == 2:
            self.got.append([lines.ends(ready[0], middle), lines.ends(ready[0], inward)])
        else:
            self.got.append([lines.ends(ready[0], sides), lines.ends(ready[1], middle)])

    def total(self):
        last = self.got[-1] if self.lines.length == 4 else self.got[0]
        result = self.blocks[0].astype(jnp.float32)
        for one in last:
            result = result + one.astype(jnp.float32)
        return result.astype(jnp.bfloat16)


def tie(*values):
    return lax.optimization_barrier(values)


def local(
    dp,
    tokens,
    segments,
    cotangent,
    attn_gain,
    ffn_gain,
    query_gain,
    key_gain,
    w_query,
    key_weight,
    value_weight,
    w_out,
    w_gate,
    w_up,
    w_down,
):
    lines = Lines(dp)
    core = lax.axis_index("tensor")
    length, width = tokens.shape
    half = length // 2
    head_dim = query_gain.shape[0]
    rows = w_query.shape[0]
    block_rows = rows * group
    query_width = w_query.shape[1] // group
    key_width = key_weight.shape[1] // group
    attn_width = query_width + 2 * key_width
    ff_sub = w_gate.shape[1] // group // sub_count

    def around(values):
        return jnp.roll(values, -lines.spot * block_rows, axis=-1)

    def back_around(values):
        return jnp.roll(values, lines.spot * block_rows, axis=-1)

    attn_gain_r, ffn_gain_r = around(attn_gain), around(ffn_gain)

    def columns(weight, start, size):
        return lax.dynamic_slice_in_dim(weight, start, size, axis=1)

    attn_pieces = lines.pieces(
        lambda j: jnp.concatenate(
            [
                columns(w_query, j * query_width, query_width),
                columns(key_weight, j * key_width, key_width),
                columns(value_weight, j * key_width, key_width),
                columns(w_out, j * query_width, query_width),
            ],
            axis=1,
        )
    )
    attn_shared = lines.flip_pieces(attn_pieces)
    source = around(lax.dynamic_slice_in_dim(tokens, core * half, half)).astype(jnp.float32)
    normed_f, scale_first = norm_rows(source, attn_gain_r)
    normed_mine = normed_f.astype(jnp.bfloat16)

    seg_near = jnp.concatenate([segments, lines.flip(segments, 1)])
    seg_second = lines.flip(seg_near, 2)
    attn_shared, normed_mine, seg_near, seg_second = tie(
        attn_shared, normed_mine, seg_near, seg_second
    )

    def ffn_piece(s):
        return lines.pieces(
            lambda j: jnp.concatenate(
                [
                    columns(weight, s * group * ff_sub + j * ff_sub, ff_sub)
                    for weight in (w_gate, w_up, w_down)
                ],
                axis=1,
            )
        )


    seg_all = jnp.concatenate([seg_near, seg_second])
    positions = jax.vmap(positions_of)(seg_all)
    index = jnp.arange(length, dtype=jnp.int32)
    cosine, sine = angles(positions, head_dim, 2 * head_dim)
    swapped = jnp.full((1, 1), core, jnp.int32)
    starts = index[None] - positions
    tables = (swapped, cosine, sine, starts[..., None], starts[:, None, :], index)
    gains_two = jnp.stack(
        [
            jnp.tile(query_gain, query_width // head_dim),
            jnp.tile(key_gain, query_width // head_dim),
        ]
    )

    attn_line = LineGather(lines, jnp.concatenate(lines.by_place(attn_shared), axis=0))
    attn_line.hop()
    near = lines.gather_near(normed_mine)
    mine_other = swap_cores(normed_mine)
    near, attn_line.got[0], tables, mine_other, w_gate, w_up, w_down = tie(
        near, attn_line.got[0], tables, mine_other, w_gate, w_up, w_down
    )
    attn_line.hop()
    across = lines.gather_across(near)
    pieces_0 = ffn_piece(0)
    near_other = swap_cores(near[0])
    near_other, near_two = tie(near_other, near[1])
    near = [near[0], near_two]
    near_other = [near_other, swap_cores(near_two)]
    across, attn_line.got[1], pieces_0, near_other, w_gate, w_up, w_down, cotangent = tie(
        across, attn_line.got[1], pieces_0, near_other, w_gate, w_up, w_down, cotangent
    )
    attn_line.hop()
    pieces_1 = ffn_piece(1)
    cot_half = around(lax.dynamic_slice_in_dim(cotangent, core * half, half))
    out_mine = cot_half.astype(jnp.bfloat16)
    across = jnp.concatenate(across)
    normed = (
        jnp.concatenate([normed_mine] + near + [across]),
        jnp.concatenate([mine_other] + near_other + [swap_cores(across)]),
    )
    shared_0 = lines.flip_pieces(pieces_0)
    normed, attn_line.got[2], shared_0, pieces_1, out_mine = tie(
        normed, attn_line.got[2], shared_0, pieces_1, out_mine
    )
    attn_w = attn_line.blocks()

    line_0 = LineGather(lines, jnp.concatenate(lines.by_place(shared_0), axis=0))
    line_0.hop()
    out_near = lines.gather_near(out_mine)
    qkv_raw, heads_out, attended_kept, attended_other = run_attention(
        True, normed, attn_w, tables, gains_two, head_dim, query_width, attn_width
    )
    attended_other, line_0.got[0], out_near, pieces_1 = tie(
        attended_other, line_0.got[0], out_near, pieces_1
    )

    line_0.hop()
    attended_other = swap_cores(attended_other)
    middle = half // 2
    out_first = lines.flip(out_near[0][:middle], 2)
    attended_other, out_first = tie(attended_other, out_first)
    first_1 = lines.flip_first(pieces_1)
    got = lines.across_terms(attended_kept, attended_other)
    got, first_1, line_0.got[1] = tie(got, first_1, line_0.got[1])
    line_0.hop()
    second_1 = lines.flip_second(pieces_1, first_1)
    attended = lines.near_terms(attended_kept, attended_other, got)
    attended, out_near = tie(attended, out_near)
    out_second = lines.flip(out_near[1][middle:], 1)
    attended, line_0.got[2], out_first, out_second, second_1 = tie(
        attended, line_0.got[2], out_first, out_second, second_1
    )
    shared_1 = lines.flipped(pieces_1, first_1, second_1)
    block_1 = jnp.concatenate(lines.by_place(shared_1), axis=0)

    line_1 = LineGather(lines, block_1)
    out_b = lines.both_cores(out_mine, out_near, [out_first, out_second])
    line_1.hop()
    state = source + attended
    normed2_f, scale_second = norm_rows(state, ffn_gain_r)
    near, across = lines.gather_far(normed2_f.astype(jnp.bfloat16))
    ffn_w = [line_0.blocks()]
    near, across, line_1.got[0], out_b, ffn_w[0] = tie(
        near, across, line_1.got[0], out_b, ffn_w[0]
    )

    line_1.hop()
    normed2 = lines.both_cores(normed2_f.astype(jnp.bfloat16), near, across)
    units_0 = run_ffn_units(normed2, out_b, ffn_w[0], ff_sub)
    units_0, line_1.got[1] = tie(units_0, line_1.got[1])
    line_1.hop()
    ffn_g = run_weight_gradients(normed2, units_0[2:], out_b, units_0[:2], lines.length)
    terms_0 = run_transposed_product([units_0[2:]], [ffn_w[0]], 0, 2 * ff_sub)
    ffn_g, line_1.got[2], units_0, terms_0 = tie(ffn_g, line_1.got[2], units_0, terms_0)
    sum_0 = LineScatter(lines, ffn_g)
    ffn_w.append(line_1.blocks())

    sum_0.hop()
    units_1 = run_ffn_units(normed2, out_b, ffn_w[1], ff_sub, terms_0)
    kept, other = units_1[4:]
    kept, other, sum_0.got[0], units_1 = tie(kept, other, sum_0.got[0], units_1)

    sum_0.hop()
    other = swap_cores(other)
    send = lines.terms(kept, other, 3).astype(jnp.bfloat16)
    send, units_1 = tie(send, units_1)
    got = lines.scatter_across(send)
    branch_kept, branch_other = run_transposed_product(
        [units_0[:2], units_1[:2]], ffn_w, 2, ff_sub
    )
    ffn_g = run_partial_gradients(normed2, units_1[2:4], lines.length, 3 * ff_sub, 0)
    got, sum_0.got[1], ffn_g, branch_kept, branch_other, units_1 = tie(
        got, sum_0.got[1], ffn_g, branch_kept, branch_other, units_1
    )
    sum_0.hop()
    branch_other = swap_cores(branch_other)
    near = lines.near_flips(kept, other, got)
    ffn_g = run_partial_gradients(out_b, units_1[:2], lines.length, 3 * ff_sub, 2, ffn_g)
    near, branch_kept, branch_other, ffn_g = tie(near, branch_kept, branch_other, ffn_g)
    sum_1 = LineScatter(lines, ffn_g)
    normed2_grad = lines.near_sum(kept, other, near)
    branch_got = lines.across_terms(branch_kept, branch_other)
    normed2_grad, sum_0.got[2], branch_got = tie(normed2_grad, sum_0.got[2], branch_got)

    sum_1.hop()
    ffn_gain_part = jnp.sum(normed2_grad * state * scale_second, axis=0)
    state_grad = cot_half + norm_back(state, scale_second, ffn_gain_r, normed2_grad)
    grad_mine = state_grad.astype(jnp.bfloat16)
    near, across = lines.gather_far(grad_mine)
    back_0 = lines.row_pieces(sum_0.total())
    branch_terms = lines.near_sends(branch_kept, branch_other, branch_got)
    ready = sum_1.ready()
    near, across, ready, back_0, branch_terms = tie(near, across, ready, back_0, branch_terms)

    sum_1.hop(ready)
    attended_b = lines.both_cores(grad_mine, near, across)

    branch = [lines.flip(branch_terms[0], 1), lines.flip(branch_terms[1], 2)]
    back_0_first = lines.flip_first(back_0)
    qkv_grad, gain_parts, kept, other, attn_gain_part = run_attention(
        False,
        attended_b,
        attn_w,
        tables,
        gains_two,
        head_dim,
        query_width,
        attn_width,
        qkv_raw,
        normed,
    )
    kept, other, qkv_grad, branch, sum_1.got[1], back_0, back_0_first = tie(
        kept, other, qkv_grad, branch, sum_1.got[1], back_0, back_0_first
    )

    sum_1.hop()
    gains = jnp.concatenate(
        [
            back_around(attn_gain_part[0] / attn_gain_r),
            back_around(ffn_gain_part),
            jnp.sum(gain_parts[0].reshape(-1, head_dim), axis=0),
            gain_parts[1][:head_dim],
        ]
    )
    other = swap_cores(other)
    back_0_second = lines.flip_second(back_0, back_0_first)
    attn_sum = LineScatter(
        lines, run_weight_gradients(normed, qkv_grad, attended_b, heads_out, lines.length)
    )
    other, attn_sum.blocks = tie(other, attn_sum.blocks)
    got = lines.across_terms(kept, other)
    got, sum_1.got[2], back_0_second, branch = tie(got, sum_1.got[2], back_0_second, branch)
    attn_sum.hop()
    mixed = state + lines.near_sum(branch_kept, branch_other, branch)
    mixed_other = swap_cores(mixed)
    back_1 = lines.row_pieces(sum_1.total())
    near = lines.near_flips(kept, other, got)
    attn_sum.hop()
    near, attn_sum.got[1], back_1, mixed, mixed_other = tie(
        near, attn_sum.got[1], back_1, mixed, mixed_other
    )
    ready = attn_sum.ready()
    near, ready = tie(near, ready)
    attn_sum.hop(ready)
    back_1 = lines.flip_pieces(back_1)
    normed_grad = lines.near_sum(kept, other, near)
    input_grad = state_grad + norm_back(source, scale_first, attn_gain_r, normed_grad)
    mixed = run_place_halves(core, lines.spot, lines.length, mixed, mixed_other)
    attn_sum.got[2], back_1, input_grad, gains, mixed = tie(
        attn_sum.got[2], back_1, input_grad, gains, mixed
    )
    gains_got = [lines.flip(gains, r) for r in range(1, group)]
    attn_send = lines.row_pieces(attn_sum.total())
    attn_grads = lines.flip_pieces(attn_send)
    input_other = swap_cores(input_grad)
    gains_got, input_other = tie(gains_got, input_other)
    gains = gains + gains_got[0] + gains_got[1] + gains_got[2]
    gains_got = [lines.turn(gains, k) for k in range(1, lines.length)]
    ffn_grads = run_place_columns(
        lines.place,
        [
            (back_0[0], back_0_first, back_0_second, back_0_second),
            back_1,
        ],
        3,
    )
    input_grad = run_place_halves(core, lines.spot, lines.length, input_grad, input_other)
    gains_got, attn_grads, input_grad = tie(gains_got, attn_grads, input_grad)
    for one in gains_got:
        gains = gains + one
    gains = gains + swap_cores(gains)

    def columns_of(related, start, stop):
        blocks = lines.by_place([b[:, start:stop] for b in related])
        return jnp.concatenate(blocks, axis=1).astype(jnp.float32)

    return (
        mixed,
        input_grad,
        gains[:width],
        gains[width : 2 * width],
        gains[2 * width : 2 * width + head_dim],
        gains[2 * width + head_dim :],
        columns_of(attn_grads, 0, query_width),
        columns_of(attn_grads, query_width, query_width + key_width),
        columns_of(attn_grads, query_width + key_width, attn_width),
        columns_of(attn_grads, attn_width, attn_width + query_width),
        *ffn_grads,
    )


def solution(mesh):
    dp = mesh.shape["dp"]
    weight = P("dp", "tensor")
    rows = P("dp", None)
    return jax.shard_map(
        lambda *arrays: local(dp, *arrays),
        mesh=mesh,
        in_specs=(rows, rows, rows, P(), P(), P(), P()) + (weight,) * 7,
        out_specs=(rows, rows, P(), P(), P(), P()) + (weight,) * 7,
        check_vma=False,
    )
```

```python
import functools

import jax
import jax.numpy as jnp
from jax import lax
from jax.experimental import pallas as pl
from jax.experimental.pallas import tpu as pltpu
from jax.sharding import PartitionSpec as P

eps = 1e-05
rope_base = 1000000.0
group = 4
sub_count = 2
mebibyte = 1024 * 1024
vmem_limit = 52 * mebibyte


def norm_rows(values, gain):
    scale = lax.rsqrt(jnp.mean(values * values, axis=-1, keepdims=True) + eps)
    return (values * scale * gain, scale)


def norm_back(values, scale, gain, incoming):
    weighted = incoming * gain
    return scale * weighted - values * (scale * scale * scale) * jnp.mean(
        weighted * values, axis=-1, keepdims=True
    )


def positions_of(segment_row):
    row_index = jnp.arange(segment_row.shape[0], dtype=jnp.int32)
    earlier = jnp.concatenate([segment_row[:1] - 1, segment_row[:-1]])
    starts = jnp.where(segment_row != earlier, row_index, jnp.zeros_like(row_index))
    return row_index - lax.cummax(starts, axis=0)


def angles(positions, width, lanes):
    frequency = rope_base ** (-jnp.arange(0, width, 2, dtype=jnp.float32) / width)
    frequency = jnp.tile(frequency, 2 * lanes // width)
    phases = positions.astype(jnp.float32)[..., None] * frequency
    return (jnp.cos(phases), jnp.sin(phases))


def dot_nn(left, right):
    return jnp.dot(left, right, preferred_element_type=jnp.float32)


def dot_nt(left, right):
    return lax.dot_general(
        left, right, (((1,), (1,)), ((), ())), preferred_element_type=jnp.float32
    )


def dot_tn(left, right):
    return lax.dot_general(
        left, right, (((0,), (0,)), ((), ())), preferred_element_type=jnp.float32
    )


def pick_dot(left, right):
    high = left.astype(jnp.bfloat16)
    low = (left - high.astype(jnp.float32)).astype(jnp.bfloat16)
    return dot_nn(high, right) + dot_nn(low, right)


def kernel_call(body, grid, in_specs, out_specs, out_shape, flops, moved, room=vmem_limit):
    return pl.pallas_call(
        body,
        grid=grid,
        in_specs=in_specs,
        out_specs=out_specs,
        out_shape=out_shape,
        compiler_params=pltpu.CompilerParams(vmem_limit_bytes=room),
        cost_estimate=pl.CostEstimate(flops=flops, bytes_accessed=moved, transcendentals=0),
    )


def whole(array):
    rank = len(array.shape)
    return pl.BlockSpec(array.shape, lambda *_: (0,) * rank)


def shape_of(shape, kind):
    return jax.ShapeDtypeStruct(shape, kind)


def turn_heads(values, head_dim):
    lanes = values.shape[-1]
    middle = head_dim // 2
    lane = lax.broadcasted_iota(jnp.int32, values.shape, 1) % head_dim
    ahead = pltpu.roll(values, lanes - middle, 1)
    behind = pltpu.roll(values, middle, 1)
    return jnp.where(lane < middle, -ahead, behind)


def index_pair(rows, columns):
    return (
        lax.broadcasted_iota(jnp.int32, (rows, columns), 0),
        lax.broadcasted_iota(jnp.int32, (rows, columns), 1),
    )


def ones_where(condition):
    return condition.astype(jnp.float32).astype(jnp.bfloat16)


def spread_of(rows, offset, columns, head_dim):
    row, column = index_pair(rows, columns)
    return ones_where(row - offset == column % head_dim)


def fold(values, head_dim):
    row, column = index_pair(values.shape[1], values.shape[1])
    return pick_dot(values, ones_where(row % head_dim == column % head_dim))


def head_mean(values, head_dim):
    row, column = index_pair(values.shape[1], values.shape[1])
    return pick_dot(values, ones_where(row // head_dim == column // head_dim)) * (1.0 / head_dim)


def prepare_heads(raw, gain, cosine, sine, head_dim):
    scale = lax.rsqrt(head_mean(raw * raw, head_dim) + eps)
    scaled = raw * scale * gain
    return scaled * cosine + turn_heads(scaled, head_dim) * sine, scale


def prepare_back(raw, scale, gain, cosine, sine, incoming, head_dim):
    turned = incoming * cosine - turn_heads(incoming * sine, head_dim)
    weighted = turned * gain
    grad = scale * weighted - raw * (scale * scale * scale) * head_mean(weighted * raw, head_dim)
    return grad, jnp.sum(turned * raw * scale, axis=0, keepdims=True)


def head_inputs(raw, gains, cosine, sine, head_dim, width):
    query, query_scale = prepare_heads(raw[:, :width], gains[0:1], cosine, sine, head_dim)
    rest = raw[:, width:]
    key_raw = pick_dot(rest, spread_of(rest.shape[1], 0, width, head_dim))
    key, key_scale = prepare_heads(key_raw, gains[1:2], cosine, sine, head_dim)
    value = dot_nn(
        rest.astype(jnp.bfloat16), spread_of(rest.shape[1], head_dim, width, head_dim)
    ).astype(jnp.bfloat16)
    return (
        query.astype(jnp.bfloat16) * jnp.bfloat16(0.125),
        query_scale,
        key_raw,
        key.astype(jnp.bfloat16),
        key_scale,
        value,
    )


def only_head(values, head, head_dim):
    lane = lax.broadcasted_iota(jnp.int32, values.shape, 1)
    return jnp.where(lane // head_dim == head, values, jnp.zeros_like(values))


def exps_of(scores, allowed):
    return jnp.exp(jnp.where(allowed, scores, -1000000000.0))


def block_product(kept, other, blocks, start, stop):
    rows = blocks[0].shape[0]
    total = None
    for k, block in enumerate(blocks):
        left = jnp.concatenate(
            [kept[:, k * rows : (k + 1) * rows], other[:, k * rows : (k + 1) * rows]], axis=0
        )
        more = dot_nn(left, block[:, start:stop])
        total = more if total is None else total + more
    return total


def by_halves(swapped, one, two):
    return jnp.where(swapped, two, one), jnp.where(swapped, one, two)


def head_tables(cosine_ref, sine_ref, width):
    repeat = width // cosine_ref.shape[-1]
    return (
        jnp.concatenate([cosine_ref[0]] * repeat, axis=1),
        jnp.concatenate([sine_ref[0]] * repeat, axis=1),
    )


def attention_forward(count, head_dim, width, *refs):
    kept, other = refs[:2]
    refs = refs[2:]
    swap_ref, cosine_ref, sine_ref, start_ref, index_column, index_row, gains = refs[:7]
    blocks = refs[7 : 7 + count]
    raw_ref, heads_kept, heads_other, part_kept, part_other = refs[7 + count :]
    half = kept.shape[0]
    attn_width = raw_ref.shape[-1]
    raw = block_product(kept, other, blocks, 0, attn_width)
    swapped = swap_ref[...] == 1
    raw = jnp.concatenate(by_halves(swapped, raw[:half], raw[half:]), axis=0)
    raw_ref[0] = raw
    cosine, sine = head_tables(cosine_ref, sine_ref, width)
    query, _, _, key, _, value = head_inputs(raw, gains[...], cosine, sine, head_dim, width)
    allowed = (index_row[...] <= index_column[...]) & (index_row[...] >= start_ref[0])
    one = jnp.zeros((half, width), jnp.float32)
    two = one
    for head in range(width // head_dim):
        query_h = only_head(query, head, head_dim)
        for first in (True, False):
            span, keys = (slice(0, half), half) if first else (slice(half, 2 * half), 2 * half)
            exps = exps_of(dot_nt(query_h[span], key[:keys]), allowed[span, :keys])
            part = dot_nn(exps.astype(jnp.bfloat16), value[:keys])
            part = part * (1.0 / jnp.sum(exps, axis=-1, keepdims=True))
            part = only_head(part, head, head_dim)
            if first:
                one = one + part
            else:
                two = two + part
    heads = by_halves(swapped, one.astype(jnp.bfloat16), two.astype(jnp.bfloat16))
    heads_kept[...] = heads[0]
    heads_other[...] = heads[1]
    heads = jnp.concatenate(heads, axis=0)
    rows = blocks[0].shape[0]
    for k, block in enumerate(blocks):
        out = dot_nt(heads, block[:, attn_width : attn_width + width]).astype(jnp.bfloat16)
        part_kept[:, k * rows : (k + 1) * rows] = out[:half]
        part_other[:, k * rows : (k + 1) * rows] = out[half:]


def attention_backward(count, head_dim, width, *refs):
    kept, other, raw_ref, normed_kept, normed_other = refs[:5]
    refs = refs[5:]
    swap_ref, cosine_ref, sine_ref, start_ref, index_column, index_row, gains = refs[:7]
    blocks = refs[7 : 7 + count]
    grad_kept, grad_other, gain_ref, part_kept, part_other, scaled_ref = refs[7 + count :]
    half = kept.shape[0]
    attn_width = raw_ref.shape[-1]
    grads = block_product(kept, other, blocks, attn_width, attn_width + width)
    grads = grads.astype(jnp.bfloat16)
    swapped = swap_ref[...] == 1
    grads = jnp.concatenate(by_halves(swapped, grads[:half], grads[half:]), axis=0)
    raw = raw_ref[0]
    cosine, sine = head_tables(cosine_ref, sine_ref, width)
    query, query_scale, key_raw, key, key_scale, value = head_inputs(
        raw, gains[...], cosine, sine, head_dim, width
    )
    allowed = (index_column[...] <= index_row[...]) & (index_column[...] >= start_ref[0])
    zero = jnp.zeros((half, width), jnp.float32)
    query_grads, key_grads, value_grads = [zero, zero], [zero, zero], [zero, zero]
    for head in range(width // head_dim):
        query_h = only_head(query, head, head_dim)
        grad_h = only_head(grads, head, head_dim)
        for part in range(2):
            span, keys = slice(part * half, (part + 1) * half), (part + 1) * half
            exps = exps_of(dot_nt(key[:keys], query_h[span]), allowed[:keys, span])
            probs_f = exps * (1.0 / jnp.sum(exps, axis=0, keepdims=True))
            weighted = probs_f * dot_nt(value[:keys], grad_h[span])
            score_grad = weighted - probs_f * jnp.sum(weighted, axis=0, keepdims=True)
            score_grad = score_grad.astype(jnp.bfloat16)
            query_grads[part] += only_head(dot_tn(score_grad, key[:keys]), head, head_dim)
            value_part = dot_nn(probs_f.astype(jnp.bfloat16), grad_h[span])
            key_part = dot_nn(score_grad, query_h[span])
            for block in range(part + 1):
                rows = slice(block * half, (block + 1) * half)
                value_grads[block] += value_part[rows]
                key_grads[block] += key_part[rows]
    query_grad = 0.125 * jnp.concatenate(query_grads, axis=0)
    key_grad = fold(jnp.concatenate(key_grads, axis=0), head_dim)
    value_grad = fold(jnp.concatenate(value_grads, axis=0), head_dim)
    query_grad, query_gain_part = prepare_back(
        raw[:, :width], query_scale, gains[0:1], cosine, sine, query_grad, head_dim
    )
    key_grad, key_gain_part = prepare_back(
        key_raw, key_scale, gains[1:2], cosine, sine, key_grad, head_dim
    )
    rest = attn_width - width
    lane = lax.broadcasted_iota(jnp.int32, (2 * half, rest), 1)
    rest_grad = jnp.where(lane < head_dim, key_grad[:, :rest], value_grad[:, :rest])
    query_grad = query_grad.astype(jnp.bfloat16)
    rest_grad = rest_grad.astype(jnp.bfloat16)
    query_sides = by_halves(swapped, query_grad[:half], query_grad[half:])
    rest_sides = by_halves(swapped, rest_grad[:half], rest_grad[half:])
    all_sides = []
    for side, out in enumerate((grad_kept, grad_other)):
        both = jnp.concatenate([query_sides[side], rest_sides[side]], axis=1)
        out[...] = both
        all_sides.append(both)
    all_sides = jnp.concatenate(all_sides, axis=0)
    parts = jnp.concatenate([query_gain_part, key_gain_part], axis=0)

    @pl.when(pl.program_id(0) == 0)
    def _():
        scaled_ref[...] = jnp.zeros_like(scaled_ref)

    rows = blocks[0].shape[0]
    for k, block in enumerate(blocks):
        span = slice(k * rows, (k + 1) * rows)
        out = dot_nt(all_sides, block[:, :attn_width])
        scaled = out[:half] * normed_kept[:, span].astype(jnp.float32)
        scaled = scaled + out[half:] * normed_other[:, span].astype(jnp.float32)
        scaled_ref[:, span] += jnp.sum(scaled, axis=0, keepdims=True)
        out = out.astype(jnp.bfloat16)
        part_kept[:, span] = out[:half]
        part_other[:, span] = out[half:]

    @pl.when(pl.program_id(0) == 0)
    def _():
        gain_ref[...] = parts

    @pl.when(pl.program_id(0) != 0)
    def _():
        gain_ref[...] = gain_ref[...] + parts


def run_attention(forward, pair, blocks, tables, gains, head_dim, width, attn_width, raw=None, normed=None):
    half = pair[0].shape[0] // group
    model = pair[0].shape[1]
    swapped, cosine, sine, start_columns, start_rows, index = tables
    starts = start_columns if forward else start_rows
    rows = lambda n: pl.BlockSpec((half, n), lambda s: (s, 0))
    per_sequence = lambda shape: pl.BlockSpec((1,) + shape[1:], lambda s: (s, 0, 0))
    column, row = index[:, None], index[None, :]
    common = [swapped, cosine, sine, starts, column, row, gains]
    common_specs = [whole(swapped)] + [per_sequence(a.shape) for a in (cosine, sine, starts)]
    common_specs += [whole(column), whole(row), whole(gains)]
    common += blocks
    common_specs += [whole(b) for b in blocks]
    raw_shape = (group, 2 * half, attn_width)
    flops = 2 * 2 * group * half * model * attn_width * 10
    moved = 16 * group * half * model
    side = lambda n: shape_of((group * half, n), jnp.bfloat16)
    if forward:
        results = kernel_call(
            functools.partial(attention_forward, len(blocks), head_dim, width),
            (group,),
            [rows(model)] * 2 + common_specs,
            [per_sequence(raw_shape), rows(width), rows(width), rows(model), rows(model)],
            [shape_of(raw_shape, jnp.float32), side(width), side(width), side(model), side(model)],
            flops,
            moved,
        )(*pair, *common)
        return results[0], tuple(results[1:3]), results[3], results[4]
    results = kernel_call(
        functools.partial(attention_backward, len(blocks), head_dim, width),
        (group,),
        [rows(model)] * 2 + [per_sequence(raw_shape)] + [rows(model)] * 2 + common_specs,
        [rows(attn_width), rows(attn_width), pl.BlockSpec((2, width), lambda s: (0, 0))]
        + [rows(model)] * 2
        + [pl.BlockSpec((1, model), lambda s: (0, 0))],
        [side(attn_width), side(attn_width), shape_of((2, width), jnp.float32)]
        + [side(model)] * 2
        + [shape_of((1, model), jnp.float32)],
        flops,
        moved,
    )(*pair, raw, *normed, *common)
    return tuple(results[:2]), *results[2:]


def ffn_units(count, ff_sub, earlier, *refs):
    normed, out = refs[0:2], refs[2:4]
    blocks, refs = refs[4 : 4 + count], refs[4 + count :]
    if earlier:
        before, refs = refs[0:2], refs[2:]
    inner_refs, grad_refs, terms = refs[0:2], refs[2:4], refs[4:6]
    tile = normed[0].shape[0]
    gate_up = block_product(normed[0], normed[1], blocks, 0, 2 * ff_sub)
    inner_grad = block_product(out[0], out[1], blocks, 2 * ff_sub, 3 * ff_sub)
    gate, up = gate_up[:, :ff_sub], gate_up[:, ff_sub:]
    sigmoid = 1.0 / (1.0 + jnp.exp(-gate))
    silu = gate * sigmoid
    inner = (silu * up).astype(jnp.bfloat16)
    gate_grad = (inner_grad * up * sigmoid * (1.0 + gate * (1.0 - sigmoid))).astype(jnp.bfloat16)
    up_grad = (inner_grad * silu).astype(jnp.bfloat16)
    for side in range(2):
        rows = slice(side * tile, (side + 1) * tile)
        inner_refs[side][...] = inner[rows]
        grad_refs[side][:, :ff_sub] = gate_grad[rows]
        grad_refs[side][:, ff_sub:] = up_grad[rows]
    if not earlier:
        return
    here = jnp.concatenate([gate_grad, up_grad], axis=1)
    rows = blocks[0].shape[0]
    for k in range(count):
        span = slice(k * rows, (k + 1) * rows)
        total = dot_nt(here, blocks[k][:, : 2 * ff_sub])
        for side in range(2):
            part = total[side * tile : (side + 1) * tile]
            part = part + before[side][:, span].astype(jnp.float32)
            terms[side][:, span] = part.astype(jnp.bfloat16)


def run_ffn_units(normed, out, blocks, ff_sub, before=None):
    tokens, model = normed[0].shape
    tile = min(256, tokens)
    rows = lambda n: pl.BlockSpec((tile, n), lambda i: (i, 0))
    earlier = before is not None
    shapes = [ff_sub] * 2 + [2 * ff_sub] * 2 + [model] * 2 * earlier
    return kernel_call(
        functools.partial(ffn_units, len(blocks), ff_sub, earlier),
        (tokens // tile,),
        [rows(model)] * 4
        + [whole(b) for b in blocks]
        + [rows(model)] * 2 * earlier,
        [rows(n) for n in shapes],
        [shape_of((tokens, n), jnp.bfloat16) for n in shapes],
        12 * tokens * model * ff_sub,
        8 * tokens * model,
    )(*normed, *out, *blocks, *(before if earlier else ()))


def weight_gradients(count, per, *refs):
    first, second = refs[0:2], refs[2:4]
    first_grad, second_grad = refs[4:6], refs[6:8]
    outs = refs[8:]
    one = dot_tn(first[0][...], first_grad[0][...]) + dot_tn(first[1][...], first_grad[1][...])
    two = dot_tn(second[0][...], second_grad[0][...]) + dot_tn(second[1][...], second_grad[1][...])
    width = one.shape[1]
    for k in range(count):

        @pl.when(pl.program_id(0) // per == k)
        def _(k=k):
            outs[k][:, :width] = one.astype(jnp.bfloat16)
            outs[k][:, width:] = two.astype(jnp.bfloat16)


def run_weight_gradients(first, first_grad, second, second_grad, count):
    tokens, model = first[0].shape
    block_rows = model // count
    tile = min(256, block_rows)
    per = block_rows // tile
    width = first_grad[0].shape[1] + second_grad[0].shape[1]
    columns = pl.BlockSpec((tokens, tile), lambda i: (0, i))
    out_spec = lambda k: pl.BlockSpec(
        (tile, width), lambda i: (jnp.clip(i - per * k, 0, per - 1), 0)
    )
    return kernel_call(
        functools.partial(weight_gradients, count, per),
        (model // tile,),
        [columns] * 4 + [whole(a) for a in (*first_grad, *second_grad)],
        [out_spec(k) for k in range(count)],
        [shape_of((block_rows, width), jnp.bfloat16)] * count,
        2 * tokens * model * 256,
        tokens * model,
        vmem_limit,
    )(*first, *second, *first_grad, *second_grad)


def partial_gradients(count, per, *refs):
    left, right, outs = refs[0:2], refs[2:4], refs[-count:]
    product = dot_tn(left[0][...], right[0][...]) + dot_tn(left[1][...], right[1][...])
    product = product.astype(jnp.bfloat16)
    for k in range(count):

        @pl.when(pl.program_id(0) // per == k)
        def _(k=k):
            outs[k][...] = product


def run_partial_gradients(left, right, count, width, column, into=()):
    tokens, model = left[0].shape
    block_rows = model // count
    tile = min(256, block_rows)
    per = block_rows // tile
    columns = pl.BlockSpec((tokens, tile), lambda i: (0, i))
    part = right[0].shape[1]
    out_spec = lambda k: pl.BlockSpec(
        (tile, part), lambda i: (jnp.clip(i - per * k, 0, per - 1), column)
    )
    return pl.pallas_call(
        functools.partial(partial_gradients, count, per),
        grid=(model // tile,),
        in_specs=[columns] * 2
        + [whole(a) for a in right]
        + [pl.BlockSpec(memory_space=pl.ANY)] * len(into),
        out_specs=[out_spec(k) for k in range(count)],
        out_shape=[shape_of((block_rows, width), jnp.bfloat16)] * count,
        input_output_aliases={4 + k: k for k in range(len(into))},
        compiler_params=pltpu.CompilerParams(vmem_limit_bytes=vmem_limit),
        cost_estimate=pl.CostEstimate(
            flops=2 * tokens * model * 128, bytes_accessed=tokens * model // 2, transcendentals=0
        ),
    )(*left, *right, *into)


def transposed_product(parts, count, *refs):
    lefts = refs[: 2 * parts]
    blocks = refs[2 * parts : 2 * parts + parts * count]
    outs = refs[2 * parts + parts * count :]
    tile = lefts[0].shape[0]
    rows = blocks[0].shape[0]
    for k in range(count):
        total = None
        span = slice(k * rows, (k + 1) * rows)
        for p in range(parts):
            left = jnp.concatenate([lefts[2 * p][...], lefts[2 * p + 1][...]], axis=0)
            more = dot_nt(left, blocks[p * count + k][...])
            total = more if total is None else total + more
        total = total.astype(jnp.bfloat16)
        outs[0][:, span] = total[:tile]
        outs[1][:, span] = total[tile:]


def run_transposed_product(pairs, blocks, column, columns):
    count = len(blocks[0])
    tokens = pairs[0][0].shape[0]
    model = count * blocks[0][0].shape[0]
    tile = min(256, tokens)
    rows = lambda n: pl.BlockSpec((tile, n), lambda i: (i, 0))
    lefts = [a for pair in pairs for a in pair]
    flat = [b for one in blocks for b in one]
    return kernel_call(
        functools.partial(transposed_product, len(pairs), count),
        (tokens // tile,),
        [rows(a.shape[1]) for a in lefts]
        + [pl.BlockSpec((b.shape[0], columns), lambda i: (0, column)) for b in flat],
        [rows(model)] * 2,
        [shape_of((tokens, model), jnp.bfloat16)] * 2,
        2 * tokens * model * 256,
        tokens * model,
        vmem_limit,
    )(*lefts, *flat)


def add_three(first, second, third, out):
    total = first[...].astype(jnp.float32) + second[...].astype(jnp.float32)
    out[...] = (total + third[...].astype(jnp.float32)).astype(jnp.bfloat16)


def add_swapped(odd_ref, one, two, first, second, out_first, out_second):
    odd = odd_ref[...] == 1
    for left, right, got, out in ((one, two, first, out_first), (two, one, second, out_second)):
        here = jnp.where(odd, right[...].astype(jnp.float32), left[...].astype(jnp.float32))
        out[...] = (here + got[...].astype(jnp.float32)).astype(jnp.bfloat16)


def run_add(body, arrays, outs, flag=None):
    rows, width = arrays[0].shape
    tile = min(256, rows)
    spec = pl.BlockSpec((tile, width), lambda i: (i, 0))
    flags = [] if flag is None else [flag]
    return kernel_call(
        body,
        (rows // tile,),
        [whole(f) for f in flags] + [spec] * len(arrays),
        [spec] * outs,
        [shape_of((rows, width), jnp.bfloat16)] * outs,
        1,
        12 * rows * width,
        16 * mebibyte if rows * width > mebibyte // 2 else vmem_limit,
    )(*flags, *arrays)


def place_columns(subs, place_ref, *refs):
    ins, outs = refs[: group * subs], refs[group * subs :]
    place = place_ref[0]
    rows = ins[0].shape[0]
    width = ins[0].shape[1] // len(outs)
    for s in range(subs):
        for r, ref in enumerate(ins[group * s : group * (s + 1)]):
            start = ref.shape[0] - rows if r == group - 1 else 0
            column = pl.multiple_of((s * group + (place ^ r)) * width, width)
            for m, out in enumerate(outs):
                piece = ref[start : start + rows, m * width : (m + 1) * width]
                out[:, pl.ds(column, width)] = piece.astype(jnp.float32)


def run_place_columns(place, parts, count):
    rows, width = parts[0][0].shape
    flat = [a for part in parts for a in part]
    full = lambda a: pl.BlockSpec(a.shape, lambda i, place: (0, 0))
    shape = shape_of((rows, width // count * group * len(parts)), jnp.float32)
    return pl.pallas_call(
        functools.partial(place_columns, len(parts)),
        grid_spec=pltpu.PrefetchScalarGridSpec(
            num_scalar_prefetch=1,
            grid=(1,),
            in_specs=[full(a) for a in flat],
            out_specs=[full(shape)] * count,
        ),
        out_shape=[shape] * count,
        compiler_params=pltpu.CompilerParams(vmem_limit_bytes=32 * mebibyte),
    )(place.reshape(1).astype(jnp.int32), *flat)


def place_halves(place, mine, other, out):
    half = mine.shape[0]
    core = place[0]
    out[pl.ds(core * half, half), :] = mine[...]
    out[pl.ds((1 - core) * half, half), :] = other[...]


def run_place_halves(core, spot, count, mine, other):
    half, model = mine.shape
    block = model // count
    source = pl.BlockSpec((half, block), lambda k, place: (0, k))
    return pl.pallas_call(
        place_halves,
        grid_spec=pltpu.PrefetchScalarGridSpec(
            num_scalar_prefetch=1,
            grid=(count,),
            in_specs=[source, source],
            out_specs=pl.BlockSpec((2 * half, block), lambda k, place: (0, (k + place[1]) % count)),
        ),
        out_shape=shape_of((2 * half, model), jnp.float32),
        compiler_params=pltpu.CompilerParams(vmem_limit_bytes=12 * mebibyte),
        cost_estimate=pl.CostEstimate(flops=1, bytes_accessed=16 * half * model, transcendentals=0),
    )(jnp.stack([core, spot]).astype(jnp.int32), mine, other)


def swap_cores(values):
    return lax.ppermute(values, "tensor", [(0, 1), (1, 0)])


sides = ((0, 1), (1, 0), (2, 3), (3, 2))
middle = ((1, 2), (2, 1))
outward = ((2, 3), (1, 0))
inward = ((0, 1), (3, 2))


class Lines:
    def __init__(self, dp):
        self.dp = dp
        self.length = dp // group
        index = lax.axis_index("dp")
        self.place = index % group
        self.spot = index // group

    def flip(self, values, relation):
        return lax.ppermute(values, "dp", [(i, i ^ relation) for i in range(self.dp)])

    def ends(self, values, moves):
        pairs = [
            (one * group + place, two * group + place)
            for one, two in moves
            for place in range(group)
        ]
        return lax.ppermute(values, "dp", pairs)

    def turn(self, values, step):
        pairs = [
            (spot * group + place, ((spot + step) % self.length) * group + place)
            for spot in range(self.length)
            for place in range(group)
        ]
        return lax.ppermute(values, "dp", pairs)

    def by_place(self, related):
        odd = self.place % 2 == 1
        high = self.place // 2 == 1
        own, one, two, three = related
        pairs = (
            (jnp.where(odd, one, own), jnp.where(odd, own, one)),
            (jnp.where(odd, three, two), jnp.where(odd, two, three)),
        )
        return [
            jnp.where(high, pairs[1][0], pairs[0][0]),
            jnp.where(high, pairs[1][1], pairs[0][1]),
            jnp.where(high, pairs[0][0], pairs[1][0]),
            jnp.where(high, pairs[0][1], pairs[1][1]),
        ]

    def pieces(self, piece_of):
        return [piece_of(self.place ^ relation) for relation in range(group)]

    def flip_pieces(self, pieces):
        return [pieces[0]] + [self.flip(pieces[r], r) for r in range(1, group)]

    def flip_first(self, pieces):
        return self.flip(jnp.concatenate([pieces[1], pieces[3]]), 1)

    def flip_second(self, pieces, got):
        return self.flip(jnp.concatenate([pieces[2], got[got.shape[0] // 2 :]]), 2)

    def flipped(self, pieces, first, second):
        rows = pieces[0].shape[0]
        return [pieces[0], first[:rows], second[:rows], second[rows:]]

    def row_pieces(self, total):
        rows = total.shape[0] // group
        return [
            lax.dynamic_slice_in_dim(total, (self.place ^ r) * rows, rows) for r in range(group)
        ]

    def gather_near(self, mine):
        return [self.flip(mine, 1), self.flip(mine, 2)]

    def gather_across(self, near):
        middle = near[0].shape[0] // 2
        return [self.flip(near[0][:middle], 2), self.flip(near[1][middle:], 1)]

    def scatter_across(self, across):
        middle = across.shape[0] // 2
        return [self.flip(across[:middle], 1), self.flip(across[middle:], 2)]

    def gather_far(self, mine):
        near = self.gather_near(mine)
        return near, self.gather_across(near)

    def gather_tokens(self, mine):
        return self.both_cores(mine, *self.gather_far(mine))

    def both_cores(self, mine, near, across):
        kept = jnp.concatenate([mine] + near + across)
        return kept, swap_cores(kept)

    def terms(self, kept, other, relation):
        rows = kept.shape[0] // group
        span = slice(relation * rows, (relation + 1) * rows)
        return kept[span].astype(jnp.float32) + other[span].astype(jnp.float32)

    def across_terms(self, kept, other):
        return self.scatter_across(self.terms(kept, other, 3).astype(jnp.bfloat16))

    def near_sends(self, kept, other, got):
        one, two = self.terms(kept, other, 1), self.terms(kept, other, 2)
        middle = one.shape[0] // 2
        one = jnp.concatenate([one[:middle], one[middle:] + got[1].astype(jnp.float32)])
        two = jnp.concatenate([two[:middle] + got[0].astype(jnp.float32), two[middle:]])
        return [one.astype(jnp.bfloat16), two.astype(jnp.bfloat16)]

    def near_flips(self, kept, other, got):
        one, two = self.near_sends(kept, other, got)
        return [self.flip(one, 1), self.flip(two, 2)]

    def near_sum(self, kept, other, near):
        one, two = near
        return self.terms(kept, other, 0) + one.astype(jnp.float32) + two.astype(jnp.float32)

    def near_terms(self, kept, other, got):
        return self.near_sum(kept, other, self.near_flips(kept, other, got))

    def scatter_tokens(self, kept, other):
        return self.near_terms(kept, other, self.across_terms(kept, other))


class LineGather:
    def __init__(self, lines, block):
        self.lines, self.block, self.got = lines, block, []

    def hop(self):
        lines, step = self.lines, len(self.got) + 1
        if lines.length != 4:
            turns = range(1, lines.length) if step == 1 else ()
            self.got.append([lines.turn(self.block, -k) for k in turns])
        elif step == 1:
            self.got.append([lines.ends(self.block, sides), lines.ends(self.block, middle)])
        elif step == 2:
            outer, inner = self.got[0]
            self.got.append([lines.ends(outer, middle), lines.ends(inner, outward)])
        else:
            self.got.append([lines.ends(self.got[1][0], outward)])

    def blocks(self):
        lines = self.lines
        if lines.length != 4:
            return [self.block] + self.got[0]
        (outer, inner), (inner_two, outer_two), (outer_three,) = self.got
        spot = lines.spot
        return [
            self.block,
            jnp.where(spot == 3, outer_three, jnp.where(spot == 1, inner, outer)),
            jnp.where((spot == 1) | (spot == 2), inner_two, outer_two),
            jnp.where(spot == 0, outer_three, jnp.where(spot == 2, inner, outer)),
        ]


class LineScatter:
    def __init__(self, lines, blocks):
        self.lines, self.blocks, self.got = lines, blocks, []

    def ready(self):
        step = len(self.got) + 1
        if self.lines.length != 4:
            return []
        if step == 1:
            return [self.blocks[3], self.blocks[1]]
        if step == 2:
            return run_add(add_three, [self.blocks[2], *self.got[0]], 1)
        odd = (self.lines.spot % 2).astype(jnp.int32).reshape(1, 1)
        return run_add(add_swapped, [self.blocks[1], self.blocks[3], *self.got[1]], 2, odd)

    def hop(self, ready=None):
        lines, step = self.lines, len(self.got) + 1
        if lines.length != 4:
            turns = range(1, lines.length) if step == 1 else ()
            self.got.append([lines.turn(self.blocks[k], k) for k in turns])
            return
        ready = self.ready() if ready is None else ready
        if step == 1:
            self.got.append([lines.ends(ready[0], ((0, 1),)), lines.ends(ready[1], ((3, 2),))])
        elif step == 2:
            self.got.append([lines.ends(ready[0], middle), lines.ends(ready[0], inward)])
        else:
            self.got.append([lines.ends(ready[0], sides), lines.ends(ready[1], middle)])

    def total(self):
        last = self.got[-1] if self.lines.length == 4 else self.got[0]
        result = self.blocks[0].astype(jnp.float32)
        for one in last:
            result = result + one.astype(jnp.float32)
        return result.astype(jnp.bfloat16)


def tie(*values):
    return lax.optimization_barrier(values)


def local(
    dp,
    tokens,
    segments,
    cotangent,
    attn_gain,
    ffn_gain,
    query_gain,
    key_gain,
    w_query,
    key_weight,
    value_weight,
    w_out,
    w_gate,
    w_up,
    w_down,
):
    lines = Lines(dp)
    core = lax.axis_index("tensor")
    length, width = tokens.shape
    half = length // 2
    head_dim = query_gain.shape[0]
    rows = w_query.shape[0]
    block_rows = rows * group
    query_width = w_query.shape[1] // group
    key_width = key_weight.shape[1] // group
    attn_width = query_width + 2 * key_width
    ff_sub = w_gate.shape[1] // group // sub_count

    def around(values):
        return jnp.roll(values, -lines.spot * block_rows, axis=-1)

    def back_around(values):
        return jnp.roll(values, lines.spot * block_rows, axis=-1)

    attn_gain_r, ffn_gain_r = around(attn_gain), around(ffn_gain)

    def columns(weight, start, size):
        return lax.dynamic_slice_in_dim(weight, start, size, axis=1)

    attn_pieces = lines.pieces(
        lambda j: jnp.concatenate(
            [
                columns(w_query, j * query_width, query_width),
                columns(key_weight, j * key_width, key_width),
                columns(value_weight, j * key_width, key_width),
                columns(w_out, j * query_width, query_width),
            ],
            axis=1,
        )
    )
    attn_shared = lines.flip_pieces(attn_pieces)
    source = around(lax.dynamic_slice_in_dim(tokens, core * half, half)).astype(jnp.float32)
    normed_f, scale_first = norm_rows(source, attn_gain_r)
    normed_mine = normed_f.astype(jnp.bfloat16)

    seg_near = jnp.concatenate([segments, lines.flip(segments, 1)])
    seg_second = lines.flip(seg_near, 2)
    attn_shared, normed_mine, seg_near, seg_second = tie(
        attn_shared, normed_mine, seg_near, seg_second
    )

    def ffn_piece(s):
        return lines.pieces(
            lambda j: jnp.concatenate(
                [
                    columns(weight, s * group * ff_sub + j * ff_sub, ff_sub)
                    for weight in (w_gate, w_up, w_down)
                ],
                axis=1,
            )
        )


    seg_all = jnp.concatenate([seg_near, seg_second])
    positions = jax.vmap(positions_of)(seg_all)
    index = jnp.arange(length, dtype=jnp.int32)
    cosine, sine = angles(positions, head_dim, 2 * head_dim)
    swapped = jnp.full((1, 1), core, jnp.int32)
    starts = index[None] - positions
    tables = (swapped, cosine, sine, starts[..., None], starts[:, None, :], index)
    gains_two = jnp.stack(
        [
            jnp.tile(query_gain, query_width // head_dim),
            jnp.tile(key_gain, query_width // head_dim),
        ]
    )

    attn_line = LineGather(lines, jnp.concatenate(lines.by_place(attn_shared), axis=0))
    attn_line.hop()
    near = lines.gather_near(normed_mine)
    mine_other = swap_cores(normed_mine)
    near, attn_line.got[0], tables, mine_other, w_gate, w_up, w_down = tie(
        near, attn_line.got[0], tables, mine_other, w_gate, w_up, w_down
    )
    attn_line.hop()
    across = lines.gather_across(near)
    pieces_0 = ffn_piece(0)
    near_other = swap_cores(near[0])
    near_other, near_two = tie(near_other, near[1])
    near = [near[0], near_two]
    near_other = [near_other, swap_cores(near_two)]
    across, attn_line.got[1], pieces_0, near_other, w_gate, w_up, w_down, cotangent = tie(
        across, attn_line.got[1], pieces_0, near_other, w_gate, w_up, w_down, cotangent
    )
    attn_line.hop()
    pieces_1 = ffn_piece(1)
    cot_half = around(lax.dynamic_slice_in_dim(cotangent, core * half, half))
    out_mine = cot_half.astype(jnp.bfloat16)
    across = jnp.concatenate(across)
    normed = (
        jnp.concatenate([normed_mine] + near + [across]),
        jnp.concatenate([mine_other] + near_other + [swap_cores(across)]),
    )
    shared_0 = lines.flip_pieces(pieces_0)
    normed, attn_line.got[2], shared_0, pieces_1, out_mine = tie(
        normed, attn_line.got[2], shared_0, pieces_1, out_mine
    )
    attn_w = attn_line.blocks()

    line_0 = LineGather(lines, jnp.concatenate(lines.by_place(shared_0), axis=0))
    line_0.hop()
    out_near = lines.gather_near(out_mine)
    qkv_raw, heads_out, attended_kept, attended_other = run_attention(
        True, normed, attn_w, tables, gains_two, head_dim, query_width, attn_width
    )
    attended_other, line_0.got[0], out_near, pieces_1 = tie(
        attended_other, line_0.got[0], out_near, pieces_1
    )

    line_0.hop()
    attended_other = swap_cores(attended_other)
    middle = half // 2
    out_first = lines.flip(out_near[0][:middle], 2)
    attended_other, out_first = tie(attended_other, out_first)
    first_1 = lines.flip_first(pieces_1)
    got = lines.across_terms(attended_kept, attended_other)
    got, first_1, line_0.got[1] = tie(got, first_1, line_0.got[1])
    line_0.hop()
    second_1 = lines.flip_second(pieces_1, first_1)
    attended = lines.near_terms(attended_kept, attended_other, got)
    attended, out_near = tie(attended, out_near)
    out_second = lines.flip(out_near[1][middle:], 1)
    attended, line_0.got[2], out_first, out_second, second_1 = tie(
        attended, line_0.got[2], out_first, out_second, second_1
    )
    shared_1 = lines.flipped(pieces_1, first_1, second_1)
    block_1 = jnp.concatenate(lines.by_place(shared_1), axis=0)

    line_1 = LineGather(lines, block_1)
    out_b = lines.both_cores(out_mine, out_near, [out_first, out_second])
    line_1.hop()
    state = source + attended
    normed2_f, scale_second = norm_rows(state, ffn_gain_r)
    near, across = lines.gather_far(normed2_f.astype(jnp.bfloat16))
    ffn_w = [line_0.blocks()]
    near, across, line_1.got[0], out_b, ffn_w[0] = tie(
        near, across, line_1.got[0], out_b, ffn_w[0]
    )

    line_1.hop()
    normed2 = lines.both_cores(normed2_f.astype(jnp.bfloat16), near, across)
    units_0 = run_ffn_units(normed2, out_b, ffn_w[0], ff_sub)
    units_0, line_1.got[1] = tie(units_0, line_1.got[1])
    line_1.hop()
    ffn_g = run_weight_gradients(normed2, units_0[2:], out_b, units_0[:2], lines.length)
    terms_0 = run_transposed_product([units_0[2:]], [ffn_w[0]], 0, 2 * ff_sub)
    ffn_g, line_1.got[2], units_0, terms_0 = tie(ffn_g, line_1.got[2], units_0, terms_0)
    sum_0 = LineScatter(lines, ffn_g)
    ffn_w.append(line_1.blocks())

    sum_0.hop()
    units_1 = run_ffn_units(normed2, out_b, ffn_w[1], ff_sub, terms_0)
    kept, other = units_1[4:]
    kept, other, sum_0.got[0], units_1 = tie(kept, other, sum_0.got[0], units_1)

    sum_0.hop()
    other = swap_cores(other)
    send = lines.terms(kept, other, 3).astype(jnp.bfloat16)
    send, units_1 = tie(send, units_1)
    got = lines.scatter_across(send)
    branch_kept, branch_other = run_transposed_product(
        [units_0[:2], units_1[:2]], ffn_w, 2, ff_sub
    )
    ffn_g = run_partial_gradients(normed2, units_1[2:4], lines.length, 3 * ff_sub, 0)
    got, sum_0.got[1], ffn_g, branch_kept, branch_other, units_1 = tie(
        got, sum_0.got[1], ffn_g, branch_kept, branch_other, units_1
    )
    sum_0.hop()
    branch_other = swap_cores(branch_other)
    near = lines.near_flips(kept, other, got)
    ffn_g = run_partial_gradients(out_b, units_1[:2], lines.length, 3 * ff_sub, 2, ffn_g)
    near, branch_kept, branch_other, ffn_g = tie(near, branch_kept, branch_other, ffn_g)
    sum_1 = LineScatter(lines, ffn_g)
    normed2_grad = lines.near_sum(kept, other, near)
    branch_got = lines.across_terms(branch_kept, branch_other)
    normed2_grad, sum_0.got[2], branch_got = tie(normed2_grad, sum_0.got[2], branch_got)

    sum_1.hop()
    ffn_gain_part = jnp.sum(normed2_grad * state * scale_second, axis=0)
    state_grad = cot_half + norm_back(state, scale_second, ffn_gain_r, normed2_grad)
    grad_mine = state_grad.astype(jnp.bfloat16)
    near, across = lines.gather_far(grad_mine)
    back_0 = lines.row_pieces(sum_0.total())
    branch_terms = lines.near_sends(branch_kept, branch_other, branch_got)
    ready = sum_1.ready()
    near, across, ready, back_0, branch_terms = tie(near, across, ready, back_0, branch_terms)

    sum_1.hop(ready)
    attended_b = lines.both_cores(grad_mine, near, across)

    branch = [lines.flip(branch_terms[0], 1), lines.flip(branch_terms[1], 2)]
    back_0_first = lines.flip_first(back_0)
    qkv_grad, gain_parts, kept, other, attn_gain_part = run_attention(
        False,
        attended_b,
        attn_w,
        tables,
        gains_two,
        head_dim,
        query_width,
        attn_width,
        qkv_raw,
        normed,
    )
    kept, other, qkv_grad, branch, sum_1.got[1], back_0, back_0_first = tie(
        kept, other, qkv_grad, branch, sum_1.got[1], back_0, back_0_first
    )

    sum_1.hop()
    gains = jnp.concatenate(
        [
            back_around(attn_gain_part[0] / attn_gain_r),
            back_around(ffn_gain_part),
            jnp.sum(gain_parts[0].reshape(-1, head_dim), axis=0),
            gain_parts[1][:head_dim],
        ]
    )
    other = swap_cores(other)
    back_0_second = lines.flip_second(back_0, back_0_first)
    attn_sum = LineScatter(
        lines, run_weight_gradients(normed, qkv_grad, attended_b, heads_out, lines.length)
    )
    other, attn_sum.blocks = tie(other, attn_sum.blocks)
    got = lines.across_terms(kept, other)
    got, sum_1.got[2], back_0_second, branch = tie(got, sum_1.got[2], back_0_second, branch)
    attn_sum.hop()
    back_1 = lines.row_pieces(sum_1.total())
    near = lines.near_flips(kept, other, got)
    back_got = [lines.flip(back_1[1], 1)]
    attn_sum.hop()
    mixed = state + lines.near_sum(branch_kept, branch_other, branch)
    near, attn_sum.got[1], back_1, back_got, mixed = tie(
        near, attn_sum.got[1], back_1, back_got, mixed
    )
    ready = attn_sum.ready()
    near, ready = tie(near, ready)
    attn_sum.hop(ready)
    mixed_other = swap_cores(mixed)
    back_got = back_got + [lines.flip(back_1[r], r) for r in (2, 3)]
    gains, mixed_other = tie(gains, mixed_other)
    gains = gains + lines.flip(gains, 1)
    gains = gains + lines.flip(gains, 2)
    normed_grad = lines.near_sum(kept, other, near)
    input_grad = state_grad + norm_back(source, scale_first, attn_gain_r, normed_grad)
    mixed = run_place_halves(core, lines.spot, lines.length, mixed, mixed_other)
    attn_sum.got[2], back_got, input_grad, gains, mixed = tie(
        attn_sum.got[2], back_got, input_grad, gains, mixed
    )
    back_1 = [back_1[0]] + back_got
    attn_grads = lines.flip_pieces(lines.row_pieces(attn_sum.total()))
    input_other = swap_cores(input_grad)
    gains_got = [lines.turn(gains, k) for k in range(1, lines.length)]
    ffn_grads = run_place_columns(
        lines.place,
        [
            (back_0[0], back_0_first, back_0_second, back_0_second),
            back_1,
        ],
        3,
    )
    input_grad = run_place_halves(core, lines.spot, lines.length, input_grad, input_other)
    gains_got, attn_grads, input_grad = tie(gains_got, attn_grads, input_grad)
    for one in gains_got:
        gains = gains + one
    gains = gains + swap_cores(gains)

    def columns_of(related, start, stop):
        blocks = lines.by_place([b[:, start:stop] for b in related])
        return jnp.concatenate(blocks, axis=1).astype(jnp.float32)

    return (
        mixed,
        input_grad,
        gains[:width],
        gains[width : 2 * width],
        gains[2 * width : 2 * width + head_dim],
        gains[2 * width + head_dim :],
        columns_of(attn_grads, 0, query_width),
        columns_of(attn_grads, query_width, query_width + key_width),
        columns_of(attn_grads, query_width + key_width, attn_width),
        columns_of(attn_grads, attn_width, attn_width + query_width),
        *ffn_grads,
    )


def solution(mesh):
    dp = mesh.shape["dp"]
    weight = P("dp", "tensor")
    rows = P("dp", None)
    return jax.shard_map(
        lambda *arrays: local(dp, *arrays),
        mesh=mesh,
        in_specs=(rows, rows, rows, P(), P(), P(), P()) + (weight,) * 7,
        out_specs=(rows, rows, P(), P(), P(), P()) + (weight,) * 7,
        check_vma=False,
    )
```

```python
import functools

import jax
import jax.numpy as jnp
from jax import lax
from jax.experimental import pallas as pl
from jax.experimental.pallas import tpu as pltpu
from jax.sharding import PartitionSpec as P

eps = 1e-05
rope_base = 1000000.0
group = 4
sub_count = 2
mebibyte = 1024 * 1024
vmem_limit = 52 * mebibyte


def norm_rows(values, gain):
    scale = lax.rsqrt(jnp.mean(values * values, axis=-1, keepdims=True) + eps)
    return (values * scale * gain, scale)


def norm_back(values, scale, gain, incoming):
    weighted = incoming * gain
    return scale * weighted - values * (scale * scale * scale) * jnp.mean(
        weighted * values, axis=-1, keepdims=True
    )


def positions_of(segment_row):
    row_index = jnp.arange(segment_row.shape[0], dtype=jnp.int32)
    earlier = jnp.concatenate([segment_row[:1] - 1, segment_row[:-1]])
    starts = jnp.where(segment_row != earlier, row_index, jnp.zeros_like(row_index))
    return row_index - lax.cummax(starts, axis=0)


def angles(positions, width, lanes):
    frequency = rope_base ** (-jnp.arange(0, width, 2, dtype=jnp.float32) / width)
    frequency = jnp.tile(frequency, 2 * lanes // width)
    phases = positions.astype(jnp.float32)[..., None] * frequency
    return (jnp.cos(phases), jnp.sin(phases))


def dot_nn(left, right):
    return jnp.dot(left, right, preferred_element_type=jnp.float32)


def dot_nt(left, right):
    return lax.dot_general(
        left, right, (((1,), (1,)), ((), ())), preferred_element_type=jnp.float32
    )


def dot_tn(left, right):
    return lax.dot_general(
        left, right, (((0,), (0,)), ((), ())), preferred_element_type=jnp.float32
    )


def pick_dot(left, right):
    high = left.astype(jnp.bfloat16)
    low = (left - high.astype(jnp.float32)).astype(jnp.bfloat16)
    return dot_nn(high, right) + dot_nn(low, right)


def kernel_call(body, grid, in_specs, out_specs, out_shape, flops, moved, room=vmem_limit):
    return pl.pallas_call(
        body,
        grid=grid,
        in_specs=in_specs,
        out_specs=out_specs,
        out_shape=out_shape,
        compiler_params=pltpu.CompilerParams(vmem_limit_bytes=room),
        cost_estimate=pl.CostEstimate(flops=flops, bytes_accessed=moved, transcendentals=0),
    )


def whole(array):
    rank = len(array.shape)
    return pl.BlockSpec(array.shape, lambda *_: (0,) * rank)


def shape_of(shape, kind):
    return jax.ShapeDtypeStruct(shape, kind)


def turn_heads(values, head_dim):
    lanes = values.shape[-1]
    middle = head_dim // 2
    lane = lax.broadcasted_iota(jnp.int32, values.shape, 1) % head_dim
    ahead = pltpu.roll(values, lanes - middle, 1)
    behind = pltpu.roll(values, middle, 1)
    return jnp.where(lane < middle, -ahead, behind)


def index_pair(rows, columns):
    return (
        lax.broadcasted_iota(jnp.int32, (rows, columns), 0),
        lax.broadcasted_iota(jnp.int32, (rows, columns), 1),
    )


def ones_where(condition):
    return condition.astype(jnp.float32).astype(jnp.bfloat16)


def spread_of(rows, offset, columns, head_dim):
    row, column = index_pair(rows, columns)
    return ones_where(row - offset == column % head_dim)


def fold(values, head_dim):
    row, column = index_pair(values.shape[1], values.shape[1])
    return pick_dot(values, ones_where(row % head_dim == column % head_dim))


def head_mean(values, head_dim):
    row, column = index_pair(values.shape[1], values.shape[1])
    return pick_dot(values, ones_where(row // head_dim == column // head_dim)) * (1.0 / head_dim)


def prepare_heads(raw, gain, cosine, sine, head_dim):
    scale = lax.rsqrt(head_mean(raw * raw, head_dim) + eps)
    scaled = raw * scale * gain
    return scaled * cosine + turn_heads(scaled, head_dim) * sine, scale


def prepare_back(raw, scale, gain, cosine, sine, incoming, head_dim):
    turned = incoming * cosine - turn_heads(incoming * sine, head_dim)
    weighted = turned * gain
    grad = scale * weighted - raw * (scale * scale * scale) * head_mean(weighted * raw, head_dim)
    return grad, jnp.sum(turned * raw * scale, axis=0, keepdims=True)


def head_inputs(raw, gains, cosine, sine, head_dim, width):
    query, query_scale = prepare_heads(raw[:, :width], gains[0:1], cosine, sine, head_dim)
    rest = raw[:, width:]
    key_raw = pick_dot(rest, spread_of(rest.shape[1], 0, width, head_dim))
    key, key_scale = prepare_heads(key_raw, gains[1:2], cosine, sine, head_dim)
    value = dot_nn(
        rest.astype(jnp.bfloat16), spread_of(rest.shape[1], head_dim, width, head_dim)
    ).astype(jnp.bfloat16)
    return (
        query.astype(jnp.bfloat16) * jnp.bfloat16(0.125),
        query_scale,
        key_raw,
        key.astype(jnp.bfloat16),
        key_scale,
        value,
    )


def only_head(values, head, head_dim):
    lane = lax.broadcasted_iota(jnp.int32, values.shape, 1)
    return jnp.where(lane // head_dim == head, values, jnp.zeros_like(values))


def exps_of(scores, allowed):
    return jnp.exp(jnp.where(allowed, scores, -1000000000.0))


def block_product(kept, other, blocks, start, stop):
    rows = blocks[0].shape[0]
    total = None
    for k, block in enumerate(blocks):
        left = jnp.concatenate(
            [kept[:, k * rows : (k + 1) * rows], other[:, k * rows : (k + 1) * rows]], axis=0
        )
        more = dot_nn(left, block[:, start:stop])
        total = more if total is None else total + more
    return total


def by_halves(swapped, one, two):
    return jnp.where(swapped, two, one), jnp.where(swapped, one, two)


def head_tables(cosine_ref, sine_ref, width):
    repeat = width // cosine_ref.shape[-1]
    return (
        jnp.concatenate([cosine_ref[0]] * repeat, axis=1),
        jnp.concatenate([sine_ref[0]] * repeat, axis=1),
    )


def attention_forward(count, head_dim, width, *refs):
    kept, other = refs[:2]
    refs = refs[2:]
    swap_ref, cosine_ref, sine_ref, start_ref, index_column, index_row, gains = refs[:7]
    blocks = refs[7 : 7 + count]
    raw_ref, heads_kept, heads_other, part_kept, part_other = refs[7 + count :]
    half = kept.shape[0]
    attn_width = raw_ref.shape[-1]
    raw = block_product(kept, other, blocks, 0, attn_width)
    swapped = swap_ref[...] == 1
    raw = jnp.concatenate(by_halves(swapped, raw[:half], raw[half:]), axis=0)
    raw_ref[0] = raw
    cosine, sine = head_tables(cosine_ref, sine_ref, width)
    query, _, _, key, _, value = head_inputs(raw, gains[...], cosine, sine, head_dim, width)
    allowed = (index_row[...] <= index_column[...]) & (index_row[...] >= start_ref[0])
    one = jnp.zeros((half, width), jnp.float32)
    two = one
    for head in range(width // head_dim):
        query_h = only_head(query, head, head_dim)
        for first in (True, False):
            span, keys = (slice(0, half), half) if first else (slice(half, 2 * half), 2 * half)
            exps = exps_of(dot_nt(query_h[span], key[:keys]), allowed[span, :keys])
            part = dot_nn(exps.astype(jnp.bfloat16), value[:keys])
            part = part * (1.0 / jnp.sum(exps, axis=-1, keepdims=True))
            part = only_head(part, head, head_dim)
            if first:
                one = one + part
            else:
                two = two + part
    heads = by_halves(swapped, one.astype(jnp.bfloat16), two.astype(jnp.bfloat16))
    heads_kept[...] = heads[0]
    heads_other[...] = heads[1]
    heads = jnp.concatenate(heads, axis=0)
    rows = blocks[0].shape[0]
    for k, block in enumerate(blocks):
        out = dot_nt(heads, block[:, attn_width : attn_width + width]).astype(jnp.bfloat16)
        part_kept[:, k * rows : (k + 1) * rows] = out[:half]
        part_other[:, k * rows : (k + 1) * rows] = out[half:]


def attention_backward(count, head_dim, width, *refs):
    kept, other, raw_ref, normed_kept, normed_other = refs[:5]
    refs = refs[5:]
    swap_ref, cosine_ref, sine_ref, start_ref, index_column, index_row, gains = refs[:7]
    blocks = refs[7 : 7 + count]
    grad_kept, grad_other, gain_ref, part_kept, part_other, scaled_ref = refs[7 + count :]
    half = kept.shape[0]
    attn_width = raw_ref.shape[-1]
    grads = block_product(kept, other, blocks, attn_width, attn_width + width)
    grads = grads.astype(jnp.bfloat16)
    swapped = swap_ref[...] == 1
    grads = jnp.concatenate(by_halves(swapped, grads[:half], grads[half:]), axis=0)
    raw = raw_ref[0]
    cosine, sine = head_tables(cosine_ref, sine_ref, width)
    query, query_scale, key_raw, key, key_scale, value = head_inputs(
        raw, gains[...], cosine, sine, head_dim, width
    )
    allowed = (index_column[...] <= index_row[...]) & (index_column[...] >= start_ref[0])
    zero = jnp.zeros((half, width), jnp.float32)
    query_grads, key_grads, value_grads = [zero, zero], [zero, zero], [zero, zero]
    for head in range(width // head_dim):
        query_h = only_head(query, head, head_dim)
        grad_h = only_head(grads, head, head_dim)
        for part in range(2):
            span, keys = slice(part * half, (part + 1) * half), (part + 1) * half
            exps = exps_of(dot_nt(key[:keys], query_h[span]), allowed[:keys, span])
            probs_f = exps * (1.0 / jnp.sum(exps, axis=0, keepdims=True))
            weighted = probs_f * dot_nt(value[:keys], grad_h[span])
            score_grad = weighted - probs_f * jnp.sum(weighted, axis=0, keepdims=True)
            score_grad = score_grad.astype(jnp.bfloat16)
            query_grads[part] += only_head(dot_tn(score_grad, key[:keys]), head, head_dim)
            value_part = dot_nn(probs_f.astype(jnp.bfloat16), grad_h[span])
            key_part = dot_nn(score_grad, query_h[span])
            for block in range(part + 1):
                rows = slice(block * half, (block + 1) * half)
                value_grads[block] += value_part[rows]
                key_grads[block] += key_part[rows]
    query_grad = 0.125 * jnp.concatenate(query_grads, axis=0)
    key_grad = fold(jnp.concatenate(key_grads, axis=0), head_dim)
    value_grad = fold(jnp.concatenate(value_grads, axis=0), head_dim)
    query_grad, query_gain_part = prepare_back(
        raw[:, :width], query_scale, gains[0:1], cosine, sine, query_grad, head_dim
    )
    key_grad, key_gain_part = prepare_back(
        key_raw, key_scale, gains[1:2], cosine, sine, key_grad, head_dim
    )
    rest = attn_width - width
    lane = lax.broadcasted_iota(jnp.int32, (2 * half, rest), 1)
    rest_grad = jnp.where(lane < head_dim, key_grad[:, :rest], value_grad[:, :rest])
    query_grad = query_grad.astype(jnp.bfloat16)
    rest_grad = rest_grad.astype(jnp.bfloat16)
    query_sides = by_halves(swapped, query_grad[:half], query_grad[half:])
    rest_sides = by_halves(swapped, rest_grad[:half], rest_grad[half:])
    all_sides = []
    for side, out in enumerate((grad_kept, grad_other)):
        both = jnp.concatenate([query_sides[side], rest_sides[side]], axis=1)
        out[...] = both
        all_sides.append(both)
    all_sides = jnp.concatenate(all_sides, axis=0)
    parts = jnp.concatenate([query_gain_part, key_gain_part], axis=0)

    @pl.when(pl.program_id(0) == 0)
    def _():
        scaled_ref[...] = jnp.zeros_like(scaled_ref)

    rows = blocks[0].shape[0]
    for k, block in enumerate(blocks):
        span = slice(k * rows, (k + 1) * rows)
        out = dot_nt(all_sides, block[:, :attn_width])
        scaled = out[:half] * normed_kept[:, span].astype(jnp.float32)
        scaled = scaled + out[half:] * normed_other[:, span].astype(jnp.float32)
        scaled_ref[:, span] += jnp.sum(scaled, axis=0, keepdims=True)
        out = out.astype(jnp.bfloat16)
        part_kept[:, span] = out[:half]
        part_other[:, span] = out[half:]

    @pl.when(pl.program_id(0) == 0)
    def _():
        gain_ref[...] = parts

    @pl.when(pl.program_id(0) != 0)
    def _():
        gain_ref[...] = gain_ref[...] + parts


def run_attention(forward, pair, blocks, tables, gains, head_dim, width, attn_width, raw=None, normed=None):
    half = pair[0].shape[0] // group
    model = pair[0].shape[1]
    swapped, cosine, sine, start_columns, start_rows, index = tables
    starts = start_columns if forward else start_rows
    rows = lambda n: pl.BlockSpec((half, n), lambda s: (s, 0))
    per_sequence = lambda shape: pl.BlockSpec((1,) + shape[1:], lambda s: (s, 0, 0))
    column, row = index[:, None], index[None, :]
    common = [swapped, cosine, sine, starts, column, row, gains]
    common_specs = [whole(swapped)] + [per_sequence(a.shape) for a in (cosine, sine, starts)]
    common_specs += [whole(column), whole(row), whole(gains)]
    common += blocks
    common_specs += [whole(b) for b in blocks]
    raw_shape = (group, 2 * half, attn_width)
    flops = 2 * 2 * group * half * model * attn_width * 10
    moved = 16 * group * half * model
    side = lambda n: shape_of((group * half, n), jnp.bfloat16)
    if forward:
        results = kernel_call(
            functools.partial(attention_forward, len(blocks), head_dim, width),
            (group,),
            [rows(model)] * 2 + common_specs,
            [per_sequence(raw_shape), rows(width), rows(width), rows(model), rows(model)],
            [shape_of(raw_shape, jnp.float32), side(width), side(width), side(model), side(model)],
            flops,
            moved,
        )(*pair, *common)
        return results[0], tuple(results[1:3]), results[3], results[4]
    results = kernel_call(
        functools.partial(attention_backward, len(blocks), head_dim, width),
        (group,),
        [rows(model)] * 2 + [per_sequence(raw_shape)] + [rows(model)] * 2 + common_specs,
        [rows(attn_width), rows(attn_width), pl.BlockSpec((2, width), lambda s: (0, 0))]
        + [rows(model)] * 2
        + [pl.BlockSpec((1, model), lambda s: (0, 0))],
        [side(attn_width), side(attn_width), shape_of((2, width), jnp.float32)]
        + [side(model)] * 2
        + [shape_of((1, model), jnp.float32)],
        flops,
        moved,
    )(*pair, raw, *normed, *common)
    return tuple(results[:2]), *results[2:]


def ffn_units(count, ff_sub, earlier, *refs):
    normed, out = refs[0:2], refs[2:4]
    blocks, refs = refs[4 : 4 + count], refs[4 + count :]
    if earlier:
        before, refs = refs[0:2], refs[2:]
    inner_refs, grad_refs, terms = refs[0:2], refs[2:4], refs[4:6]
    tile = normed[0].shape[0]
    gate_up = block_product(normed[0], normed[1], blocks, 0, 2 * ff_sub)
    inner_grad = block_product(out[0], out[1], blocks, 2 * ff_sub, 3 * ff_sub)
    gate, up = gate_up[:, :ff_sub], gate_up[:, ff_sub:]
    sigmoid = 1.0 / (1.0 + jnp.exp(-gate))
    silu = gate * sigmoid
    inner = (silu * up).astype(jnp.bfloat16)
    gate_grad = (inner_grad * up * sigmoid * (1.0 + gate * (1.0 - sigmoid))).astype(jnp.bfloat16)
    up_grad = (inner_grad * silu).astype(jnp.bfloat16)
    for side in range(2):
        rows = slice(side * tile, (side + 1) * tile)
        inner_refs[side][...] = inner[rows]
        grad_refs[side][:, :ff_sub] = gate_grad[rows]
        grad_refs[side][:, ff_sub:] = up_grad[rows]
    if not earlier:
        return
    here = jnp.concatenate([gate_grad, up_grad], axis=1)
    rows = blocks[0].shape[0]
    for k in range(count):
        span = slice(k * rows, (k + 1) * rows)
        total = dot_nt(here, blocks[k][:, : 2 * ff_sub])
        for side in range(2):
            part = total[side * tile : (side + 1) * tile]
            part = part + before[side][:, span].astype(jnp.float32)
            terms[side][:, span] = part.astype(jnp.bfloat16)


def run_ffn_units(normed, out, blocks, ff_sub, before=None):
    tokens, model = normed[0].shape
    tile = min(256, tokens)
    rows = lambda n: pl.BlockSpec((tile, n), lambda i: (i, 0))
    earlier = before is not None
    shapes = [ff_sub] * 2 + [2 * ff_sub] * 2 + [model] * 2 * earlier
    return kernel_call(
        functools.partial(ffn_units, len(blocks), ff_sub, earlier),
        (tokens // tile,),
        [rows(model)] * 4
        + [whole(b) for b in blocks]
        + [rows(model)] * 2 * earlier,
        [rows(n) for n in shapes],
        [shape_of((tokens, n), jnp.bfloat16) for n in shapes],
        12 * tokens * model * ff_sub,
        8 * tokens * model,
    )(*normed, *out, *blocks, *(before if earlier else ()))


def weight_gradients(count, per, *refs):
    first, second = refs[0:2], refs[2:4]
    first_grad, second_grad = refs[4:6], refs[6:8]
    outs = refs[8:]
    one = dot_tn(first[0][...], first_grad[0][...]) + dot_tn(first[1][...], first_grad[1][...])
    two = dot_tn(second[0][...], second_grad[0][...]) + dot_tn(second[1][...], second_grad[1][...])
    width = one.shape[1]
    for k in range(count):

        @pl.when(pl.program_id(0) // per == k)
        def _(k=k):
            outs[k][:, :width] = one.astype(jnp.bfloat16)
            outs[k][:, width:] = two.astype(jnp.bfloat16)


def run_weight_gradients(first, first_grad, second, second_grad, count):
    tokens, model = first[0].shape
    block_rows = model // count
    tile = min(256, block_rows)
    per = block_rows // tile
    width = first_grad[0].shape[1] + second_grad[0].shape[1]
    columns = pl.BlockSpec((tokens, tile), lambda i: (0, i))
    out_spec = lambda k: pl.BlockSpec(
        (tile, width), lambda i: (jnp.clip(i - per * k, 0, per - 1), 0)
    )
    return kernel_call(
        functools.partial(weight_gradients, count, per),
        (model // tile,),
        [columns] * 4 + [whole(a) for a in (*first_grad, *second_grad)],
        [out_spec(k) for k in range(count)],
        [shape_of((block_rows, width), jnp.bfloat16)] * count,
        2 * tokens * model * 256,
        tokens * model,
        vmem_limit,
    )(*first, *second, *first_grad, *second_grad)


def partial_gradients(count, per, *refs):
    left, right, outs = refs[0:2], refs[2:4], refs[-count:]
    product = dot_tn(left[0][...], right[0][...]) + dot_tn(left[1][...], right[1][...])
    product = product.astype(jnp.bfloat16)
    for k in range(count):

        @pl.when(pl.program_id(0) // per == k)
        def _(k=k):
            outs[k][...] = product


def run_partial_gradients(left, right, count, width, column, into=()):
    tokens, model = left[0].shape
    block_rows = model // count
    tile = min(256, block_rows)
    per = block_rows // tile
    columns = pl.BlockSpec((tokens, tile), lambda i: (0, i))
    part = right[0].shape[1]
    out_spec = lambda k: pl.BlockSpec(
        (tile, part), lambda i: (jnp.clip(i - per * k, 0, per - 1), column)
    )
    return pl.pallas_call(
        functools.partial(partial_gradients, count, per),
        grid=(model // tile,),
        in_specs=[columns] * 2
        + [whole(a) for a in right]
        + [pl.BlockSpec(memory_space=pl.ANY)] * len(into),
        out_specs=[out_spec(k) for k in range(count)],
        out_shape=[shape_of((block_rows, width), jnp.bfloat16)] * count,
        input_output_aliases={4 + k: k for k in range(len(into))},
        compiler_params=pltpu.CompilerParams(vmem_limit_bytes=vmem_limit),
        cost_estimate=pl.CostEstimate(
            flops=2 * tokens * model * 128, bytes_accessed=tokens * model // 2, transcendentals=0
        ),
    )(*left, *right, *into)


def transposed_product(parts, count, *refs):
    lefts = refs[: 2 * parts]
    blocks = refs[2 * parts : 2 * parts + parts * count]
    outs = refs[2 * parts + parts * count :]
    tile = lefts[0].shape[0]
    rows = blocks[0].shape[0]
    for k in range(count):
        total = None
        span = slice(k * rows, (k + 1) * rows)
        for p in range(parts):
            left = jnp.concatenate([lefts[2 * p][...], lefts[2 * p + 1][...]], axis=0)
            more = dot_nt(left, blocks[p * count + k][...])
            total = more if total is None else total + more
        total = total.astype(jnp.bfloat16)
        outs[0][:, span] = total[:tile]
        outs[1][:, span] = total[tile:]


def run_transposed_product(pairs, blocks, column, columns):
    count = len(blocks[0])
    tokens = pairs[0][0].shape[0]
    model = count * blocks[0][0].shape[0]
    tile = min(256, tokens)
    rows = lambda n: pl.BlockSpec((tile, n), lambda i: (i, 0))
    lefts = [a for pair in pairs for a in pair]
    flat = [b for one in blocks for b in one]
    return kernel_call(
        functools.partial(transposed_product, len(pairs), count),
        (tokens // tile,),
        [rows(a.shape[1]) for a in lefts]
        + [pl.BlockSpec((b.shape[0], columns), lambda i: (0, column)) for b in flat],
        [rows(model)] * 2,
        [shape_of((tokens, model), jnp.bfloat16)] * 2,
        2 * tokens * model * 256,
        tokens * model,
        vmem_limit,
    )(*lefts, *flat)


def add_three(first, second, third, out):
    total = first[...].astype(jnp.float32) + second[...].astype(jnp.float32)
    out[...] = (total + third[...].astype(jnp.float32)).astype(jnp.bfloat16)


def add_swapped(odd_ref, one, two, first, second, out_first, out_second):
    odd = odd_ref[...] == 1
    for left, right, got, out in ((one, two, first, out_first), (two, one, second, out_second)):
        here = jnp.where(odd, right[...].astype(jnp.float32), left[...].astype(jnp.float32))
        out[...] = (here + got[...].astype(jnp.float32)).astype(jnp.bfloat16)


def run_add(body, arrays, outs, flag=None):
    rows, width = arrays[0].shape
    tile = min(256, rows)
    spec = pl.BlockSpec((tile, width), lambda i: (i, 0))
    flags = [] if flag is None else [flag]
    return kernel_call(
        body,
        (rows // tile,),
        [whole(f) for f in flags] + [spec] * len(arrays),
        [spec] * outs,
        [shape_of((rows, width), jnp.bfloat16)] * outs,
        1,
        12 * rows * width,
        16 * mebibyte if rows * width > mebibyte // 2 else vmem_limit,
    )(*flags, *arrays)


def place_columns(subs, place_ref, *refs):
    ins, outs = refs[: group * subs], refs[group * subs :]
    place = place_ref[0]
    rows = ins[0].shape[0]
    width = ins[0].shape[1] // len(outs)
    for s in range(subs):
        for r, ref in enumerate(ins[group * s : group * (s + 1)]):
            start = ref.shape[0] - rows if r == group - 1 else 0
            column = pl.multiple_of((s * group + (place ^ r)) * width, width)
            for m, out in enumerate(outs):
                piece = ref[start : start + rows, m * width : (m + 1) * width]
                out[:, pl.ds(column, width)] = piece.astype(jnp.float32)


def run_place_columns(place, parts, count):
    rows, width = parts[0][0].shape
    flat = [a for part in parts for a in part]
    full = lambda a: pl.BlockSpec(a.shape, lambda i, place: (0, 0))
    shape = shape_of((rows, width // count * group * len(parts)), jnp.float32)
    return pl.pallas_call(
        functools.partial(place_columns, len(parts)),
        grid_spec=pltpu.PrefetchScalarGridSpec(
            num_scalar_prefetch=1,
            grid=(1,),
            in_specs=[full(a) for a in flat],
            out_specs=[full(shape)] * count,
        ),
        out_shape=[shape] * count,
        compiler_params=pltpu.CompilerParams(vmem_limit_bytes=32 * mebibyte),
    )(place.reshape(1).astype(jnp.int32), *flat)


def place_halves(place, mine, other, out):
    half = mine.shape[0]
    core = place[0]
    out[pl.ds(core * half, half), :] = mine[...]
    out[pl.ds((1 - core) * half, half), :] = other[...]


def run_place_halves(core, spot, count, mine, other):
    half, model = mine.shape
    block = model // count
    source = pl.BlockSpec((half, block), lambda k, place: (0, k))
    return pl.pallas_call(
        place_halves,
        grid_spec=pltpu.PrefetchScalarGridSpec(
            num_scalar_prefetch=1,
            grid=(count,),
            in_specs=[source, source],
            out_specs=pl.BlockSpec((2 * half, block), lambda k, place: (0, (k + place[1]) % count)),
        ),
        out_shape=shape_of((2 * half, model), jnp.float32),
        compiler_params=pltpu.CompilerParams(vmem_limit_bytes=12 * mebibyte),
        cost_estimate=pl.CostEstimate(flops=1, bytes_accessed=16 * half * model, transcendentals=0),
    )(jnp.stack([core, spot]).astype(jnp.int32), mine, other)


def swap_cores(values):
    return lax.ppermute(values, "tensor", [(0, 1), (1, 0)])


sides = ((0, 1), (1, 0), (2, 3), (3, 2))
middle = ((1, 2), (2, 1))
outward = ((2, 3), (1, 0))
inward = ((0, 1), (3, 2))


class Lines:
    def __init__(self, dp):
        self.dp = dp
        self.length = dp // group
        index = lax.axis_index("dp")
        self.place = index % group
        self.spot = index // group

    def flip(self, values, relation):
        return lax.ppermute(values, "dp", [(i, i ^ relation) for i in range(self.dp)])

    def ends(self, values, moves):
        pairs = [
            (one * group + place, two * group + place)
            for one, two in moves
            for place in range(group)
        ]
        return lax.ppermute(values, "dp", pairs)

    def turn(self, values, step):
        pairs = [
            (spot * group + place, ((spot + step) % self.length) * group + place)
            for spot in range(self.length)
            for place in range(group)
        ]
        return lax.ppermute(values, "dp", pairs)

    def by_place(self, related):
        odd = self.place % 2 == 1
        high = self.place // 2 == 1
        own, one, two, three = related
        pairs = (
            (jnp.where(odd, one, own), jnp.where(odd, own, one)),
            (jnp.where(odd, three, two), jnp.where(odd, two, three)),
        )
        return [
            jnp.where(high, pairs[1][0], pairs[0][0]),
            jnp.where(high, pairs[1][1], pairs[0][1]),
            jnp.where(high, pairs[0][0], pairs[1][0]),
            jnp.where(high, pairs[0][1], pairs[1][1]),
        ]

    def pieces(self, piece_of):
        return [piece_of(self.place ^ relation) for relation in range(group)]

    def flip_pieces(self, pieces):
        return [pieces[0]] + [self.flip(pieces[r], r) for r in range(1, group)]

    def flip_first(self, pieces):
        return self.flip(jnp.concatenate([pieces[1], pieces[3]]), 1)

    def flip_second(self, pieces, got):
        return self.flip(jnp.concatenate([pieces[2], got[got.shape[0] // 2 :]]), 2)

    def flipped(self, pieces, first, second):
        rows = pieces[0].shape[0]
        return [pieces[0], first[:rows], second[:rows], second[rows:]]

    def row_pieces(self, total):
        rows = total.shape[0] // group
        return [
            lax.dynamic_slice_in_dim(total, (self.place ^ r) * rows, rows) for r in range(group)
        ]

    def gather_near(self, mine):
        return [self.flip(mine, 1), self.flip(mine, 2)]

    def gather_across(self, near):
        middle = near[0].shape[0] // 2
        return [self.flip(near[0][:middle], 2), self.flip(near[1][middle:], 1)]

    def scatter_across(self, across):
        middle = across.shape[0] // 2
        return [self.flip(across[:middle], 1), self.flip(across[middle:], 2)]

    def gather_far(self, mine):
        near = self.gather_near(mine)
        return near, self.gather_across(near)

    def gather_tokens(self, mine):
        return self.both_cores(mine, *self.gather_far(mine))

    def both_cores(self, mine, near, across):
        kept = jnp.concatenate([mine] + near + across)
        return kept, swap_cores(kept)

    def terms(self, kept, other, relation):
        rows = kept.shape[0] // group
        span = slice(relation * rows, (relation + 1) * rows)
        return kept[span].astype(jnp.float32) + other[span].astype(jnp.float32)

    def across_terms(self, kept, other):
        return self.scatter_across(self.terms(kept, other, 3).astype(jnp.bfloat16))

    def near_sends(self, kept, other, got):
        one, two = self.terms(kept, other, 1), self.terms(kept, other, 2)
        middle = one.shape[0] // 2
        one = jnp.concatenate([one[:middle], one[middle:] + got[1].astype(jnp.float32)])
        two = jnp.concatenate([two[:middle] + got[0].astype(jnp.float32), two[middle:]])
        return [one.astype(jnp.bfloat16), two.astype(jnp.bfloat16)]

    def near_flips(self, kept, other, got):
        one, two = self.near_sends(kept, other, got)
        return [self.flip(one, 1), self.flip(two, 2)]

    def near_sum(self, kept, other, near):
        one, two = near
        return self.terms(kept, other, 0) + one.astype(jnp.float32) + two.astype(jnp.float32)

    def near_terms(self, kept, other, got):
        return self.near_sum(kept, other, self.near_flips(kept, other, got))

    def scatter_tokens(self, kept, other):
        return self.near_terms(kept, other, self.across_terms(kept, other))


class LineGather:
    def __init__(self, lines, block):
        self.lines, self.block, self.got = lines, block, []

    def hop(self):
        lines, step = self.lines, len(self.got) + 1
        if lines.length != 4:
            turns = range(1, lines.length) if step == 1 else ()
            self.got.append([lines.turn(self.block, -k) for k in turns])
        elif step == 1:
            self.got.append([lines.ends(self.block, sides), lines.ends(self.block, middle)])
        elif step == 2:
            outer, inner = self.got[0]
            self.got.append([lines.ends(outer, middle), lines.ends(inner, outward)])
        else:
            self.got.append([lines.ends(self.got[1][0], outward)])

    def blocks(self):
        lines = self.lines
        if lines.length != 4:
            return [self.block] + self.got[0]
        (outer, inner), (inner_two, outer_two), (outer_three,) = self.got
        spot = lines.spot
        return [
            self.block,
            jnp.where(spot == 3, outer_three, jnp.where(spot == 1, inner, outer)),
            jnp.where((spot == 1) | (spot == 2), inner_two, outer_two),
            jnp.where(spot == 0, outer_three, jnp.where(spot == 2, inner, outer)),
        ]


class LineScatter:
    def __init__(self, lines, blocks):
        self.lines, self.blocks, self.got = lines, blocks, []

    def ready(self):
        step = len(self.got) + 1
        if self.lines.length != 4:
            return []
        if step == 1:
            return [self.blocks[3], self.blocks[1]]
        if step == 2:
            return run_add(add_three, [self.blocks[2], *self.got[0]], 1)
        odd = (self.lines.spot % 2).astype(jnp.int32).reshape(1, 1)
        return run_add(add_swapped, [self.blocks[1], self.blocks[3], *self.got[1]], 2, odd)

    def hop(self, ready=None):
        lines, step = self.lines, len(self.got) + 1
        if lines.length != 4:
            turns = range(1, lines.length) if step == 1 else ()
            self.got.append([lines.turn(self.blocks[k], k) for k in turns])
            return
        ready = self.ready() if ready is None else ready
        if step == 1:
            self.got.append([lines.ends(ready[0], ((0, 1),)), lines.ends(ready[1], ((3, 2),))])
        elif step == 2:
            self.got.append([lines.ends(ready[0], middle), lines.ends(ready[0], inward)])
        else:
            self.got.append([lines.ends(ready[0], sides), lines.ends(ready[1], middle)])

    def total(self):
        last = self.got[-1] if self.lines.length == 4 else self.got[0]
        result = self.blocks[0].astype(jnp.float32)
        for one in last:
            result = result + one.astype(jnp.float32)
        return result.astype(jnp.bfloat16)


def tie(*values):
    return lax.optimization_barrier(values)


def local(
    dp,
    tokens,
    segments,
    cotangent,
    attn_gain,
    ffn_gain,
    query_gain,
    key_gain,
    w_query,
    key_weight,
    value_weight,
    w_out,
    w_gate,
    w_up,
    w_down,
):
    lines = Lines(dp)
    core = lax.axis_index("tensor")
    length, width = tokens.shape
    half = length // 2
    head_dim = query_gain.shape[0]
    rows = w_query.shape[0]
    block_rows = rows * group
    query_width = w_query.shape[1] // group
    key_width = key_weight.shape[1] // group
    attn_width = query_width + 2 * key_width
    ff_sub = w_gate.shape[1] // group // sub_count

    def around(values):
        return jnp.roll(values, -lines.spot * block_rows, axis=-1)

    def back_around(values):
        return jnp.roll(values, lines.spot * block_rows, axis=-1)

    attn_gain_r, ffn_gain_r = around(attn_gain), around(ffn_gain)

    def columns(weight, start, size):
        return lax.dynamic_slice_in_dim(weight, start, size, axis=1)

    attn_pieces = lines.pieces(
        lambda j: jnp.concatenate(
            [
                columns(w_query, j * query_width, query_width),
                columns(key_weight, j * key_width, key_width),
                columns(value_weight, j * key_width, key_width),
                columns(w_out, j * query_width, query_width),
            ],
            axis=1,
        )
    )
    attn_shared = lines.flip_pieces(attn_pieces)
    source = around(lax.dynamic_slice_in_dim(tokens, core * half, half)).astype(jnp.float32)
    normed_f, scale_first = norm_rows(source, attn_gain_r)
    normed_mine = normed_f.astype(jnp.bfloat16)

    seg_near = jnp.concatenate([segments, lines.flip(segments, 1)])
    seg_second = lines.flip(seg_near, 2)
    attn_shared, normed_mine, seg_near, seg_second = tie(
        attn_shared, normed_mine, seg_near, seg_second
    )

    def ffn_piece(s):
        return lines.pieces(
            lambda j: jnp.concatenate(
                [
                    columns(weight, s * group * ff_sub + j * ff_sub, ff_sub)
                    for weight in (w_gate, w_up, w_down)
                ],
                axis=1,
            )
        )


    seg_all = jnp.concatenate([seg_near, seg_second])
    positions = jax.vmap(positions_of)(seg_all)
    index = jnp.arange(length, dtype=jnp.int32)
    cosine, sine = angles(positions, head_dim, 2 * head_dim)
    swapped = jnp.full((1, 1), core, jnp.int32)
    starts = index[None] - positions
    tables = (swapped, cosine, sine, starts[..., None], starts[:, None, :], index)
    gains_two = jnp.stack(
        [
            jnp.tile(query_gain, query_width // head_dim),
            jnp.tile(key_gain, query_width // head_dim),
        ]
    )

    attn_line = LineGather(lines, jnp.concatenate(lines.by_place(attn_shared), axis=0))
    attn_line.hop()
    near = lines.gather_near(normed_mine)
    mine_other = swap_cores(normed_mine)
    near, attn_line.got[0], tables, mine_other, w_gate, w_up, w_down = tie(
        near, attn_line.got[0], tables, mine_other, w_gate, w_up, w_down
    )
    attn_line.hop()
    across = lines.gather_across(near)
    pieces_0 = ffn_piece(0)
    near_other = swap_cores(near[0])
    near_other, near_two = tie(near_other, near[1])
    near = [near[0], near_two]
    near_other = [near_other, swap_cores(near_two)]
    across, attn_line.got[1], pieces_0, near_other, w_gate, w_up, w_down, cotangent = tie(
        across, attn_line.got[1], pieces_0, near_other, w_gate, w_up, w_down, cotangent
    )
    attn_line.hop()
    pieces_1 = ffn_piece(1)
    cot_half = around(lax.dynamic_slice_in_dim(cotangent, core * half, half))
    out_mine = cot_half.astype(jnp.bfloat16)
    across = jnp.concatenate(across)
    normed = (
        jnp.concatenate([normed_mine] + near + [across]),
        jnp.concatenate([mine_other] + near_other + [swap_cores(across)]),
    )
    shared_0 = lines.flip_pieces(pieces_0)
    normed, attn_line.got[2], shared_0, pieces_1, out_mine = tie(
        normed, attn_line.got[2], shared_0, pieces_1, out_mine
    )
    attn_w = attn_line.blocks()

    line_0 = LineGather(lines, jnp.concatenate(lines.by_place(shared_0), axis=0))
    line_0.hop()
    out_near = lines.gather_near(out_mine)
    qkv_raw, heads_out, attended_kept, attended_other = run_attention(
        True, normed, attn_w, tables, gains_two, head_dim, query_width, attn_width
    )
    attended_other, line_0.got[0], out_near, pieces_1 = tie(
        attended_other, line_0.got[0], out_near, pieces_1
    )

    line_0.hop()
    attended_other = swap_cores(attended_other)
    middle = half // 2
    out_first = lines.flip(out_near[0][:middle], 2)
    attended_other, out_first = tie(attended_other, out_first)
    first_1 = lines.flip_first(pieces_1)
    got = lines.across_terms(attended_kept, attended_other)
    got, first_1, line_0.got[1] = tie(got, first_1, line_0.got[1])
    line_0.hop()
    second_1 = lines.flip_second(pieces_1, first_1)
    attended = lines.near_terms(attended_kept, attended_other, got)
    attended, out_near = tie(attended, out_near)
    out_second = lines.flip(out_near[1][middle:], 1)
    attended, line_0.got[2], out_first, out_second, second_1 = tie(
        attended, line_0.got[2], out_first, out_second, second_1
    )
    shared_1 = lines.flipped(pieces_1, first_1, second_1)
    block_1 = jnp.concatenate(lines.by_place(shared_1), axis=0)

    line_1 = LineGather(lines, block_1)
    out_b = lines.both_cores(out_mine, out_near, [out_first, out_second])
    line_1.hop()
    state = source + attended
    normed2_f, scale_second = norm_rows(state, ffn_gain_r)
    near, across = lines.gather_far(normed2_f.astype(jnp.bfloat16))
    ffn_w = [line_0.blocks()]
    near, across, line_1.got[0], out_b, ffn_w[0] = tie(
        near, across, line_1.got[0], out_b, ffn_w[0]
    )

    line_1.hop()
    normed2 = lines.both_cores(normed2_f.astype(jnp.bfloat16), near, across)
    units_0 = run_ffn_units(normed2, out_b, ffn_w[0], ff_sub)
    units_0, line_1.got[1] = tie(units_0, line_1.got[1])
    line_1.hop()
    ffn_g = run_weight_gradients(normed2, units_0[2:], out_b, units_0[:2], lines.length)
    terms_0 = run_transposed_product([units_0[2:]], [ffn_w[0]], 0, 2 * ff_sub)
    ffn_g, line_1.got[2], units_0, terms_0 = tie(ffn_g, line_1.got[2], units_0, terms_0)
    sum_0 = LineScatter(lines, ffn_g)
    ffn_w.append(line_1.blocks())

    sum_0.hop()
    units_1 = run_ffn_units(normed2, out_b, ffn_w[1], ff_sub, terms_0)
    kept, other = units_1[4:]
    kept, other, sum_0.got[0], units_1 = tie(kept, other, sum_0.got[0], units_1)

    sum_0.hop()
    other = swap_cores(other)
    send = lines.terms(kept, other, 3).astype(jnp.bfloat16)
    send, units_1 = tie(send, units_1)
    got = lines.scatter_across(send)
    branch_kept, branch_other = run_transposed_product(
        [units_0[:2], units_1[:2]], ffn_w, 2, ff_sub
    )
    ffn_g = run_partial_gradients(normed2, units_1[2:4], lines.length, 3 * ff_sub, 0)
    got, sum_0.got[1], ffn_g, branch_kept, branch_other, units_1 = tie(
        got, sum_0.got[1], ffn_g, branch_kept, branch_other, units_1
    )
    sum_0.hop()
    branch_other = swap_cores(branch_other)
    near = lines.near_flips(kept, other, got)
    ffn_g = run_partial_gradients(out_b, units_1[:2], lines.length, 3 * ff_sub, 2, ffn_g)
    near, branch_kept, branch_other, ffn_g = tie(near, branch_kept, branch_other, ffn_g)
    sum_1 = LineScatter(lines, ffn_g)
    normed2_grad = lines.near_sum(kept, other, near)
    branch_got = lines.across_terms(branch_kept, branch_other)
    normed2_grad, sum_0.got[2], branch_got = tie(normed2_grad, sum_0.got[2], branch_got)

    sum_1.hop()
    ffn_gain_part = jnp.sum(normed2_grad * state * scale_second, axis=0)
    state_grad = cot_half + norm_back(state, scale_second, ffn_gain_r, normed2_grad)
    grad_mine = state_grad.astype(jnp.bfloat16)
    near, across = lines.gather_far(grad_mine)
    back_0 = lines.row_pieces(sum_0.total())
    branch_terms = lines.near_sends(branch_kept, branch_other, branch_got)
    ready = sum_1.ready()
    near, across, ready, back_0, branch_terms = tie(near, across, ready, back_0, branch_terms)

    sum_1.hop(ready)
    attended_b = lines.both_cores(grad_mine, near, across)

    branch = [lines.flip(branch_terms[0], 1), lines.flip(branch_terms[1], 2)]
    back_0_first = lines.flip_first(back_0)
    qkv_grad, gain_parts, kept, other, attn_gain_part = run_attention(
        False,
        attended_b,
        attn_w,
        tables,
        gains_two,
        head_dim,
        query_width,
        attn_width,
        qkv_raw,
        normed,
    )
    kept, other, qkv_grad, branch, sum_1.got[1], back_0, back_0_first = tie(
        kept, other, qkv_grad, branch, sum_1.got[1], back_0, back_0_first
    )

    sum_1.hop()
    gains = jnp.concatenate(
        [
            back_around(attn_gain_part[0] / attn_gain_r),
            back_around(ffn_gain_part),
            jnp.sum(gain_parts[0].reshape(-1, head_dim), axis=0),
            gain_parts[1][:head_dim],
        ]
    )
    other = swap_cores(other)
    back_0_second = lines.flip_second(back_0, back_0_first)
    attn_sum = LineScatter(
        lines, run_weight_gradients(normed, qkv_grad, attended_b, heads_out, lines.length)
    )
    other, attn_sum.blocks = tie(other, attn_sum.blocks)
    got = lines.across_terms(kept, other)
    got, sum_1.got[2], back_0_second, branch = tie(got, sum_1.got[2], back_0_second, branch)
    attn_sum.hop()
    back_1 = lines.row_pieces(sum_1.total())
    near = lines.near_flips(kept, other, got)
    back_got = [lines.flip(back_1[1], 1)]
    attn_sum.hop()
    mixed = state + lines.near_sum(branch_kept, branch_other, branch)
    near, attn_sum.got[1], back_1, back_got, mixed = tie(
        near, attn_sum.got[1], back_1, back_got, mixed
    )
    ready = attn_sum.ready()
    near, ready = tie(near, ready)
    attn_sum.hop(ready)
    mixed_other = swap_cores(mixed)
    back_got = back_got + [lines.flip(back_1[r], r) for r in (2, 3)]
    gains, mixed_other = tie(gains, mixed_other)
    gains = gains + lines.flip(gains, 1)
    gains = gains + lines.flip(gains, 2)
    normed_grad = lines.near_sum(kept, other, near)
    input_grad = state_grad + norm_back(source, scale_first, attn_gain_r, normed_grad)
    mixed = run_place_halves(core, lines.spot, lines.length, mixed, mixed_other)
    attn_sum.got[2], back_got, input_grad, gains, mixed = tie(
        attn_sum.got[2], back_got, input_grad, gains, mixed
    )
    back_1 = [back_1[0]] + back_got
    attn_grads = lines.flip_pieces(lines.row_pieces(attn_sum.total()))
    input_other = swap_cores(input_grad)
    ffn_grads = run_place_columns(
        lines.place,
        [
            (back_0[0], back_0_first, back_0_second, back_0_second),
            back_1,
        ],
        3,
    )
    input_grad = run_place_halves(core, lines.spot, lines.length, input_grad, input_other)
    bit = group
    while bit < dp:
        gains = gains + lines.flip(gains, bit)
        bit *= 2
    gains, attn_grads, ffn_grads = tie(gains, attn_grads, ffn_grads)
    gains = gains + swap_cores(gains)

    def columns_of(related, start, stop):
        blocks = lines.by_place([b[:, start:stop] for b in related])
        return jnp.concatenate(blocks, axis=1).astype(jnp.float32)

    return (
        mixed,
        input_grad,
        gains[:width],
        gains[width : 2 * width],
        gains[2 * width : 2 * width + head_dim],
        gains[2 * width + head_dim :],
        columns_of(attn_grads, 0, query_width),
        columns_of(attn_grads, query_width, query_width + key_width),
        columns_of(attn_grads, query_width + key_width, attn_width),
        columns_of(attn_grads, attn_width, attn_width + query_width),
        *ffn_grads,
    )


def solution(mesh):
    dp = mesh.shape["dp"]
    weight = P("dp", "tensor")
    rows = P("dp", None)
    return jax.shard_map(
        lambda *arrays: local(dp, *arrays),
        mesh=mesh,
        in_specs=(rows, rows, rows, P(), P(), P(), P()) + (weight,) * 7,
        out_specs=(rows, rows, P(), P(), P(), P()) + (weight,) * 7,
        check_vma=False,
    )
```

```python
import functools

import jax
import jax.numpy as jnp
from jax import lax
from jax.experimental import pallas as pl
from jax.experimental.pallas import tpu as pltpu
from jax.sharding import PartitionSpec as P

eps = 1e-05
rope_base = 1000000.0
group = 4
sub_count = 2
mebibyte = 1024 * 1024
vmem_limit = 52 * mebibyte


def norm_rows(values, gain):
    scale = lax.rsqrt(jnp.mean(values * values, axis=-1, keepdims=True) + eps)
    return (values * scale * gain, scale)


def norm_back(values, scale, gain, incoming):
    weighted = incoming * gain
    return scale * weighted - values * (scale * scale * scale) * jnp.mean(
        weighted * values, axis=-1, keepdims=True
    )


def positions_of(segment_row):
    row_index = jnp.arange(segment_row.shape[0], dtype=jnp.int32)
    earlier = jnp.concatenate([segment_row[:1] - 1, segment_row[:-1]])
    starts = jnp.where(segment_row != earlier, row_index, jnp.zeros_like(row_index))
    return row_index - lax.cummax(starts, axis=0)


def angles(positions, width, lanes):
    frequency = rope_base ** (-jnp.arange(0, width, 2, dtype=jnp.float32) / width)
    frequency = jnp.tile(frequency, 2 * lanes // width)
    phases = positions.astype(jnp.float32)[..., None] * frequency
    return (jnp.cos(phases), jnp.sin(phases))


def dot_nn(left, right):
    return jnp.dot(left, right, preferred_element_type=jnp.float32)


def dot_nt(left, right):
    return lax.dot_general(
        left, right, (((1,), (1,)), ((), ())), preferred_element_type=jnp.float32
    )


def dot_tn(left, right):
    return lax.dot_general(
        left, right, (((0,), (0,)), ((), ())), preferred_element_type=jnp.float32
    )


def pick_dot(left, right):
    high = left.astype(jnp.bfloat16)
    low = (left - high.astype(jnp.float32)).astype(jnp.bfloat16)
    return dot_nn(high, right) + dot_nn(low, right)


def kernel_call(body, grid, in_specs, out_specs, out_shape, flops, moved, room=vmem_limit):
    return pl.pallas_call(
        body,
        grid=grid,
        in_specs=in_specs,
        out_specs=out_specs,
        out_shape=out_shape,
        compiler_params=pltpu.CompilerParams(vmem_limit_bytes=room),
        cost_estimate=pl.CostEstimate(flops=flops, bytes_accessed=moved, transcendentals=0),
    )


def whole(array):
    rank = len(array.shape)
    return pl.BlockSpec(array.shape, lambda *_: (0,) * rank)


def shape_of(shape, kind):
    return jax.ShapeDtypeStruct(shape, kind)


def turn_heads(values, head_dim):
    lanes = values.shape[-1]
    middle = head_dim // 2
    lane = lax.broadcasted_iota(jnp.int32, values.shape, 1) % head_dim
    ahead = pltpu.roll(values, lanes - middle, 1)
    behind = pltpu.roll(values, middle, 1)
    return jnp.where(lane < middle, -ahead, behind)


def index_pair(rows, columns):
    return (
        lax.broadcasted_iota(jnp.int32, (rows, columns), 0),
        lax.broadcasted_iota(jnp.int32, (rows, columns), 1),
    )


def ones_where(condition):
    return condition.astype(jnp.float32).astype(jnp.bfloat16)


def spread_of(rows, offset, columns, head_dim):
    row, column = index_pair(rows, columns)
    return ones_where(row - offset == column % head_dim)


def fold(values, head_dim):
    row, column = index_pair(values.shape[1], values.shape[1])
    return pick_dot(values, ones_where(row % head_dim == column % head_dim))


def head_mean(values, head_dim):
    row, column = index_pair(values.shape[1], values.shape[1])
    return pick_dot(values, ones_where(row // head_dim == column // head_dim)) * (1.0 / head_dim)


def prepare_heads(raw, gain, cosine, sine, head_dim):
    scale = lax.rsqrt(head_mean(raw * raw, head_dim) + eps)
    scaled = raw * scale * gain
    return scaled * cosine + turn_heads(scaled, head_dim) * sine, scale


def prepare_back(raw, scale, gain, cosine, sine, incoming, head_dim):
    turned = incoming * cosine - turn_heads(incoming * sine, head_dim)
    weighted = turned * gain
    grad = scale * weighted - raw * (scale * scale * scale) * head_mean(weighted * raw, head_dim)
    return grad, jnp.sum(turned * raw * scale, axis=0, keepdims=True)


def head_inputs(raw, gains, cosine, sine, head_dim, width):
    query, query_scale = prepare_heads(raw[:, :width], gains[0:1], cosine, sine, head_dim)
    rest = raw[:, width:]
    key_raw = pick_dot(rest, spread_of(rest.shape[1], 0, width, head_dim))
    key, key_scale = prepare_heads(key_raw, gains[1:2], cosine, sine, head_dim)
    value = dot_nn(
        rest.astype(jnp.bfloat16), spread_of(rest.shape[1], head_dim, width, head_dim)
    ).astype(jnp.bfloat16)
    return (
        query.astype(jnp.bfloat16) * jnp.bfloat16(0.125),
        query_scale,
        key_raw,
        key.astype(jnp.bfloat16),
        key_scale,
        value,
    )


def only_head(values, head, head_dim):
    lane = lax.broadcasted_iota(jnp.int32, values.shape, 1)
    return jnp.where(lane // head_dim == head, values, jnp.zeros_like(values))


def exps_of(scores, allowed):
    return jnp.exp(jnp.where(allowed, scores, -1000000000.0))


def block_product(kept, other, blocks, start, stop):
    rows = blocks[0].shape[0]
    total = None
    for k, block in enumerate(blocks):
        left = jnp.concatenate(
            [kept[:, k * rows : (k + 1) * rows], other[:, k * rows : (k + 1) * rows]], axis=0
        )
        more = dot_nn(left, block[:, start:stop])
        total = more if total is None else total + more
    return total


def by_halves(swapped, one, two):
    return jnp.where(swapped, two, one), jnp.where(swapped, one, two)


def head_tables(cosine_ref, sine_ref, width):
    repeat = width // cosine_ref.shape[-1]
    return (
        jnp.concatenate([cosine_ref[0]] * repeat, axis=1),
        jnp.concatenate([sine_ref[0]] * repeat, axis=1),
    )


def attention_forward(count, head_dim, width, *refs):
    kept, other = refs[:2]
    refs = refs[2:]
    swap_ref, cosine_ref, sine_ref, start_ref, index_column, index_row, gains = refs[:7]
    blocks = refs[7 : 7 + count]
    raw_ref, heads_kept, heads_other, part_kept, part_other = refs[7 + count :]
    half = kept.shape[0]
    attn_width = raw_ref.shape[-1]
    raw = block_product(kept, other, blocks, 0, attn_width)
    swapped = swap_ref[...] == 1
    raw = jnp.concatenate(by_halves(swapped, raw[:half], raw[half:]), axis=0)
    raw_ref[0] = raw
    cosine, sine = head_tables(cosine_ref, sine_ref, width)
    query, _, _, key, _, value = head_inputs(raw, gains[...], cosine, sine, head_dim, width)
    allowed = (index_row[...] <= index_column[...]) & (index_row[...] >= start_ref[0])
    one = jnp.zeros((half, width), jnp.float32)
    two = one
    for head in range(width // head_dim):
        query_h = only_head(query, head, head_dim)
        for first in (True, False):
            span, keys = (slice(0, half), half) if first else (slice(half, 2 * half), 2 * half)
            exps = exps_of(dot_nt(query_h[span], key[:keys]), allowed[span, :keys])
            part = dot_nn(exps.astype(jnp.bfloat16), value[:keys])
            part = part * (1.0 / jnp.sum(exps, axis=-1, keepdims=True))
            part = only_head(part, head, head_dim)
            if first:
                one = one + part
            else:
                two = two + part
    heads = by_halves(swapped, one.astype(jnp.bfloat16), two.astype(jnp.bfloat16))
    heads_kept[...] = heads[0]
    heads_other[...] = heads[1]
    heads = jnp.concatenate(heads, axis=0)
    rows = blocks[0].shape[0]
    for k, block in enumerate(blocks):
        out = dot_nt(heads, block[:, attn_width : attn_width + width]).astype(jnp.bfloat16)
        part_kept[:, k * rows : (k + 1) * rows] = out[:half]
        part_other[:, k * rows : (k + 1) * rows] = out[half:]


def attention_backward(count, head_dim, width, *refs):
    kept, other, raw_ref, normed_kept, normed_other = refs[:5]
    refs = refs[5:]
    swap_ref, cosine_ref, sine_ref, start_ref, index_column, index_row, gains = refs[:7]
    blocks = refs[7 : 7 + count]
    grad_kept, grad_other, gain_ref, part_kept, part_other, scaled_ref = refs[7 + count :]
    half = kept.shape[0]
    attn_width = raw_ref.shape[-1]
    grads = block_product(kept, other, blocks, attn_width, attn_width + width)
    grads = grads.astype(jnp.bfloat16)
    swapped = swap_ref[...] == 1
    grads = jnp.concatenate(by_halves(swapped, grads[:half], grads[half:]), axis=0)
    raw = raw_ref[0]
    cosine, sine = head_tables(cosine_ref, sine_ref, width)
    query, query_scale, key_raw, key, key_scale, value = head_inputs(
        raw, gains[...], cosine, sine, head_dim, width
    )
    allowed = (index_column[...] <= index_row[...]) & (index_column[...] >= start_ref[0])
    zero = jnp.zeros((half, width), jnp.float32)
    query_grads, key_grads, value_grads = [zero, zero], [zero, zero], [zero, zero]
    for head in range(width // head_dim):
        query_h = only_head(query, head, head_dim)
        grad_h = only_head(grads, head, head_dim)
        for part in range(2):
            span, keys = slice(part * half, (part + 1) * half), (part + 1) * half
            exps = exps_of(dot_nt(key[:keys], query_h[span]), allowed[:keys, span])
            probs_f = exps * (1.0 / jnp.sum(exps, axis=0, keepdims=True))
            weighted = probs_f * dot_nt(value[:keys], grad_h[span])
            score_grad = weighted - probs_f * jnp.sum(weighted, axis=0, keepdims=True)
            score_grad = score_grad.astype(jnp.bfloat16)
            query_grads[part] += only_head(dot_tn(score_grad, key[:keys]), head, head_dim)
            value_part = dot_nn(probs_f.astype(jnp.bfloat16), grad_h[span])
            key_part = dot_nn(score_grad, query_h[span])
            for block in range(part + 1):
                rows = slice(block * half, (block + 1) * half)
                value_grads[block] += value_part[rows]
                key_grads[block] += key_part[rows]
    query_grad = 0.125 * jnp.concatenate(query_grads, axis=0)
    key_grad = fold(jnp.concatenate(key_grads, axis=0), head_dim)
    value_grad = fold(jnp.concatenate(value_grads, axis=0), head_dim)
    query_grad, query_gain_part = prepare_back(
        raw[:, :width], query_scale, gains[0:1], cosine, sine, query_grad, head_dim
    )
    key_grad, key_gain_part = prepare_back(
        key_raw, key_scale, gains[1:2], cosine, sine, key_grad, head_dim
    )
    rest = attn_width - width
    lane = lax.broadcasted_iota(jnp.int32, (2 * half, rest), 1)
    rest_grad = jnp.where(lane < head_dim, key_grad[:, :rest], value_grad[:, :rest])
    query_grad = query_grad.astype(jnp.bfloat16)
    rest_grad = rest_grad.astype(jnp.bfloat16)
    query_sides = by_halves(swapped, query_grad[:half], query_grad[half:])
    rest_sides = by_halves(swapped, rest_grad[:half], rest_grad[half:])
    all_sides = []
    for side, out in enumerate((grad_kept, grad_other)):
        both = jnp.concatenate([query_sides[side], rest_sides[side]], axis=1)
        out[...] = both
        all_sides.append(both)
    all_sides = jnp.concatenate(all_sides, axis=0)
    parts = jnp.concatenate([query_gain_part, key_gain_part], axis=0)

    @pl.when(pl.program_id(0) == 0)
    def _():
        scaled_ref[...] = jnp.zeros_like(scaled_ref)

    rows = blocks[0].shape[0]
    for k, block in enumerate(blocks):
        span = slice(k * rows, (k + 1) * rows)
        out = dot_nt(all_sides, block[:, :attn_width])
        scaled = out[:half] * normed_kept[:, span].astype(jnp.float32)
        scaled = scaled + out[half:] * normed_other[:, span].astype(jnp.float32)
        scaled_ref[:, span] += jnp.sum(scaled, axis=0, keepdims=True)
        out = out.astype(jnp.bfloat16)
        part_kept[:, span] = out[:half]
        part_other[:, span] = out[half:]

    @pl.when(pl.program_id(0) == 0)
    def _():
        gain_ref[...] = parts

    @pl.when(pl.program_id(0) != 0)
    def _():
        gain_ref[...] = gain_ref[...] + parts


def run_attention(forward, pair, blocks, tables, gains, head_dim, width, attn_width, raw=None, normed=None):
    half = pair[0].shape[0] // group
    model = pair[0].shape[1]
    swapped, cosine, sine, start_columns, start_rows, index = tables
    starts = start_columns if forward else start_rows
    rows = lambda n: pl.BlockSpec((half, n), lambda s: (s, 0))
    per_sequence = lambda shape: pl.BlockSpec((1,) + shape[1:], lambda s: (s, 0, 0))
    column, row = index[:, None], index[None, :]
    common = [swapped, cosine, sine, starts, column, row, gains]
    common_specs = [whole(swapped)] + [per_sequence(a.shape) for a in (cosine, sine, starts)]
    common_specs += [whole(column), whole(row), whole(gains)]
    common += blocks
    common_specs += [whole(b) for b in blocks]
    raw_shape = (group, 2 * half, attn_width)
    flops = 2 * 2 * group * half * model * attn_width * 10
    moved = 16 * group * half * model
    side = lambda n: shape_of((group * half, n), jnp.bfloat16)
    if forward:
        results = kernel_call(
            functools.partial(attention_forward, len(blocks), head_dim, width),
            (group,),
            [rows(model)] * 2 + common_specs,
            [per_sequence(raw_shape), rows(width), rows(width), rows(model), rows(model)],
            [shape_of(raw_shape, jnp.float32), side(width), side(width), side(model), side(model)],
            flops,
            moved,
        )(*pair, *common)
        return results[0], tuple(results[1:3]), results[3], results[4]
    results = kernel_call(
        functools.partial(attention_backward, len(blocks), head_dim, width),
        (group,),
        [rows(model)] * 2 + [per_sequence(raw_shape)] + [rows(model)] * 2 + common_specs,
        [rows(attn_width), rows(attn_width), pl.BlockSpec((2, width), lambda s: (0, 0))]
        + [rows(model)] * 2
        + [pl.BlockSpec((1, model), lambda s: (0, 0))],
        [side(attn_width), side(attn_width), shape_of((2, width), jnp.float32)]
        + [side(model)] * 2
        + [shape_of((1, model), jnp.float32)],
        flops,
        moved,
    )(*pair, raw, *normed, *common)
    return tuple(results[:2]), *results[2:]


def ffn_units(count, ff_sub, earlier, *refs):
    normed, out = refs[0:2], refs[2:4]
    blocks, refs = refs[4 : 4 + count], refs[4 + count :]
    if earlier:
        before, refs = refs[0:2], refs[2:]
    inner_refs, grad_refs, terms = refs[0:2], refs[2:4], refs[4:6]
    tile = normed[0].shape[0]
    gate_up = block_product(normed[0], normed[1], blocks, 0, 2 * ff_sub)
    inner_grad = block_product(out[0], out[1], blocks, 2 * ff_sub, 3 * ff_sub)
    gate, up = gate_up[:, :ff_sub], gate_up[:, ff_sub:]
    sigmoid = 1.0 / (1.0 + jnp.exp(-gate))
    silu = gate * sigmoid
    inner = (silu * up).astype(jnp.bfloat16)
    gate_grad = (inner_grad * up * sigmoid * (1.0 + gate * (1.0 - sigmoid))).astype(jnp.bfloat16)
    up_grad = (inner_grad * silu).astype(jnp.bfloat16)
    for side in range(2):
        rows = slice(side * tile, (side + 1) * tile)
        inner_refs[side][...] = inner[rows]
        grad_refs[side][:, :ff_sub] = gate_grad[rows]
        grad_refs[side][:, ff_sub:] = up_grad[rows]
    if not earlier:
        return
    here = jnp.concatenate([gate_grad, up_grad], axis=1)
    rows = blocks[0].shape[0]
    for k in range(count):
        span = slice(k * rows, (k + 1) * rows)
        total = dot_nt(here, blocks[k][:, : 2 * ff_sub])
        for side in range(2):
            part = total[side * tile : (side + 1) * tile]
            part = part + before[side][:, span].astype(jnp.float32)
            terms[side][:, span] = part.astype(jnp.bfloat16)


def run_ffn_units(normed, out, blocks, ff_sub, before=None):
    tokens, model = normed[0].shape
    tile = min(256, tokens)
    rows = lambda n: pl.BlockSpec((tile, n), lambda i: (i, 0))
    earlier = before is not None
    shapes = [ff_sub] * 2 + [2 * ff_sub] * 2 + [model] * 2 * earlier
    return kernel_call(
        functools.partial(ffn_units, len(blocks), ff_sub, earlier),
        (tokens // tile,),
        [rows(model)] * 4
        + [whole(b) for b in blocks]
        + [rows(model)] * 2 * earlier,
        [rows(n) for n in shapes],
        [shape_of((tokens, n), jnp.bfloat16) for n in shapes],
        12 * tokens * model * ff_sub,
        8 * tokens * model,
    )(*normed, *out, *blocks, *(before if earlier else ()))


def weight_gradients(count, per, *refs):
    first, second = refs[0:2], refs[2:4]
    first_grad, second_grad = refs[4:6], refs[6:8]
    outs = refs[8:]
    one = dot_tn(first[0][...], first_grad[0][...]) + dot_tn(first[1][...], first_grad[1][...])
    two = dot_tn(second[0][...], second_grad[0][...]) + dot_tn(second[1][...], second_grad[1][...])
    width = one.shape[1]
    for k in range(count):

        @pl.when(pl.program_id(0) // per == k)
        def _(k=k):
            outs[k][:, :width] = one.astype(jnp.bfloat16)
            outs[k][:, width:] = two.astype(jnp.bfloat16)


def run_weight_gradients(first, first_grad, second, second_grad, count):
    tokens, model = first[0].shape
    block_rows = model // count
    tile = min(256, block_rows)
    per = block_rows // tile
    width = first_grad[0].shape[1] + second_grad[0].shape[1]
    columns = pl.BlockSpec((tokens, tile), lambda i: (0, i))
    out_spec = lambda k: pl.BlockSpec(
        (tile, width), lambda i: (jnp.clip(i - per * k, 0, per - 1), 0)
    )
    return kernel_call(
        functools.partial(weight_gradients, count, per),
        (model // tile,),
        [columns] * 4 + [whole(a) for a in (*first_grad, *second_grad)],
        [out_spec(k) for k in range(count)],
        [shape_of((block_rows, width), jnp.bfloat16)] * count,
        2 * tokens * model * 256,
        tokens * model,
        vmem_limit,
    )(*first, *second, *first_grad, *second_grad)


def partial_gradients(count, per, *refs):
    left, right, outs = refs[0:2], refs[2:4], refs[-count:]
    product = dot_tn(left[0][...], right[0][...]) + dot_tn(left[1][...], right[1][...])
    product = product.astype(jnp.bfloat16)
    for k in range(count):

        @pl.when(pl.program_id(0) // per == k)
        def _(k=k):
            outs[k][...] = product


def run_partial_gradients(left, right, count, width, column, into=()):
    tokens, model = left[0].shape
    block_rows = model // count
    tile = min(256, block_rows)
    per = block_rows // tile
    columns = pl.BlockSpec((tokens, tile), lambda i: (0, i))
    part = right[0].shape[1]
    out_spec = lambda k: pl.BlockSpec(
        (tile, part), lambda i: (jnp.clip(i - per * k, 0, per - 1), column)
    )
    return pl.pallas_call(
        functools.partial(partial_gradients, count, per),
        grid=(model // tile,),
        in_specs=[columns] * 2
        + [whole(a) for a in right]
        + [pl.BlockSpec(memory_space=pl.ANY)] * len(into),
        out_specs=[out_spec(k) for k in range(count)],
        out_shape=[shape_of((block_rows, width), jnp.bfloat16)] * count,
        input_output_aliases={4 + k: k for k in range(len(into))},
        compiler_params=pltpu.CompilerParams(vmem_limit_bytes=vmem_limit),
        cost_estimate=pl.CostEstimate(
            flops=2 * tokens * model * 128, bytes_accessed=tokens * model // 2, transcendentals=0
        ),
    )(*left, *right, *into)


def transposed_product(parts, count, *refs):
    lefts = refs[: 2 * parts]
    blocks = refs[2 * parts : 2 * parts + parts * count]
    outs = refs[2 * parts + parts * count :]
    tile = lefts[0].shape[0]
    rows = blocks[0].shape[0]
    for k in range(count):
        total = None
        span = slice(k * rows, (k + 1) * rows)
        for p in range(parts):
            left = jnp.concatenate([lefts[2 * p][...], lefts[2 * p + 1][...]], axis=0)
            more = dot_nt(left, blocks[p * count + k][...])
            total = more if total is None else total + more
        total = total.astype(jnp.bfloat16)
        outs[0][:, span] = total[:tile]
        outs[1][:, span] = total[tile:]


def run_transposed_product(pairs, blocks, column, columns):
    count = len(blocks[0])
    tokens = pairs[0][0].shape[0]
    model = count * blocks[0][0].shape[0]
    tile = min(256, tokens)
    rows = lambda n: pl.BlockSpec((tile, n), lambda i: (i, 0))
    lefts = [a for pair in pairs for a in pair]
    flat = [b for one in blocks for b in one]
    return kernel_call(
        functools.partial(transposed_product, len(pairs), count),
        (tokens // tile,),
        [rows(a.shape[1]) for a in lefts]
        + [pl.BlockSpec((b.shape[0], columns), lambda i: (0, column)) for b in flat],
        [rows(model)] * 2,
        [shape_of((tokens, model), jnp.bfloat16)] * 2,
        2 * tokens * model * 256,
        tokens * model,
        28 * mebibyte,
    )(*lefts, *flat)


def add_three(first, second, third, out):
    total = first[...].astype(jnp.float32) + second[...].astype(jnp.float32)
    out[...] = (total + third[...].astype(jnp.float32)).astype(jnp.bfloat16)


def add_swapped(odd_ref, one, two, first, second, out_first, out_second):
    odd = odd_ref[...] == 1
    for left, right, got, out in ((one, two, first, out_first), (two, one, second, out_second)):
        here = jnp.where(odd, right[...].astype(jnp.float32), left[...].astype(jnp.float32))
        out[...] = (here + got[...].astype(jnp.float32)).astype(jnp.bfloat16)


def run_add(body, arrays, outs, flag=None):
    rows, width = arrays[0].shape
    tile = min(256, rows)
    spec = pl.BlockSpec((tile, width), lambda i: (i, 0))
    flags = [] if flag is None else [flag]
    return kernel_call(
        body,
        (rows // tile,),
        [whole(f) for f in flags] + [spec] * len(arrays),
        [spec] * outs,
        [shape_of((rows, width), jnp.bfloat16)] * outs,
        1,
        12 * rows * width,
        16 * mebibyte if rows * width > mebibyte // 2 else vmem_limit,
    )(*flags, *arrays)


def place_columns(subs, place_ref, *refs):
    ins, outs = refs[: group * subs], refs[group * subs :]
    place = place_ref[0]
    rows = ins[0].shape[0]
    width = ins[0].shape[1] // len(outs)
    for s in range(subs):
        for r, ref in enumerate(ins[group * s : group * (s + 1)]):
            start = ref.shape[0] - rows if r == group - 1 else 0
            column = pl.multiple_of((s * group + (place ^ r)) * width, width)
            for m, out in enumerate(outs):
                piece = ref[start : start + rows, m * width : (m + 1) * width]
                out[:, pl.ds(column, width)] = piece.astype(jnp.float32)


def run_place_columns(place, parts, count):
    rows, width = parts[0][0].shape
    flat = [a for part in parts for a in part]
    full = lambda a: pl.BlockSpec(a.shape, lambda i, place: (0, 0))
    shape = shape_of((rows, width // count * group * len(parts)), jnp.float32)
    return pl.pallas_call(
        functools.partial(place_columns, len(parts)),
        grid_spec=pltpu.PrefetchScalarGridSpec(
            num_scalar_prefetch=1,
            grid=(1,),
            in_specs=[full(a) for a in flat],
            out_specs=[full(shape)] * count,
        ),
        out_shape=[shape] * count,
        compiler_params=pltpu.CompilerParams(vmem_limit_bytes=32 * mebibyte),
    )(place.reshape(1).astype(jnp.int32), *flat)


def place_halves(place, mine, other, out):
    half = mine.shape[0]
    core = place[0]
    out[pl.ds(core * half, half), :] = mine[...]
    out[pl.ds((1 - core) * half, half), :] = other[...]


def run_place_halves(core, spot, count, mine, other):
    half, model = mine.shape
    block = model // count
    source = pl.BlockSpec((half, block), lambda k, place: (0, k))
    return pl.pallas_call(
        place_halves,
        grid_spec=pltpu.PrefetchScalarGridSpec(
            num_scalar_prefetch=1,
            grid=(count,),
            in_specs=[source, source],
            out_specs=pl.BlockSpec((2 * half, block), lambda k, place: (0, (k + place[1]) % count)),
        ),
        out_shape=shape_of((2 * half, model), jnp.float32),
        compiler_params=pltpu.CompilerParams(vmem_limit_bytes=12 * mebibyte),
        cost_estimate=pl.CostEstimate(flops=1, bytes_accessed=16 * half * model, transcendentals=0),
    )(jnp.stack([core, spot]).astype(jnp.int32), mine, other)


def swap_cores(values):
    return lax.ppermute(values, "tensor", [(0, 1), (1, 0)])


sides = ((0, 1), (1, 0), (2, 3), (3, 2))
middle = ((1, 2), (2, 1))
outward = ((2, 3), (1, 0))
inward = ((0, 1), (3, 2))


class Lines:
    def __init__(self, dp):
        self.dp = dp
        self.length = dp // group
        index = lax.axis_index("dp")
        self.place = index % group
        self.spot = index // group

    def flip(self, values, relation):
        return lax.ppermute(values, "dp", [(i, i ^ relation) for i in range(self.dp)])

    def ends(self, values, moves):
        pairs = [
            (one * group + place, two * group + place)
            for one, two in moves
            for place in range(group)
        ]
        return lax.ppermute(values, "dp", pairs)

    def turn(self, values, step):
        pairs = [
            (spot * group + place, ((spot + step) % self.length) * group + place)
            for spot in range(self.length)
            for place in range(group)
        ]
        return lax.ppermute(values, "dp", pairs)

    def by_place(self, related):
        odd = self.place % 2 == 1
        high = self.place // 2 == 1
        own, one, two, three = related
        pairs = (
            (jnp.where(odd, one, own), jnp.where(odd, own, one)),
            (jnp.where(odd, three, two), jnp.where(odd, two, three)),
        )
        return [
            jnp.where(high, pairs[1][0], pairs[0][0]),
            jnp.where(high, pairs[1][1], pairs[0][1]),
            jnp.where(high, pairs[0][0], pairs[1][0]),
            jnp.where(high, pairs[0][1], pairs[1][1]),
        ]

    def pieces(self, piece_of):
        return [piece_of(self.place ^ relation) for relation in range(group)]

    def flip_pieces(self, pieces):
        return [pieces[0]] + [self.flip(pieces[r], r) for r in range(1, group)]

    def flip_first(self, pieces):
        return self.flip(jnp.concatenate([pieces[1], pieces[3]]), 1)

    def flip_second(self, pieces, got):
        return self.flip(jnp.concatenate([pieces[2], got[got.shape[0] // 2 :]]), 2)

    def flipped(self, pieces, first, second):
        rows = pieces[0].shape[0]
        return [pieces[0], first[:rows], second[:rows], second[rows:]]

    def row_pieces(self, total):
        rows = total.shape[0] // group
        return [
            lax.dynamic_slice_in_dim(total, (self.place ^ r) * rows, rows) for r in range(group)
        ]

    def gather_near(self, mine):
        return [self.flip(mine, 1), self.flip(mine, 2)]

    def gather_across(self, near):
        middle = near[0].shape[0] // 2
        return [self.flip(near[0][:middle], 2), self.flip(near[1][middle:], 1)]

    def scatter_across(self, across):
        middle = across.shape[0] // 2
        return [self.flip(across[:middle], 1), self.flip(across[middle:], 2)]

    def gather_far(self, mine):
        near = self.gather_near(mine)
        return near, self.gather_across(near)

    def gather_tokens(self, mine):
        return self.both_cores(mine, *self.gather_far(mine))

    def both_cores(self, mine, near, across):
        kept = jnp.concatenate([mine] + near + across)
        return kept, swap_cores(kept)

    def terms(self, kept, other, relation):
        rows = kept.shape[0] // group
        span = slice(relation * rows, (relation + 1) * rows)
        return kept[span].astype(jnp.float32) + other[span].astype(jnp.float32)

    def across_terms(self, kept, other):
        return self.scatter_across(self.terms(kept, other, 3).astype(jnp.bfloat16))

    def near_sends(self, kept, other, got):
        one, two = self.terms(kept, other, 1), self.terms(kept, other, 2)
        middle = one.shape[0] // 2
        one = jnp.concatenate([one[:middle], one[middle:] + got[1].astype(jnp.float32)])
        two = jnp.concatenate([two[:middle] + got[0].astype(jnp.float32), two[middle:]])
        return [one.astype(jnp.bfloat16), two.astype(jnp.bfloat16)]

    def near_flips(self, kept, other, got):
        one, two = self.near_sends(kept, other, got)
        return [self.flip(one, 1), self.flip(two, 2)]

    def near_sum(self, kept, other, near):
        one, two = near
        return self.terms(kept, other, 0) + one.astype(jnp.float32) + two.astype(jnp.float32)

    def near_terms(self, kept, other, got):
        return self.near_sum(kept, other, self.near_flips(kept, other, got))

    def scatter_tokens(self, kept, other):
        return self.near_terms(kept, other, self.across_terms(kept, other))


class LineGather:
    def __init__(self, lines, block):
        self.lines, self.block, self.got = lines, block, []

    def hop(self):
        lines, step = self.lines, len(self.got) + 1
        if lines.length != 4:
            turns = range(1, lines.length) if step == 1 else ()
            self.got.append([lines.turn(self.block, -k) for k in turns])
        elif step == 1:
            self.got.append([lines.ends(self.block, sides), lines.ends(self.block, middle)])
        elif step == 2:
            outer, inner = self.got[0]
            self.got.append([lines.ends(outer, middle), lines.ends(inner, outward)])
        else:
            self.got.append([lines.ends(self.got[1][0], outward)])

    def blocks(self):
        lines = self.lines
        if lines.length != 4:
            return [self.block] + self.got[0]
        (outer, inner), (inner_two, outer_two), (outer_three,) = self.got
        spot = lines.spot
        return [
            self.block,
            jnp.where(spot == 3, outer_three, jnp.where(spot == 1, inner, outer)),
            jnp.where((spot == 1) | (spot == 2), inner_two, outer_two),
            jnp.where(spot == 0, outer_three, jnp.where(spot == 2, inner, outer)),
        ]


class LineScatter:
    def __init__(self, lines, blocks):
        self.lines, self.blocks, self.got = lines, blocks, []

    def ready(self):
        step = len(self.got) + 1
        if self.lines.length != 4:
            return []
        if step == 1:
            return [self.blocks[3], self.blocks[1]]
        if step == 2:
            return run_add(add_three, [self.blocks[2], *self.got[0]], 1)
        odd = (self.lines.spot % 2).astype(jnp.int32).reshape(1, 1)
        return run_add(add_swapped, [self.blocks[1], self.blocks[3], *self.got[1]], 2, odd)

    def hop(self, ready=None):
        lines, step = self.lines, len(self.got) + 1
        if lines.length != 4:
            turns = range(1, lines.length) if step == 1 else ()
            self.got.append([lines.turn(self.blocks[k], k) for k in turns])
            return
        ready = self.ready() if ready is None else ready
        if step == 1:
            self.got.append([lines.ends(ready[0], ((0, 1),)), lines.ends(ready[1], ((3, 2),))])
        elif step == 2:
            self.got.append([lines.ends(ready[0], middle), lines.ends(ready[0], inward)])
        else:
            self.got.append([lines.ends(ready[0], sides), lines.ends(ready[1], middle)])

    def total(self):
        last = self.got[-1] if self.lines.length == 4 else self.got[0]
        result = self.blocks[0].astype(jnp.float32)
        for one in last:
            result = result + one.astype(jnp.float32)
        return result.astype(jnp.bfloat16)


def tie(*values):
    return lax.optimization_barrier(values)


def local(
    dp,
    tokens,
    segments,
    cotangent,
    attn_gain,
    ffn_gain,
    query_gain,
    key_gain,
    w_query,
    key_weight,
    value_weight,
    w_out,
    w_gate,
    w_up,
    w_down,
):
    lines = Lines(dp)
    core = lax.axis_index("tensor")
    length, width = tokens.shape
    half = length // 2
    head_dim = query_gain.shape[0]
    rows = w_query.shape[0]
    block_rows = rows * group
    query_width = w_query.shape[1] // group
    key_width = key_weight.shape[1] // group
    attn_width = query_width + 2 * key_width
    ff_sub = w_gate.shape[1] // group // sub_count

    def around(values):
        return jnp.roll(values, -lines.spot * block_rows, axis=-1)

    def back_around(values):
        return jnp.roll(values, lines.spot * block_rows, axis=-1)

    attn_gain_r, ffn_gain_r = around(attn_gain), around(ffn_gain)

    def columns(weight, start, size):
        return lax.dynamic_slice_in_dim(weight, start, size, axis=1)

    attn_pieces = lines.pieces(
        lambda j: jnp.concatenate(
            [
                columns(w_query, j * query_width, query_width),
                columns(key_weight, j * key_width, key_width),
                columns(value_weight, j * key_width, key_width),
                columns(w_out, j * query_width, query_width),
            ],
            axis=1,
        )
    )
    attn_shared = lines.flip_pieces(attn_pieces)
    source = around(lax.dynamic_slice_in_dim(tokens, core * half, half)).astype(jnp.float32)
    normed_f, scale_first = norm_rows(source, attn_gain_r)
    normed_mine = normed_f.astype(jnp.bfloat16)

    seg_near = jnp.concatenate([segments, lines.flip(segments, 1)])
    seg_second = lines.flip(seg_near, 2)
    attn_shared, normed_mine, seg_near, seg_second = tie(
        attn_shared, normed_mine, seg_near, seg_second
    )

    def ffn_piece(s):
        return lines.pieces(
            lambda j: jnp.concatenate(
                [
                    columns(weight, s * group * ff_sub + j * ff_sub, ff_sub)
                    for weight in (w_gate, w_up, w_down)
                ],
                axis=1,
            )
        )


    seg_all = jnp.concatenate([seg_near, seg_second])
    positions = jax.vmap(positions_of)(seg_all)
    index = jnp.arange(length, dtype=jnp.int32)
    cosine, sine = angles(positions, head_dim, 2 * head_dim)
    swapped = jnp.full((1, 1), core, jnp.int32)
    starts = index[None] - positions
    tables = (swapped, cosine, sine, starts[..., None], starts[:, None, :], index)
    gains_two = jnp.stack(
        [
            jnp.tile(query_gain, query_width // head_dim),
            jnp.tile(key_gain, query_width // head_dim),
        ]
    )

    attn_line = LineGather(lines, jnp.concatenate(lines.by_place(attn_shared), axis=0))
    attn_line.hop()
    near = lines.gather_near(normed_mine)
    mine_other = swap_cores(normed_mine)
    near, attn_line.got[0], tables, mine_other, w_gate, w_up, w_down = tie(
        near, attn_line.got[0], tables, mine_other, w_gate, w_up, w_down
    )
    attn_line.hop()
    across = lines.gather_across(near)
    pieces_0 = ffn_piece(0)
    near_other = swap_cores(near[0])
    near_other, near_two = tie(near_other, near[1])
    near = [near[0], near_two]
    near_other = [near_other, swap_cores(near_two)]
    across, attn_line.got[1], pieces_0, near_other, w_gate, w_up, w_down, cotangent = tie(
        across, attn_line.got[1], pieces_0, near_other, w_gate, w_up, w_down, cotangent
    )
    attn_line.hop()
    pieces_1 = ffn_piece(1)
    cot_half = around(lax.dynamic_slice_in_dim(cotangent, core * half, half))
    out_mine = cot_half.astype(jnp.bfloat16)
    across = jnp.concatenate(across)
    normed = (
        jnp.concatenate([normed_mine] + near + [across]),
        jnp.concatenate([mine_other] + near_other + [swap_cores(across)]),
    )
    shared_0 = lines.flip_pieces(pieces_0)
    normed, attn_line.got[2], shared_0, pieces_1, out_mine = tie(
        normed, attn_line.got[2], shared_0, pieces_1, out_mine
    )
    attn_w = attn_line.blocks()

    line_0 = LineGather(lines, jnp.concatenate(lines.by_place(shared_0), axis=0))
    line_0.hop()
    out_near = lines.gather_near(out_mine)
    qkv_raw, heads_out, attended_kept, attended_other = run_attention(
        True, normed, attn_w, tables, gains_two, head_dim, query_width, attn_width
    )
    attended_other, line_0.got[0], out_near, pieces_1 = tie(
        attended_other, line_0.got[0], out_near, pieces_1
    )

    line_0.hop()
    attended_other = swap_cores(attended_other)
    middle = half // 2
    out_first = lines.flip(out_near[0][:middle], 2)
    attended_other, out_first = tie(attended_other, out_first)
    first_1 = lines.flip_first(pieces_1)
    got = lines.across_terms(attended_kept, attended_other)
    got, first_1, line_0.got[1] = tie(got, first_1, line_0.got[1])
    line_0.hop()
    second_1 = lines.flip_second(pieces_1, first_1)
    attended = lines.near_terms(attended_kept, attended_other, got)
    attended, out_near = tie(attended, out_near)
    out_second = lines.flip(out_near[1][middle:], 1)
    attended, line_0.got[2], out_first, out_second, second_1 = tie(
        attended, line_0.got[2], out_first, out_second, second_1
    )
    shared_1 = lines.flipped(pieces_1, first_1, second_1)
    block_1 = jnp.concatenate(lines.by_place(shared_1), axis=0)

    line_1 = LineGather(lines, block_1)
    out_b = lines.both_cores(out_mine, out_near, [out_first, out_second])
    line_1.hop()
    state = source + attended
    normed2_f, scale_second = norm_rows(state, ffn_gain_r)
    near, across = lines.gather_far(normed2_f.astype(jnp.bfloat16))
    ffn_w = [line_0.blocks()]
    near, across, line_1.got[0], out_b, ffn_w[0] = tie(
        near, across, line_1.got[0], out_b, ffn_w[0]
    )

    line_1.hop()
    normed2 = lines.both_cores(normed2_f.astype(jnp.bfloat16), near, across)
    units_0 = run_ffn_units(normed2, out_b, ffn_w[0], ff_sub)
    units_0, line_1.got[1] = tie(units_0, line_1.got[1])
    line_1.hop()
    ffn_g = run_weight_gradients(normed2, units_0[2:], out_b, units_0[:2], lines.length)
    terms_0 = run_transposed_product([units_0[2:]], [ffn_w[0]], 0, 2 * ff_sub)
    ffn_g, line_1.got[2], units_0, terms_0 = tie(ffn_g, line_1.got[2], units_0, terms_0)
    sum_0 = LineScatter(lines, ffn_g)
    ffn_w.append(line_1.blocks())

    sum_0.hop()
    units_1 = run_ffn_units(normed2, out_b, ffn_w[1], ff_sub, terms_0)
    kept, other = units_1[4:]
    kept, other, sum_0.got[0], units_1 = tie(kept, other, sum_0.got[0], units_1)

    sum_0.hop()
    other = swap_cores(other)
    send = lines.terms(kept, other, 3).astype(jnp.bfloat16)
    send, units_1 = tie(send, units_1)
    got = lines.scatter_across(send)
    branch_kept, branch_other = run_transposed_product(
        [units_0[:2], units_1[:2]], ffn_w, 2, ff_sub
    )
    ffn_g = run_partial_gradients(normed2, units_1[2:4], lines.length, 3 * ff_sub, 0)
    got, sum_0.got[1], ffn_g, branch_kept, branch_other, units_1 = tie(
        got, sum_0.got[1], ffn_g, branch_kept, branch_other, units_1
    )
    sum_0.hop()
    branch_other = swap_cores(branch_other)
    near = lines.near_flips(kept, other, got)
    ffn_g = run_partial_gradients(out_b, units_1[:2], lines.length, 3 * ff_sub, 2, ffn_g)
    near, branch_kept, branch_other, ffn_g = tie(near, branch_kept, branch_other, ffn_g)
    sum_1 = LineScatter(lines, ffn_g)
    normed2_grad = lines.near_sum(kept, other, near)
    branch_got = lines.across_terms(branch_kept, branch_other)
    normed2_grad, sum_0.got[2], branch_got = tie(normed2_grad, sum_0.got[2], branch_got)

    sum_1.hop()
    ffn_gain_part = jnp.sum(normed2_grad * state * scale_second, axis=0)
    state_grad = cot_half + norm_back(state, scale_second, ffn_gain_r, normed2_grad)
    grad_mine = state_grad.astype(jnp.bfloat16)
    near, across = lines.gather_far(grad_mine)
    back_0 = lines.row_pieces(sum_0.total())
    branch_terms = lines.near_sends(branch_kept, branch_other, branch_got)
    ready = sum_1.ready()
    near, across, ready, back_0, branch_terms = tie(near, across, ready, back_0, branch_terms)

    sum_1.hop(ready)
    attended_b = lines.both_cores(grad_mine, near, across)

    branch = [lines.flip(branch_terms[0], 1), lines.flip(branch_terms[1], 2)]
    back_0_first = lines.flip_first(back_0)
    qkv_grad, gain_parts, kept, other, attn_gain_part = run_attention(
        False,
        attended_b,
        attn_w,
        tables,
        gains_two,
        head_dim,
        query_width,
        attn_width,
        qkv_raw,
        normed,
    )
    kept, other, qkv_grad, branch, sum_1.got[1], back_0, back_0_first = tie(
        kept, other, qkv_grad, branch, sum_1.got[1], back_0, back_0_first
    )

    sum_1.hop()
    gains = jnp.concatenate(
        [
            back_around(attn_gain_part[0] / attn_gain_r),
            back_around(ffn_gain_part),
            jnp.sum(gain_parts[0].reshape(-1, head_dim), axis=0),
            gain_parts[1][:head_dim],
        ]
    )
    other = swap_cores(other)
    back_0_second = lines.flip_second(back_0, back_0_first)
    attn_sum = LineScatter(
        lines, run_weight_gradients(normed, qkv_grad, attended_b, heads_out, lines.length)
    )
    other, attn_sum.blocks = tie(other, attn_sum.blocks)
    got = lines.across_terms(kept, other)
    got, sum_1.got[2], back_0_second, branch = tie(got, sum_1.got[2], back_0_second, branch)
    attn_sum.hop()
    back_1 = lines.row_pieces(sum_1.total())
    near = lines.near_flips(kept, other, got)
    back_got = [lines.flip(back_1[1], 1)]
    attn_sum.hop()
    mixed = state + lines.near_sum(branch_kept, branch_other, branch)
    near, attn_sum.got[1], back_1, back_got, mixed = tie(
        near, attn_sum.got[1], back_1, back_got, mixed
    )
    ready = attn_sum.ready()
    near, ready = tie(near, ready)
    attn_sum.hop(ready)
    mixed_other = swap_cores(mixed)
    back_got = back_got + [lines.flip(back_1[r], r) for r in (2, 3)]
    gains, mixed_other = tie(gains, mixed_other)
    gains = gains + lines.flip(gains, 1)
    gains = gains + lines.flip(gains, 2)
    normed_grad = lines.near_sum(kept, other, near)
    input_grad = state_grad + norm_back(source, scale_first, attn_gain_r, normed_grad)
    mixed = run_place_halves(core, lines.spot, lines.length, mixed, mixed_other)
    attn_sum.got[2], back_got, input_grad, gains, mixed = tie(
        attn_sum.got[2], back_got, input_grad, gains, mixed
    )
    back_1 = [back_1[0]] + back_got
    attn_grads = lines.flip_pieces(lines.row_pieces(attn_sum.total()))
    input_other = swap_cores(input_grad)
    ffn_grads = run_place_columns(
        lines.place,
        [
            (back_0[0], back_0_first, back_0_second, back_0_second),
            back_1,
        ],
        3,
    )
    input_grad = run_place_halves(core, lines.spot, lines.length, input_grad, input_other)
    bit = group
    while bit < dp:
        gains = gains + lines.flip(gains, bit)
        bit *= 2
    gains, attn_grads, ffn_grads = tie(gains, attn_grads, ffn_grads)
    gains = gains + swap_cores(gains)

    def columns_of(related, start, stop):
        blocks = lines.by_place([b[:, start:stop] for b in related])
        return jnp.concatenate(blocks, axis=1).astype(jnp.float32)

    return (
        mixed,
        input_grad,
        gains[:width],
        gains[width : 2 * width],
        gains[2 * width : 2 * width + head_dim],
        gains[2 * width + head_dim :],
        columns_of(attn_grads, 0, query_width),
        columns_of(attn_grads, query_width, query_width + key_width),
        columns_of(attn_grads, query_width + key_width, attn_width),
        columns_of(attn_grads, attn_width, attn_width + query_width),
        *ffn_grads,
    )


def solution(mesh):
    dp = mesh.shape["dp"]
    weight = P("dp", "tensor")
    rows = P("dp", None)
    return jax.shard_map(
        lambda *arrays: local(dp, *arrays),
        mesh=mesh,
        in_specs=(rows, rows, rows, P(), P(), P(), P()) + (weight,) * 7,
        out_specs=(rows, rows, P(), P(), P(), P()) + (weight,) * 7,
        check_vma=False,
    )
```
